32 devices in a mesh: dp: 8 (over z, x), owner: 4 (over y, core).
Axes of the slice: x: 2, y: 2, z: 4, core: 2. Of those that a mesh axis runs over, the one named last changes fastest.
Arguments:
- hidden: bfloat16 [8192, 6912], P(('dp', 'owner')), may hold values from -6 to 6
- grad_out: bfloat16 [8192, 2560], P(('dp', 'owner')), may hold values from -6 to 6
- block_list: int32 [128, 2], replicated, may hold values from 0 to 107, as said below
- live_block_count: int32 [32], replicated, may hold values from 1 to 4, as said below
- master: float32 [128, 4096], P(('dp', 'owner')), may hold values from -6 to 6
- moment: float32 [128, 4096], P(('dp', 'owner')), may hold values from -6 to 6
- variance: float32 [128, 4096], P(('dp', 'owner')), may hold values from 0.25 to 4
Outputs:
- new_master: float32 [128, 4096], P(('dp', 'owner'))
- new_moment: float32 [128, 4096], P(('dp', 'owner'))
- new_variance: float32 [128, 4096], P(('dp', 'owner'))
- clipped_grad: float32 [128, 4096], P(('dp', 'owner'))
- published: bfloat16 [128, 4096], replicated
The draws below stay inside these ranges and needn't reach their ends.
Inputs may be any that keep to these rules, and one draw needn't show every extreme that they name: `block_list`: each row names a block: its row index below 108, its column index below 40; all rows name different blocks. Rows 4 o to 4 o + 3 are owner o's slots; owner o is the device whose index along dp is o // 4 and whose index along the mesh axis `owner` is o mod 4. Owner o's first live_block_count[o] slots are live, the rest padding; some owner's slots are all live.
All inputs are finite; a program needn't handle non-finite values.
Results may differ from the reference program's by a relative error of at most 0.001.
Values may be sent and summed in bfloat16 or wider, within the bound.
No kernel may reach another device: no remote copies, remote signals or barrier semaphores. Data moves between devices by JAX's collectives and lax.ppermute only.
A program may use at most 128 MiB of HBM per device.

```python
import math
import jax
import jax.numpy as jnp
from jax import lax

D_WIN = 2560
FF_WIN = 6912
BLOCK_SIDE_SIZE = 64
OWNER_SLOTS = 4
OWNERS = 32
TOTAL_SLOTS = 128
TOKENS = 8192


def draw_block_list(key, part):
    key = jax.random.fold_in(key, 11)
    across = D_WIN // BLOCK_SIDE_SIZE
    all_block_list = FF_WIN // BLOCK_SIDE_SIZE * across
    picked_slots = jax.random.permutation(key, all_block_list)[:TOTAL_SLOTS].astype(jnp.int32)
    return jnp.stack([picked_slots // across, picked_slots % across], axis=1).astype(jnp.int32)


def draw_live_block_count(key, part):
    key = jax.random.fold_in(key, 23)
    first_key, second_key = jax.random.split(key)
    counts = jax.random.randint(first_key, (OWNERS,), max(1, OWNER_SLOTS // 4), OWNER_SLOTS + 1)
    full_owner = jax.random.randint(second_key, (), 0, OWNERS)
    return jnp.where(jnp.arange(OWNERS) == full_owner, OWNER_SLOTS, counts).astype(jnp.int32)


def block_scale(key, extent, cuts, smallest, largest):
    level = 1.0
    for position, shards_of in cuts:
        heights = jax.random.uniform(jax.random.fold_in(jax.random.fold_in(key, 6), position), (shards_of,), jnp.float32, smallest / len(cuts), largest / len(cuts))
        level = level * jnp.repeat(jnp.exp(heights), extent[position] // shards_of).reshape((-1,) + (1,) * (len(extent) - 1 - position))
    return level


def scatter_about(rng, extent, scale, most, cuts=(), held_as=jnp.bfloat16):
    loudness = block_scale(rng, extent, cuts, -0.22, 0.18) if cuts else 1.0
    drawn = jax.random.normal(rng, extent, jnp.float32) * scale * loudness
    return jnp.minimum(jnp.maximum(drawn, -most), most).astype(held_as)


def setup_inputs(seed: int = 0) -> dict:
    arg_keys = jax.random.split(jax.random.key(seed), 8)
    hidden = scatter_about(arg_keys[0], (TOKENS, FF_WIN), 1.0, 6.0, ((0, 32),))
    grad_out = scatter_about(arg_keys[1], (TOKENS, D_WIN), 1.0, 6.0, ((0, 32),))
    block_list = draw_block_list(jax.random.fold_in(arg_keys[7], 71), 0)
    live_block_count = draw_live_block_count(jax.random.fold_in(arg_keys[7], 71), 0)
    master = scatter_about(arg_keys[4], (TOTAL_SLOTS, BLOCK_SIDE_SIZE * BLOCK_SIDE_SIZE), 1.0, 6.0, ((0, 32),), jnp.float32)
    moment = scatter_about(arg_keys[5], (TOTAL_SLOTS, BLOCK_SIDE_SIZE * BLOCK_SIDE_SIZE), 0.5, 6.0, ((0, 32),), jnp.float32)
    variance = jnp.clip(jnp.exp(math.log(4.0) - 2.7725887 * jax.random.uniform(arg_keys[6], (TOTAL_SLOTS, BLOCK_SIDE_SIZE * BLOCK_SIDE_SIZE), jnp.float32) ** block_scale(arg_keys[6], (TOTAL_SLOTS, BLOCK_SIDE_SIZE * BLOCK_SIDE_SIZE), ((0, 32),), -0.2, 0.2)), 0.25, 4.0)
    return dict(hidden=hidden, grad_out=grad_out, block_list=block_list, live_block_count=live_block_count, master=master, moment=moment, variance=variance)


def reference(hidden, grad_out, block_list, live_block_count, master, moment, variance):
    offsets = jnp.arange(BLOCK_SIDE_SIZE, dtype=jnp.int32)
    row_indices = block_list[:, 0].reshape(OWNERS, OWNER_SLOTS)
    column_indices = block_list[:, 1].reshape(OWNERS, OWNER_SLOTS)

    def owned_block_grad(id_pair):
        row_sel, col_sel = id_pair
        row_index = (row_sel[:, None] * BLOCK_SIDE_SIZE + offsets[None, :]).reshape(-1).astype(jnp.int32)
        col_index = (col_sel[:, None] * BLOCK_SIDE_SIZE + offsets[None, :]).reshape(-1).astype(jnp.int32)
        left_cols = jnp.take(hidden, row_index, axis=1).astype(jnp.float32).reshape(TOKENS, OWNER_SLOTS, BLOCK_SIDE_SIZE)
        right_cols = jnp.take(grad_out, col_index, axis=1).astype(jnp.float32).reshape(TOKENS, OWNER_SLOTS, BLOCK_SIDE_SIZE)
        return jnp.einsum('tsa,tsb->sab', left_cols, right_cols).reshape(OWNER_SLOTS, BLOCK_SIDE_SIZE * BLOCK_SIDE_SIZE)
    weight_gradient = lax.map(owned_block_grad, (row_indices, column_indices)).reshape(TOTAL_SLOTS, BLOCK_SIDE_SIZE * BLOCK_SIDE_SIZE)
    active_slot_mask = (jnp.arange(OWNER_SLOTS, dtype=jnp.int32)[None, :] < live_block_count[:, None]).reshape(TOTAL_SLOTS, 1)
    weight_gradient = jnp.where(active_slot_mask, weight_gradient, jnp.zeros_like(weight_gradient))
    live_total = jnp.sum(live_block_count).astype(jnp.float32) * (BLOCK_SIDE_SIZE * BLOCK_SIDE_SIZE)
    mean_square = jnp.sum(weight_gradient * weight_gradient) / live_total
    clip_scale = jnp.minimum(1.0, 1.0 / jnp.sqrt(mean_square + 1e-06))
    clipped_grad = clip_scale * weight_gradient
    new_moment = 0.9 * moment + 0.1 * clipped_grad
    new_variance = 0.95 * variance + 0.05 * clipped_grad * clipped_grad
    moment_hat = new_moment / (1.0 - 0.9 ** 20)
    variance_hat = new_variance / (1.0 - 0.95 ** 20)
    new_master = master - 0.02 * (moment_hat / (jnp.sqrt(variance_hat) + 1e-08) + 0.1 * master)
    published = new_master.astype(jnp.bfloat16)
    return (new_master, new_moment, new_variance, clipped_grad, published)
```

```python
import functools

import jax
import jax.numpy as jnp
from jax import lax
from jax.experimental import pallas as pl
from jax.experimental.pallas import tpu as pltpu
from jax.sharding import PartitionSpec as P

SIDE = 64
LANES = 128
SLOTS = 4
BLOCK = SIDE * SIDE
TILES = BLOCK // LANES
HALF = TILES // 2
CODE_ROWS = HALF * SLOTS
EXP_ROWS = 8
CODE_BITS = 13
AXES = ("dp", "owner")
INV_LN2 = 1.4426950408889634


def terms_kernel(blocks_ref, hidden_ref, grad_ref, out_ref, prod_ref):
    owners = out_ref.shape[0]
    low_lane = lax.broadcasted_iota(jnp.int32, (TILES, LANES), 1) < SIDE

    def one_owner(o, carry):
        packed = []
        for s in range(SLOTS):
            r = blocks_ref[0, o * SLOTS + s]
            c = blocks_ref[1, o * SLOTS + s]
            left = hidden_ref[:, pl.ds(pl.multiple_of((r // 2) * LANES, LANES), LANES)]
            right = grad_ref[:, pl.ds(pl.multiple_of((c // 2) * LANES, LANES), LANES)]
            prod_ref[s] = lax.dot_general(
                left, right, (((0,), (0,)), ((), ())), preferred_element_type=jnp.float32
            )
            base = (r % 2) * SIDE
            even = prod_ref[s, pl.ds(base, TILES, stride=2), :]
            odd = prod_ref[s, pl.ds(base + 1, TILES, stride=2), :]
            crossed = pltpu.roll(jnp.where(low_lane, odd, even), SIDE, 1)
            first_half = c % 2 == 0
            keep_even = jnp.where(first_half, even, crossed)
            keep_odd = jnp.where(first_half, crossed, odd)
            packed.append(jnp.where(low_lane, keep_even, keep_odd))
        peak = functools.reduce(jnp.maximum, [jnp.abs(p) for p in packed])
        peak = jnp.max(peak, axis=0, keepdims=True)
        exponent = jnp.floor(jnp.log(jnp.maximum(peak, 1e-30)) * INV_LN2)
        scale = jnp.exp2(CODE_BITS - exponent)
        for s in range(SLOTS):
            code = jnp.round(packed[s] * scale).astype(jnp.int32)
            word = (code[:HALF] << 16) | (code[HALF:] & 0xFFFF)
            out_ref[o, pl.ds(s, HALF, stride=SLOTS), :] = word
        out_ref[o, pl.ds(CODE_ROWS, EXP_ROWS), :] = jnp.broadcast_to(
            exponent.astype(jnp.int32), (EXP_ROWS, LANES)
        )
        return carry

    lax.fori_loop(0, owners, one_owner, 0)


def sum_kernel(live_ref, recv_ref, grad_ref, square_ref):
    owners = recv_ref.shape[0]

    def add(d, totals):
        high, low = totals
        word = recv_ref[d, pl.ds(0, CODE_ROWS), :]
        exponent = recv_ref[d, pl.ds(CODE_ROWS, EXP_ROWS), :][:1].astype(jnp.float32)
        scale = jnp.exp2(exponent - CODE_BITS)
        high = high + (word >> 16).astype(jnp.float32) * scale
        low = low + ((word << 16) >> 16).astype(jnp.float32) * scale
        return high, low

    zero = jnp.zeros((CODE_ROWS, LANES), jnp.float32)
    high, low = lax.fori_loop(0, owners, add, (zero, zero), unroll=4)
    slot = lax.broadcasted_iota(jnp.int32, (CODE_ROWS, LANES), 0) % SLOTS
    live = slot < live_ref[0]
    high = jnp.where(live, high, 0.0)
    low = jnp.where(live, low, 0.0)
    grad_ref[pl.ds(0, CODE_ROWS), :] = high
    grad_ref[pl.ds(CODE_ROWS, CODE_ROWS), :] = low
    square_ref[...] = jnp.broadcast_to(
        jnp.sum(high * high + low * low, keepdims=True), square_ref.shape
    )


def update_kernel(
    live_total_ref, square_ref, grad_ref, master_ref, moment_ref, variance_ref,
    new_master_ref, new_moment_ref, new_variance_ref, clipped_ref, own_ref,
):
    entries = jnp.full((1, LANES), live_total_ref[0], jnp.int32).astype(jnp.float32) * BLOCK
    mean_square = square_ref[:1] / entries
    clip = jnp.minimum(1.0, 1.0 / jnp.sqrt(mean_square + 1e-06))
    for t in range(TILES):
        lanes = pl.ds(t * LANES, LANES)
        clipped = clip * grad_ref[pl.ds(t * SLOTS, SLOTS), :]
        moment = 0.9 * moment_ref[:, lanes] + 0.1 * clipped
        variance = 0.95 * variance_ref[:, lanes] + 0.05 * clipped * clipped
        master = master_ref[:, lanes]
        moment_hat = moment / (1.0 - 0.9**20)
        variance_hat = variance / (1.0 - 0.95**20)
        step = moment_hat / (jnp.sqrt(variance_hat) + 1e-08) + 0.1 * master
        master = master - 0.02 * step
        clipped_ref[:, lanes] = clipped
        new_moment_ref[:, lanes] = moment
        new_variance_ref[:, lanes] = variance
        new_master_ref[:, lanes] = master
        own_ref[:, lanes] = master.astype(jnp.bfloat16)


VMEM = pl.BlockSpec(memory_space=pltpu.VMEM)
SMEM = pl.BlockSpec(memory_space=pltpu.SMEM)
PARAMS = pltpu.CompilerParams(vmem_limit_bytes=40 * 1024 * 1024)


def local(hidden, grad_out, block_list, live_block_count, master, moment, variance):
    owners = lax.axis_size(AXES)
    tokens = hidden.shape[0]
    me = lax.axis_index(AXES)
    codes = pl.pallas_call(
        terms_kernel,
        out_shape=jax.ShapeDtypeStruct((owners, CODE_ROWS + EXP_ROWS, LANES), jnp.int32),
        in_specs=[SMEM, VMEM, VMEM],
        out_specs=VMEM,
        scratch_shapes=[pltpu.VMEM((SLOTS, LANES, LANES), jnp.float32)],
        compiler_params=PARAMS,
        cost_estimate=pl.CostEstimate(
            flops=2 * owners * SLOTS * LANES * LANES * tokens,
            bytes_accessed=2 * (hidden.size + grad_out.size),
            transcendentals=0,
        ),
        name="block_terms",
    )(block_list.T, hidden, grad_out)
    received = lax.all_to_all(codes, AXES, split_axis=0, concat_axis=0, tiled=True)
    gradient, square = pl.pallas_call(
        sum_kernel,
        out_shape=(
            jax.ShapeDtypeStruct((TILES * SLOTS, LANES), jnp.float32),
            jax.ShapeDtypeStruct((8, LANES), jnp.float32),
        ),
        in_specs=[SMEM, VMEM],
        out_specs=(VMEM, VMEM),
        compiler_params=PARAMS,
        name="sum_sources",
    )(lax.dynamic_slice(live_block_count, (me,), (1,)), received)
    distance = 1
    while distance < owners:
        pairs = [(i, i ^ distance) for i in range(owners)]
        square = square + lax.ppermute(square, AXES, pairs)
        distance *= 2
    shape = jax.ShapeDtypeStruct(master.shape, jnp.float32)
    new_master, new_moment, new_variance, clipped, own = pl.pallas_call(
        update_kernel,
        out_shape=(shape, shape, shape, shape, jax.ShapeDtypeStruct(master.shape, jnp.bfloat16)),
        in_specs=[SMEM, VMEM, VMEM, VMEM, VMEM, VMEM],
        out_specs=(VMEM,) * 5,
        compiler_params=PARAMS,
        name="adamw",
    )(jnp.sum(live_block_count).reshape(1), square, gradient, master, moment, variance)
    spread = jnp.broadcast_to(own[None], (owners,) + own.shape)
    published = lax.all_to_all(spread, AXES, split_axis=0, concat_axis=0, tiled=True)
    return new_master, new_moment, new_variance, clipped, published.reshape(-1, BLOCK)


def solution(mesh):
    rows = P(AXES, None)
    return jax.shard_map(
        local,
        mesh=mesh,
        in_specs=(rows, rows, P(), P(), rows, rows, rows),
        out_specs=(rows, rows, rows, rows, P()),
        check_vma=False,
    )
```

```python
import functools

import jax
import jax.numpy as jnp
from jax import lax
from jax.experimental import pallas as pl
from jax.experimental.pallas import tpu as pltpu
from jax.sharding import Mesh
from jax.sharding import PartitionSpec as P

SIDE = 64
LANES = 128
SLOTS = 4
PAIRS = SLOTS // 2
BLOCK = SIDE * SIDE
TILES = BLOCK // LANES
EXP_ROWS = 8
CODE_BITS = 13
CORES = 2
INV_LN2 = 1.4426950408889634


def transpose_kernel_part(grad_ref, turned_ref):
    for k in range(grad_ref.shape[1] // LANES):
        turned_ref[pl.ds(k * LANES, LANES), :] = grad_ref[:, pl.ds(k * LANES, LANES)].T


def block_products(core, blocks_ref, hidden_ref, turned_ref, out_ref):
    low_lane = lax.broadcasted_iota(jnp.int32, (SIDE, LANES), 1) < SIDE

    def one_chip(chip, carry):
        owner = chip * CORES + core
        for pair in range(PAIRS):
            sides = []
            for k in range(2):
                slot = owner * SLOTS + pair * 2 + k
                r = blocks_ref[0, slot]
                c = blocks_ref[1, slot]
                left = turned_ref[pl.ds(pl.multiple_of(c * SIDE, SIDE), SIDE), :]
                right = hidden_ref[:, pl.ds(pl.multiple_of((r // 2) * LANES, LANES), LANES)]
                product = jnp.dot(left, right, preferred_element_type=jnp.float32)
                sides.append(pltpu.roll(product, ((r + k) % 2) * SIDE, 1))
            out_ref[chip, pl.ds(pair * SIDE, SIDE), :] = jnp.where(low_lane, sides[0], sides[1])
        return carry

    lax.fori_loop(0, out_ref.shape[0], one_chip, 0, unroll=2)


def first_terms_kernel(core_ref, blocks_ref, hidden_ref, grad_ref, out_ref, turned_ref):
    transpose_kernel_part(grad_ref, turned_ref)
    block_products(1 - core_ref[0], blocks_ref, hidden_ref, turned_ref, out_ref)


def second_terms_kernel(core_ref, blocks_ref, hidden_ref, turned_ref, out_ref):
    block_products(core_ref[0], blocks_ref, hidden_ref, turned_ref, out_ref)


def code_kernel(own_ref, other_ref, out_ref):
    def one_chip(chip, carry):
        totals = []
        for pair in range(PAIRS):
            rows = pl.ds(pair * SIDE, SIDE)
            totals.append(own_ref[chip, rows, :] + other_ref[chip, rows, :])
        peak = functools.reduce(jnp.maximum, [jnp.abs(p) for p in totals])
        peak = jnp.max(peak, axis=0, keepdims=True)
        exponent = jnp.floor(jnp.log(jnp.maximum(peak, 1e-30)) * INV_LN2)
        scale = jnp.exp2(CODE_BITS - exponent)
        code = [jnp.round(p * scale).astype(jnp.int32) for p in totals]
        out_ref[chip, pl.ds(0, SIDE), :] = (code[0] << 16) | (code[1] & 0xFFFF)
        out_ref[chip, pl.ds(SIDE, EXP_ROWS), :] = jnp.broadcast_to(
            exponent.astype(jnp.int32), (EXP_ROWS, LANES)
        )
        return carry

    lax.fori_loop(0, out_ref.shape[0], one_chip, 0, unroll=2)


def sum_kernel(live_ref, recv_ref, grad_ref, square_ref, turned_ref):
    def add(d, totals):
        high, low = totals
        word = recv_ref[d, pl.ds(0, SIDE), :]
        exponent = recv_ref[d, pl.ds(SIDE, EXP_ROWS), :][:1].astype(jnp.float32)
        scale = jnp.exp2(exponent - CODE_BITS)
        high = high + (word >> 16).astype(jnp.float32) * scale
        low = low + ((word << 16) >> 16).astype(jnp.float32) * scale
        return high, low

    zero = jnp.zeros((SIDE, LANES), jnp.float32)
    totals = lax.fori_loop(0, recv_ref.shape[0], add, (zero, zero), unroll=4)
    slot = lax.broadcasted_iota(jnp.int32, (SIDE, LANES), 1) // SIDE
    square = jnp.zeros((SIDE, LANES), jnp.float32)
    for pair in range(PAIRS):
        total = jnp.where(slot + pair * 2 < live_ref[0], totals[pair], 0.0)
        square = square + total * total
        turned_ref[pair] = jnp.concatenate([total.T, total.T], axis=1)
    low_lane = lax.broadcasted_iota(jnp.int32, (TILES, LANES), 1) < SIDE
    for s in range(SLOTS):
        base = (s % 2) * SIDE
        even = turned_ref[s // 2, pl.ds(base, TILES, stride=2), :]
        odd = turned_ref[s // 2, pl.ds(base + 1, TILES, stride=2), :]
        grad_ref[pl.ds(s, TILES, stride=SLOTS), :] = jnp.where(low_lane, even, odd)
    square_ref[...] = jnp.broadcast_to(jnp.sum(square, keepdims=True), square_ref.shape)


def update_kernel(
    live_total_ref, square_ref, grad_ref, master_ref, moment_ref, variance_ref,
    new_master_ref, new_moment_ref, new_variance_ref, clipped_ref, own_ref,
):
    entries = jnp.full((1, LANES), live_total_ref[0], jnp.int32).astype(jnp.float32) * BLOCK
    square = square_ref[0, :1]
    for chip in range(1, square_ref.shape[0]):
        square = square + square_ref[chip, :1]
    clip = jnp.minimum(1.0, 1.0 / jnp.sqrt(square / entries + 1e-06))
    for t in range(TILES):
        lanes = pl.ds(t * LANES, LANES)
        clipped = clip * grad_ref[pl.ds(t * SLOTS, SLOTS), :]
        moment = 0.9 * moment_ref[:, lanes] + 0.1 * clipped
        variance = 0.95 * variance_ref[:, lanes] + 0.05 * clipped * clipped
        master = master_ref[:, lanes]
        moment_hat = moment / (1.0 - 0.9**20)
        variance_hat = variance / (1.0 - 0.95**20)
        step = moment_hat / (jnp.sqrt(variance_hat) + 1e-08) + 0.1 * master
        master = master - 0.02 * step
        clipped_ref[:, lanes] = clipped
        new_moment_ref[:, lanes] = moment
        new_variance_ref[:, lanes] = variance
        new_master_ref[:, lanes] = master
        own_ref[:, lanes] = master.astype(jnp.bfloat16)


def publish_kernel(core_ref, mine_ref, other_ref, out_ref):
    rows = CORES * SLOTS
    group = 2

    def weave(first_ref, second_ref):
        for chip in range(0, first_ref.shape[0], group):
            parts = []
            for k in range(group):
                parts.append(first_ref[chip + k].astype(jnp.float32))
                parts.append(second_ref[chip + k].astype(jnp.float32))
            block = jnp.concatenate(parts, axis=0).astype(jnp.bfloat16)
            out_ref[pl.ds(chip * rows, group * rows), :] = block

    @pl.when(core_ref[0] == 0)
    def _():
        weave(mine_ref, other_ref)

    @pl.when(core_ref[0] == 1)
    def _():
        weave(other_ref, mine_ref)


VMEM = pl.BlockSpec(memory_space=pltpu.VMEM)
SMEM = pl.BlockSpec(memory_space=pltpu.SMEM)
PARAMS = pltpu.CompilerParams(vmem_limit_bytes=40 * 1024 * 1024)


def local(hidden, grad_out, block_list, live_block_count, master, moment, variance):
    chips = lax.axis_size("chip")
    tokens = hidden.shape[0]
    core = lax.axis_index("core").reshape(1)
    me = lax.axis_index(("chip", "core"))
    swap = [(0, 1), (1, 0)]
    blocks = block_list.T
    cost = pl.CostEstimate(
        flops=2 * chips * SLOTS * SIDE * LANES * tokens,
        bytes_accessed=2 * (hidden.size + grad_out.size),
        transcendentals=0,
    )
    terms = jax.ShapeDtypeStruct((chips, PAIRS * SIDE, LANES), jnp.float32)
    partner_terms, turned = pl.pallas_call(
        first_terms_kernel,
        out_shape=(terms, jax.ShapeDtypeStruct(grad_out.shape[::-1], grad_out.dtype)),
        in_specs=[SMEM, SMEM, VMEM, VMEM],
        out_specs=(VMEM, VMEM),
        compiler_params=PARAMS,
        cost_estimate=cost,
        name="partner_terms",
    )(core, blocks, hidden, grad_out)
    arrived = lax.ppermute(partner_terms, "core", swap)
    own_terms = pl.pallas_call(
        second_terms_kernel,
        out_shape=terms,
        in_specs=[SMEM, SMEM, VMEM, VMEM],
        out_specs=VMEM,
        compiler_params=PARAMS,
        cost_estimate=cost,
        name="own_terms",
    )(core, blocks, hidden, turned)
    codes = pl.pallas_call(
        code_kernel,
        out_shape=jax.ShapeDtypeStruct((chips, SIDE + EXP_ROWS, LANES), jnp.int32),
        in_specs=[VMEM, VMEM],
        out_specs=VMEM,
        compiler_params=PARAMS,
        name="code_terms",
    )(own_terms, arrived)
    received = lax.all_to_all(codes, "chip", split_axis=0, concat_axis=0, tiled=True)
    gradient, square = pl.pallas_call(
        sum_kernel,
        out_shape=(
            jax.ShapeDtypeStruct((TILES * SLOTS, LANES), jnp.float32),
            jax.ShapeDtypeStruct((chips, 8, LANES), jnp.float32),
        ),
        in_specs=[SMEM, VMEM],
        out_specs=(VMEM, VMEM),
        scratch_shapes=[pltpu.VMEM((PAIRS, LANES, LANES), jnp.float32)],
        compiler_params=PARAMS,
        name="sum_sources",
    )(lax.dynamic_slice(live_block_count, (me,), (1,)), received)
    square = square + lax.ppermute(square, "core", swap)
    square = lax.all_to_all(square, "chip", split_axis=0, concat_axis=0, tiled=True)
    shape = jax.ShapeDtypeStruct(master.shape, jnp.float32)
    new_master, new_moment, new_variance, clipped, own = pl.pallas_call(
        update_kernel,
        out_shape=(shape, shape, shape, shape, jax.ShapeDtypeStruct(master.shape, jnp.bfloat16)),
        in_specs=[SMEM, VMEM, VMEM, VMEM, VMEM, VMEM],
        out_specs=(VMEM,) * 5,
        compiler_params=PARAMS,
        name="adamw",
    )(jnp.sum(live_block_count).reshape(1), square, gradient, master, moment, variance)
    spread = jnp.broadcast_to(own[None], (chips,) + own.shape)
    mine = lax.all_to_all(spread, "chip", split_axis=0, concat_axis=0, tiled=True)
    other = lax.ppermute(mine, "core", swap)
    published = pl.pallas_call(
        publish_kernel,
        out_shape=jax.ShapeDtypeStruct((chips * CORES * SLOTS, BLOCK), jnp.bfloat16),
        in_specs=[SMEM, VMEM, VMEM],
        out_specs=VMEM,
        compiler_params=PARAMS,
        name="publish",
    )(core, mine, other)
    return new_master, new_moment, new_variance, clipped, published


def solution(mesh):
    devices = mesh.devices.reshape(-1, CORES)
    rows = P(("chip", "core"), None)
    return jax.shard_map(
        local,
        mesh=Mesh(devices, ("chip", "core")),
        in_specs=(rows, rows, P(), P(), rows, rows, rows),
        out_specs=(rows, rows, rows, rows, P()),
        check_vma=False,
    )
```

```python
import functools

import jax
import jax.numpy as jnp
from jax import lax
from jax.experimental import pallas as pl
from jax.experimental.pallas import tpu as pltpu
from jax.sharding import Mesh
from jax.sharding import PartitionSpec as P

SIDE = 64
LANES = 128
SLOTS = 4
PAIRS = SLOTS // 2
BLOCK = SIDE * SIDE
TILES = BLOCK // LANES
EXP_ROWS = 8
CODE_BITS = 13
CORES = 2
AXES = ("chip", "core")
INV_LN2 = 1.4426950408889634


def turn_kernel(grad_ref, turned_ref):
    for k in range(grad_ref.shape[1] // LANES):
        turned_ref[pl.ds(k * LANES, LANES), :] = grad_ref[:, pl.ds(k * LANES, LANES)].T


def block_products(core, blocks_ref, hidden_ref, turned_ref, out_ref):
    low_lane = lax.broadcasted_iota(jnp.int32, (SIDE, LANES), 1) < SIDE

    def one_chip(chip, carry):
        owner = chip * CORES + core
        for pair in range(PAIRS):
            sides = []
            for k in range(2):
                slot = owner * SLOTS + pair * 2 + k
                r = blocks_ref[0, slot]
                c = blocks_ref[1, slot]
                left = turned_ref[pl.ds(pl.multiple_of(c * SIDE, SIDE), SIDE), :]
                right = hidden_ref[:, pl.ds(pl.multiple_of((r // 2) * LANES, LANES), LANES)]
                product = jnp.dot(left, right, preferred_element_type=jnp.float32)
                sides.append(pltpu.roll(product, ((r + k) % 2) * SIDE, 1))
            out_ref[chip, pl.ds(pair * SIDE, SIDE), :] = jnp.where(low_lane, sides[0], sides[1])
        return carry

    lax.fori_loop(0, out_ref.shape[0], one_chip, 0, unroll=2)


def partner_terms_kernel(core_ref, blocks_ref, hidden_ref, turned_ref, out_ref):
    block_products(1 - core_ref[0], blocks_ref, hidden_ref, turned_ref, out_ref)


def own_terms_kernel(
    core_ref, blocks_ref, hidden_ref, turned_ref, master_in, moment_in, variance_in,
    out_ref, master_ref, moment_ref, variance_ref,
):
    block_products(core_ref[0], blocks_ref, hidden_ref, turned_ref, out_ref)
    master_ref[...] = master_in[...]
    moment_ref[...] = moment_in[...]
    variance_ref[...] = variance_in[...]


def code_kernel(own_ref, other_ref, out_ref):
    def one_chip(chip, carry):
        totals = []
        for pair in range(PAIRS):
            rows = pl.ds(pair * SIDE, SIDE)
            totals.append(own_ref[chip, rows, :] + other_ref[chip, rows, :])
        peak = functools.reduce(jnp.maximum, [jnp.abs(p) for p in totals])
        peak = jnp.max(peak, axis=0, keepdims=True)
        exponent = jnp.floor(jnp.log(jnp.maximum(peak, 1e-30)) * INV_LN2)
        scale = jnp.exp2(CODE_BITS - exponent)
        code = [jnp.round(p * scale).astype(jnp.int32) for p in totals]
        out_ref[chip, pl.ds(0, SIDE), :] = (code[0] << 16) | (code[1] & 0xFFFF)
        out_ref[chip, pl.ds(SIDE, EXP_ROWS), :] = jnp.broadcast_to(
            exponent.astype(jnp.int32), (EXP_ROWS, LANES)
        )
        return carry

    lax.fori_loop(0, out_ref.shape[0], one_chip, 0, unroll=2)


def sum_kernel(me_ref, live_ref, recv_ref, grad_ref, square_ref, turned_ref):
    def add(d, totals):
        high, low = totals
        word = recv_ref[d, pl.ds(0, SIDE), :]
        exponent = recv_ref[d, pl.ds(SIDE, EXP_ROWS), :][:1].astype(jnp.float32)
        scale = jnp.exp2(exponent - CODE_BITS)
        high = high + (word >> 16).astype(jnp.float32) * scale
        low = low + ((word << 16) >> 16).astype(jnp.float32) * scale
        return high, low

    live = live_ref[me_ref[0]]
    zero = jnp.zeros((SIDE, LANES), jnp.float32)
    totals = lax.fori_loop(0, recv_ref.shape[0], add, (zero, zero), unroll=4)
    slot = lax.broadcasted_iota(jnp.int32, (SIDE, LANES), 1) // SIDE
    square = jnp.zeros((SIDE, LANES), jnp.float32)
    for pair in range(PAIRS):
        total = jnp.where(slot + pair * 2 < live, totals[pair], 0.0)
        square = square + total * total
        turned_ref[pair] = jnp.concatenate([total.T, total.T], axis=1)
    low_lane = lax.broadcasted_iota(jnp.int32, (TILES, LANES), 1) < SIDE
    for s in range(SLOTS):
        base = (s % 2) * SIDE
        even = turned_ref[s // 2, pl.ds(base, TILES, stride=2), :]
        odd = turned_ref[s // 2, pl.ds(base + 1, TILES, stride=2), :]
        grad_ref[pl.ds(s, TILES, stride=SLOTS), :] = jnp.where(low_lane, even, odd)
    square_ref[...] = jnp.broadcast_to(jnp.sum(square, keepdims=True), square_ref.shape)


def update_kernel(
    live_ref, square_ref, grad_ref, master_ref, moment_ref, variance_ref,
    new_master_ref, new_moment_ref, new_variance_ref, clipped_ref, own_ref,
):
    live_total = live_ref[0]
    square = square_ref[0, :1]
    for owner in range(1, square_ref.shape[0]):
        live_total = live_total + live_ref[owner]
        square = square + square_ref[owner, :1]
    entries = jnp.full((1, LANES), live_total, jnp.int32).astype(jnp.float32) * BLOCK
    clip = jnp.minimum(1.0, 1.0 / jnp.sqrt(square / entries + 1e-06))
    for t in range(TILES):
        lanes = pl.ds(t * LANES, LANES)
        clipped = clip * grad_ref[pl.ds(t * SLOTS, SLOTS), :]
        moment = 0.9 * moment_ref[:, lanes] + 0.1 * clipped
        variance = 0.95 * variance_ref[:, lanes] + 0.05 * clipped * clipped
        master = master_ref[:, lanes]
        moment_hat = moment / (1.0 - 0.9**20)
        variance_hat = variance / (1.0 - 0.95**20)
        step = moment_hat / (jnp.sqrt(variance_hat) + 1e-08) + 0.1 * master
        master = master - 0.02 * step
        clipped_ref[:, lanes] = clipped
        new_moment_ref[:, lanes] = moment
        new_variance_ref[:, lanes] = variance
        new_master_ref[:, lanes] = master
        own_ref[:, lanes] = master.astype(jnp.bfloat16)


def publish_kernel(core_ref, mine_ref, other_ref, out_ref):
    rows = CORES * SLOTS
    group = 2

    def weave(first_ref, second_ref):
        for chip in range(0, first_ref.shape[0], group):
            parts = []
            for k in range(group):
                parts.append(first_ref[chip + k].astype(jnp.float32))
                parts.append(second_ref[chip + k].astype(jnp.float32))
            block = jnp.concatenate(parts, axis=0).astype(jnp.bfloat16)
            out_ref[pl.ds(chip * rows, group * rows), :] = block

    @pl.when(core_ref[0] == 0)
    def _():
        weave(mine_ref, other_ref)

    @pl.when(core_ref[0] == 1)
    def _():
        weave(other_ref, mine_ref)


VMEM = pl.BlockSpec(memory_space=pltpu.VMEM)
SMEM = pl.BlockSpec(memory_space=pltpu.SMEM)
FLOPS_TURN = 6000
PARAMS = pltpu.CompilerParams(vmem_limit_bytes=40 * 1024 * 1024)


def local(hidden, grad_out, block_list, live_block_count, master, moment, variance):
    chips = lax.axis_size("chip")
    tokens = hidden.shape[0]
    core = lax.axis_index("core").reshape(1)
    me = lax.axis_index(AXES).reshape(1)
    swap = [(0, 1), (1, 0)]
    shape = jax.ShapeDtypeStruct(master.shape, jnp.float32)
    blocks = block_list.T
    cost = pl.CostEstimate(
        flops=2 * chips * SLOTS * SIDE * LANES * tokens,
        bytes_accessed=2 * (hidden.size + grad_out.size),
        transcendentals=0,
    )
    terms = jax.ShapeDtypeStruct((chips, PAIRS * SIDE, LANES), jnp.float32)
    turned = pl.pallas_call(
        turn_kernel,
        out_shape=jax.ShapeDtypeStruct(grad_out.shape[::-1], grad_out.dtype),
        in_specs=[VMEM],
        out_specs=VMEM,
        compiler_params=PARAMS,
        cost_estimate=pl.CostEstimate(
            flops=FLOPS_TURN * grad_out.size, bytes_accessed=4 * grad_out.size, transcendentals=0
        ),
        name="turn_grad_out",
    )(grad_out)
    partner_terms = pl.pallas_call(
        partner_terms_kernel,
        out_shape=terms,
        in_specs=[SMEM, SMEM, VMEM, VMEM],
        out_specs=VMEM,
        compiler_params=PARAMS,
        cost_estimate=cost,
        name="partner_terms",
    )(core, blocks, hidden, turned)
    arrived = lax.ppermute(partner_terms, "core", swap)
    own_terms, master, moment, variance = pl.pallas_call(
        own_terms_kernel,
        out_shape=(terms, shape, shape, shape),
        in_specs=[SMEM, SMEM] + [VMEM] * 5,
        out_specs=(VMEM,) * 4,
        compiler_params=PARAMS,
        cost_estimate=cost,
        name="own_terms",
    )(core, blocks, hidden, turned, master, moment, variance)
    codes = pl.pallas_call(
        code_kernel,
        out_shape=jax.ShapeDtypeStruct((chips, SIDE + EXP_ROWS, LANES), jnp.int32),
        in_specs=[VMEM, VMEM],
        out_specs=VMEM,
        compiler_params=PARAMS,
        name="code_terms",
    )(own_terms, arrived)
    received = lax.all_to_all(codes, "chip", split_axis=0, concat_axis=0, tiled=True)
    gradient, square = pl.pallas_call(
        sum_kernel,
        out_shape=(
            jax.ShapeDtypeStruct((TILES * SLOTS, LANES), jnp.float32),
            jax.ShapeDtypeStruct((chips * CORES, 8, LANES), jnp.float32),
        ),
        in_specs=[SMEM, SMEM, VMEM],
        out_specs=(VMEM, VMEM),
        scratch_shapes=[pltpu.VMEM((PAIRS, LANES, LANES), jnp.float32)],
        compiler_params=PARAMS,
        name="sum_sources",
    )(me, live_block_count, received)
    square = lax.all_to_all(square, AXES[::-1], split_axis=0, concat_axis=0, tiled=True)
    new_master, new_moment, new_variance, clipped, own = pl.pallas_call(
        update_kernel,
        out_shape=(shape, shape, shape, shape, jax.ShapeDtypeStruct(master.shape, jnp.bfloat16)),
        in_specs=[SMEM, VMEM, VMEM, VMEM, VMEM, VMEM],
        out_specs=(VMEM,) * 5,
        compiler_params=PARAMS,
        name="adamw",
    )(live_block_count, square, gradient, master, moment, variance)
    spread = jnp.broadcast_to(own[None], (chips,) + own.shape)
    mine = lax.all_to_all(spread, "chip", split_axis=0, concat_axis=0, tiled=True)
    other = lax.ppermute(mine, "core", swap)
    published = pl.pallas_call(
        publish_kernel,
        out_shape=jax.ShapeDtypeStruct((chips * CORES * SLOTS, BLOCK), jnp.bfloat16),
        in_specs=[SMEM, VMEM, VMEM],
        out_specs=VMEM,
        compiler_params=PARAMS,
        name="publish",
    )(core, mine, other)
    return new_master, new_moment, new_variance, clipped, published


def solution(mesh):
    devices = mesh.devices.reshape(-1, CORES)
    rows = P(AXES, None)
    return jax.shard_map(
        local,
        mesh=Mesh(devices, AXES),
        in_specs=(rows, rows, P(), P(), rows, rows, rows),
        out_specs=(rows, rows, rows, rows, P()),
        check_vma=False,
    )
```

```python
import functools

import jax
import jax.numpy as jnp
from jax import lax
from jax.experimental import pallas as pl
from jax.experimental.pallas import tpu as pltpu
from jax.sharding import Mesh
from jax.sharding import PartitionSpec as P

SIDE = 64
LANES = 128
SLOTS = 4
PAIRS = SLOTS // 2
BLOCK = SIDE * SIDE
TILES = BLOCK // LANES
EXP_ROWS = 8
CODE_BITS = 13
GRAD_PARTS = 4
HIDDEN_PARTS = 8
STORE_PARTS = 8
CORES = 2
AXES = ("chip", "core")
INV_LN2 = 1.4426950408889634


def block_products(core, blocks_ref, hidden_ref, turned_ref, out_ref):
    low_lane = lax.broadcasted_iota(jnp.int32, (SIDE, LANES), 1) < SIDE

    def one_chip(chip, carry):
        owner = chip * CORES + core
        for pair in range(PAIRS):
            lefts, rights, rows = [], [], []
            for k in range(2):
                slot = owner * SLOTS + pair * 2 + k
                r = blocks_ref[0, slot]
                c = blocks_ref[1, slot]
                lefts.append(turned_ref[pl.ds(pl.multiple_of(c * SIDE, SIDE), SIDE), :])
                lanes = pl.ds(pl.multiple_of((r // 2) * LANES, LANES), LANES)
                rights.append(hidden_ref[:, lanes])
                rows.append(r)
            product = jnp.dot(
                jnp.concatenate(lefts, axis=0),
                jnp.concatenate(rights, axis=1),
                preferred_element_type=jnp.float32,
            )
            first = pltpu.roll(product[:SIDE, :LANES], (rows[0] % 2) * SIDE, 1)
            second = pltpu.roll(product[SIDE:, LANES:], ((rows[1] + 1) % 2) * SIDE, 1)
            out_ref[chip, pl.ds(pair * SIDE, SIDE), :] = jnp.where(low_lane, first, second)
        return carry

    lax.fori_loop(0, out_ref.shape[0], one_chip, 0, unroll=4)


def partner_terms_kernel(
    place_ref, blocks_hbm, hidden_hbm, grad_hbm, master_hbm, moment_hbm, variance_hbm,
    out_ref, hidden_ref, turned_ref, master_ref, moment_ref, variance_ref,
    blocks_ref, grad_ref, sems,
):
    copies = [pltpu.make_async_copy(blocks_hbm, blocks_ref, sems.at[0])]
    for source, target, parts in ((grad_hbm, grad_ref, GRAD_PARTS), (hidden_hbm, hidden_ref, HIDDEN_PARTS)):
        step = source.shape[0] // parts
        for k in range(parts):
            rows = pl.ds(k * step, step)
            copies.append(
                pltpu.make_async_copy(source.at[rows], target.at[rows], sems.at[len(copies)])
            )
    for source, target in (
        (master_hbm, master_ref), (moment_hbm, moment_ref), (variance_hbm, variance_ref)
    ):
        copies.append(pltpu.make_async_copy(source, target, sems.at[len(copies)]))
    for copy in copies:
        copy.start()
    grad_end = 1 + GRAD_PARTS
    hidden_end = grad_end + HIDDEN_PARTS
    for copy in copies[:grad_end]:
        copy.wait()
    for k in range(grad_ref.shape[1] // LANES):
        turned_ref[pl.ds(k * LANES, LANES), :] = grad_ref[:, pl.ds(k * LANES, LANES)].T
    for copy in copies[grad_end:hidden_end]:
        copy.wait()
    block_products(1 - place_ref[0], blocks_ref, hidden_ref, turned_ref, out_ref)
    for copy in copies[hidden_end:]:
        copy.wait()


def own_terms_kernel(
    place_ref, blocks_ref, live_ref, hidden_ref, turned_ref, out_ref, live_rows_ref
):
    block_products(place_ref[0], blocks_ref, hidden_ref, turned_ref, out_ref)
    total = live_ref[0]
    for owner in range(1, live_ref.shape[0]):
        total = total + live_ref[owner]
    live_rows_ref[pl.ds(0, 8), :] = jnp.full((8, LANES), live_ref[place_ref[1]], jnp.int32)
    live_rows_ref[pl.ds(8, 8), :] = jnp.full((8, LANES), total, jnp.int32)


def code_kernel(own_ref, other_ref, out_ref):
    def one_chip(chip, carry):
        totals = []
        for pair in range(PAIRS):
            rows = pl.ds(pair * SIDE, SIDE)
            totals.append(own_ref[chip, rows, :] + other_ref[chip, rows, :])
        peak = functools.reduce(jnp.maximum, [jnp.abs(p) for p in totals])
        peak = jnp.max(peak, axis=0, keepdims=True)
        exponent = jnp.floor(jnp.log(jnp.maximum(peak, 1e-30)) * INV_LN2)
        scale = jnp.exp2(CODE_BITS - exponent)
        code = [jnp.round(p * scale).astype(jnp.int32) for p in totals]
        out_ref[chip, pl.ds(0, SIDE), :] = (code[0] << 16) | (code[1] & 0xFFFF)
        out_ref[chip, pl.ds(SIDE, EXP_ROWS), :] = jnp.broadcast_to(
            exponent.astype(jnp.int32), (EXP_ROWS, LANES)
        )
        return carry

    lax.fori_loop(0, out_ref.shape[0], one_chip, 0, unroll=2)


def sum_kernel(live_ref, recv_ref, grad_ref, square_ref, turned_ref):
    def add(d, totals):
        high, low = totals
        word = recv_ref[d, pl.ds(0, SIDE), :]
        exponent = recv_ref[d, pl.ds(SIDE, EXP_ROWS), :][:1].astype(jnp.float32)
        scale = jnp.exp2(exponent - CODE_BITS)
        high = high + (word >> 16).astype(jnp.float32) * scale
        low = low + ((word << 16) >> 16).astype(jnp.float32) * scale
        return high, low

    live = live_ref[0:1, :]
    zero = jnp.zeros((SIDE, LANES), jnp.float32)
    totals = lax.fori_loop(0, recv_ref.shape[0], add, (zero, zero), unroll=4)
    slot = lax.broadcasted_iota(jnp.int32, (SIDE, LANES), 1) // SIDE
    square = jnp.zeros((SIDE, LANES), jnp.float32)
    for pair in range(PAIRS):
        total = jnp.where(slot + pair * 2 < live, totals[pair], 0.0)
        square = square + total * total
        turned_ref[pair] = jnp.concatenate([total.T, total.T], axis=1)
    low_lane = lax.broadcasted_iota(jnp.int32, (TILES, LANES), 1) < SIDE
    for s in range(SLOTS):
        base = (s % 2) * SIDE
        even = turned_ref[s // 2, pl.ds(base, TILES, stride=2), :]
        odd = turned_ref[s // 2, pl.ds(base + 1, TILES, stride=2), :]
        grad_ref[pl.ds(s, TILES, stride=SLOTS), :] = jnp.where(low_lane, even, odd)
    square = jnp.sum(square, axis=0, keepdims=True)
    square_ref[...] = jnp.broadcast_to(square[None], square_ref.shape)


def update_kernel(
    live_ref, square_ref, grad_ref, master_ref, moment_ref, variance_ref,
    spread_ref, new_master_ref, new_moment_ref, new_variance_ref, clipped_ref,
):
    square = square_ref[0]
    for owner in range(1, square_ref.shape[0]):
        square = square + square_ref[owner]
    square = jnp.sum(square, axis=1, keepdims=True)
    entries = live_ref[8:9, :].astype(jnp.float32) * BLOCK
    clip = jnp.minimum(1.0, 1.0 / jnp.sqrt(square / entries + 1e-06))
    for t in range(TILES):
        lanes = pl.ds(t * LANES, LANES)
        clipped = clip * grad_ref[pl.ds(t * SLOTS, SLOTS), :]
        moment = 0.9 * moment_ref[:, lanes] + 0.1 * clipped
        variance = 0.95 * variance_ref[:, lanes] + 0.05 * clipped * clipped
        master = master_ref[:, lanes]
        moment_hat = moment / (1.0 - 0.9**20)
        variance_hat = variance / (1.0 - 0.95**20)
        step = moment_hat / (jnp.sqrt(variance_hat) + 1e-08) + 0.1 * master
        master = master - 0.02 * step
        clipped_ref[:, lanes] = clipped
        new_moment_ref[:, lanes] = moment
        new_variance_ref[:, lanes] = variance
        new_master_ref[:, lanes] = master
    own = new_master_ref[...].astype(jnp.bfloat16)
    for chip in range(spread_ref.shape[0]):
        spread_ref[chip] = own


def store_kernel(after_ref, *refs):
    half = len(refs) // 2
    for source, target in zip(refs[:half], refs[half:]):
        target[...] = source[...]


def publish_kernel(place_ref, mine_ref, other_ref, out_hbm, woven_ref, sems):
    rows = CORES * SLOTS
    group = sems.shape[0]
    step = mine_ref.shape[0] // group

    def weave(first_ref, second_ref):
        copies = []
        for g in range(group):
            parts = []
            for chip in range(g * step, (g + 1) * step):
                parts.append(first_ref[chip].astype(jnp.float32))
                parts.append(second_ref[chip].astype(jnp.float32))
            block = jnp.concatenate(parts, axis=0).astype(jnp.bfloat16)
            span = pl.ds(g * step * rows, step * rows)
            woven_ref[span, :] = block
            copies.append(
                pltpu.make_async_copy(woven_ref.at[span], out_hbm.at[span], sems.at[g])
            )
            copies[-1].start()
        for copy in copies:
            copy.wait()

    @pl.when(place_ref[0] == 0)
    def _():
        weave(mine_ref, other_ref)

    @pl.when(place_ref[0] == 1)
    def _():
        weave(other_ref, mine_ref)


VMEM = pl.BlockSpec(memory_space=pltpu.VMEM)
SMEM = pl.BlockSpec(memory_space=pltpu.SMEM)
ANY = pl.BlockSpec(memory_space=pl.ANY)
PARAMS = pltpu.CompilerParams(vmem_limit_bytes=40 * 1024 * 1024)


def local(hidden, grad_out, block_list, live_block_count, master, moment, variance):
    chips = lax.axis_size("chip")
    tokens = hidden.shape[0]
    place = jnp.stack([lax.axis_index("core"), lax.axis_index(AXES)])
    swap = [(0, 1), (1, 0)]
    shape = jax.ShapeDtypeStruct(master.shape, jnp.float32)
    kept = pltpu.VMEM(master.shape, jnp.float32)
    blocks = block_list.T
    cost = pl.CostEstimate(
        flops=2 * chips * SLOTS * SIDE * LANES * tokens,
        bytes_accessed=2 * (hidden.size + grad_out.size),
        transcendentals=0,
    )
    terms = pltpu.VMEM((chips, PAIRS * SIDE, LANES), jnp.float32)
    partner_terms, hidden, turned, master, moment, variance = pl.pallas_call(
        partner_terms_kernel,
        out_shape=(
            terms,
            pltpu.VMEM(hidden.shape, hidden.dtype),
            pltpu.VMEM(grad_out.shape[::-1], grad_out.dtype),
            kept,
            kept,
            kept,
        ),
        in_specs=[SMEM] + [ANY] * 6,
        out_specs=(VMEM,) * 6,
        scratch_shapes=[
            pltpu.SMEM(blocks.shape, jnp.int32),
            pltpu.VMEM(grad_out.shape, grad_out.dtype),
            pltpu.SemaphoreType.DMA((4 + GRAD_PARTS + HIDDEN_PARTS,)),
        ],
        compiler_params=PARAMS,
        cost_estimate=cost,
        name="partner_terms",
    )(
        place,
        *(
            pltpu.with_memory_space_constraint(x, pltpu.HBM)
            for x in (blocks, hidden, grad_out, master, moment, variance)
        ),
    )
    arrived = lax.ppermute(partner_terms, "core", swap)
    own_terms, live_rows = pl.pallas_call(
        own_terms_kernel,
        out_shape=(terms, pltpu.VMEM((16, LANES), jnp.int32)),
        in_specs=[SMEM, SMEM, SMEM, VMEM, VMEM],
        out_specs=(VMEM, VMEM),
        compiler_params=PARAMS,
        cost_estimate=cost,
        name="own_terms",
    )(place, blocks, live_block_count, hidden, turned)
    codes = pl.pallas_call(
        code_kernel,
        out_shape=pltpu.VMEM((chips, SIDE + EXP_ROWS, LANES), jnp.int32),
        in_specs=[VMEM, VMEM],
        out_specs=VMEM,
        compiler_params=PARAMS,
        name="code_terms",
    )(own_terms, arrived)
    received = lax.all_to_all(codes, "chip", split_axis=0, concat_axis=0, tiled=True)
    gradient, square = pl.pallas_call(
        sum_kernel,
        out_shape=(
            pltpu.VMEM((TILES * SLOTS, LANES), jnp.float32),
            pltpu.VMEM((chips * CORES, 1, LANES), jnp.float32),
        ),
        in_specs=[VMEM, VMEM],
        out_specs=(VMEM, VMEM),
        scratch_shapes=[pltpu.VMEM((PAIRS, LANES, LANES), jnp.float32)],
        compiler_params=PARAMS,
        name="sum_sources",
    )(live_rows, received)
    square = lax.all_to_all(square, AXES[::-1], split_axis=0, concat_axis=0, tiled=True)
    spread, *updated = pl.pallas_call(
        update_kernel,
        out_shape=(pltpu.VMEM((chips,) + master.shape, jnp.bfloat16), kept, kept, kept, kept),
        in_specs=[VMEM] * 6,
        out_specs=(VMEM,) * 5,
        compiler_params=PARAMS,
        name="adamw",
    )(live_rows, square, gradient, master, moment, variance)
    mine = lax.all_to_all(spread, "chip", split_axis=0, concat_axis=0, tiled=True)
    other = lax.ppermute(mine, "core", swap)
    results = pl.pallas_call(
        store_kernel,
        out_shape=(shape,) * 4,
        in_specs=[ANY] + [VMEM] * 4,
        out_specs=(VMEM,) * 4,
        compiler_params=PARAMS,
        name="store_state",
    )(mine, *updated)
    published = pl.pallas_call(
        publish_kernel,
        out_shape=jax.ShapeDtypeStruct((chips * CORES * SLOTS, BLOCK), jnp.bfloat16),
        in_specs=[SMEM, VMEM, VMEM],
        out_specs=ANY,
        scratch_shapes=[
            pltpu.VMEM((chips * CORES * SLOTS, BLOCK), jnp.bfloat16),
            pltpu.SemaphoreType.DMA((STORE_PARTS,)),
        ],
        compiler_params=PARAMS,
        name="publish",
    )(place, mine, other)
    return (*results, published)


def solution(mesh):
    devices = mesh.devices.reshape(-1, CORES)
    rows = P(AXES, None)
    return jax.shard_map(
        local,
        mesh=Mesh(devices, AXES),
        in_specs=(rows, rows, P(), P(), rows, rows, rows),
        out_specs=(rows, rows, rows, rows, P()),
        check_vma=False,
    )
```

```python
import functools
import math

import jax
import jax.numpy as jnp
from jax import lax
from jax.experimental import pallas as pl
from jax.experimental.pallas import tpu as pltpu
from jax.sharding import Mesh
from jax.sharding import PartitionSpec as P

SIDE = 64
LANES = 128
SLOTS = 4
PAIRS = SLOTS // 2
BLOCK = SIDE * SIDE
TILES = BLOCK // LANES
LOW_OCTAVE = -36
LARGEST = 6.0
GRAD_PARTS = 4
HIDDEN_PARTS = 8
STORE_PARTS = 2
CORES = 2
AXES = ("chip", "core")
INV_LN2 = 1.4426950408889634


def block_products(core, blocks_ref, hidden_ref, turned_ref, out_ref):
    low_lane = lax.broadcasted_iota(jnp.int32, (SIDE, LANES), 1) < SIDE

    def one_chip(chip, carry):
        owner = chip * CORES + core
        for pair in range(PAIRS):
            lefts, rights, rows = [], [], []
            for k in range(2):
                slot = owner * SLOTS + pair * 2 + k
                r = blocks_ref[0, slot]
                c = blocks_ref[1, slot]
                lefts.append(turned_ref[pl.ds(pl.multiple_of(c * SIDE, SIDE), SIDE), :])
                lanes = pl.ds(pl.multiple_of((r // 2) * LANES, LANES), LANES)
                rights.append(hidden_ref[:, lanes])
                rows.append(r)
            product = jnp.dot(
                jnp.concatenate(lefts, axis=0),
                jnp.concatenate(rights, axis=1),
                preferred_element_type=jnp.float32,
            )
            first = pltpu.roll(product[:SIDE, :LANES], (rows[0] % 2) * SIDE, 1)
            second = pltpu.roll(product[SIDE:, LANES:], ((rows[1] + 1) % 2) * SIDE, 1)
            out_ref[chip, pl.ds(pair * SIDE, SIDE), :] = jnp.where(low_lane, first, second)
        return carry

    lax.fori_loop(0, out_ref.shape[0], one_chip, 0, unroll=4)


def partner_terms_kernel(
    place_ref, blocks_hbm, hidden_hbm, grad_hbm, master_hbm, moment_hbm, variance_hbm,
    out_ref, hidden_ref, turned_ref, master_ref, moment_ref, variance_ref,
    blocks_ref, grad_ref, sems,
):
    copies = [pltpu.make_async_copy(blocks_hbm, blocks_ref, sems.at[0])]
    for source, target, parts in ((grad_hbm, grad_ref, GRAD_PARTS), (hidden_hbm, hidden_ref, HIDDEN_PARTS)):
        step = source.shape[0] // parts
        for k in range(parts):
            rows = pl.ds(k * step, step)
            copies.append(
                pltpu.make_async_copy(source.at[rows], target.at[rows], sems.at[len(copies)])
            )
    for source, target in (
        (master_hbm, master_ref), (moment_hbm, moment_ref), (variance_hbm, variance_ref)
    ):
        copies.append(pltpu.make_async_copy(source, target, sems.at[len(copies)]))
    for copy in copies:
        copy.start()
    grad_end = 1 + GRAD_PARTS
    hidden_end = grad_end + HIDDEN_PARTS
    for copy in copies[:grad_end]:
        copy.wait()
    for k in range(grad_ref.shape[1] // LANES):
        turned_ref[pl.ds(k * LANES, LANES), :] = grad_ref[:, pl.ds(k * LANES, LANES)].T
    for copy in copies[grad_end:hidden_end]:
        copy.wait()
    block_products(1 - place_ref[0], blocks_ref, hidden_ref, turned_ref, out_ref)
    for copy in copies[hidden_end:]:
        copy.wait()


def own_terms_kernel(
    place_ref, blocks_ref, live_ref, hidden_ref, turned_ref, out_ref, live_rows_ref
):
    block_products(place_ref[0], blocks_ref, hidden_ref, turned_ref, out_ref)
    total = live_ref[0]
    for owner in range(1, live_ref.shape[0]):
        total = total + live_ref[owner]
    live_rows_ref[pl.ds(0, 8), :] = jnp.full((8, LANES), live_ref[place_ref[1]], jnp.int32)
    live_rows_ref[pl.ds(8, 8), :] = jnp.full((8, LANES), total, jnp.int32)


def code_kernel(per_octave, own_ref, other_ref, out_ref):
    def encode(value):
        octave = jnp.log(jnp.maximum(jnp.abs(value), 2.0**LOW_OCTAVE)) * INV_LN2
        code = (octave - LOW_OCTAVE) * per_octave
        return jnp.round(jnp.where(value < 0, -code, code)).astype(jnp.int32)

    def one_chip(chip, carry):
        code = []
        for pair in range(PAIRS):
            rows = pl.ds(pair * SIDE, SIDE)
            code.append(encode(own_ref[chip, rows, :] + other_ref[chip, rows, :]))
        out_ref[chip] = (code[0] << 16) | (code[1] & 0xFFFF)
        return carry

    lax.fori_loop(0, out_ref.shape[0], one_chip, 0, unroll=2)


def sum_kernel(per_octave, live_ref, recv_ref, grad_ref, square_ref, turned_ref):
    def decode(code):
        value = code.astype(jnp.float32)
        size = jnp.exp2(jnp.abs(value) * (1.0 / per_octave) + LOW_OCTAVE)
        return jnp.where(code > 0, size, jnp.where(code < 0, -size, 0.0))

    def add(d, totals):
        word = recv_ref[d]
        return totals[0] + decode(word >> 16), totals[1] + decode((word << 16) >> 16)

    live = live_ref[0:1, :]
    zero = jnp.zeros((SIDE, LANES), jnp.float32)
    totals = lax.fori_loop(0, recv_ref.shape[0], add, (zero, zero), unroll=4)
    slot = lax.broadcasted_iota(jnp.int32, (SIDE, LANES), 1) // SIDE
    square = jnp.zeros((SIDE, LANES), jnp.float32)
    for pair in range(PAIRS):
        total = jnp.where(slot + pair * 2 < live, totals[pair], 0.0)
        square = square + total * total
        turned_ref[pair] = jnp.concatenate([total.T, total.T], axis=1)
    low_lane = lax.broadcasted_iota(jnp.int32, (TILES, LANES), 1) < SIDE
    for s in range(SLOTS):
        base = (s % 2) * SIDE
        even = turned_ref[s // 2, pl.ds(base, TILES, stride=2), :]
        odd = turned_ref[s // 2, pl.ds(base + 1, TILES, stride=2), :]
        grad_ref[pl.ds(s, TILES, stride=SLOTS), :] = jnp.where(low_lane, even, odd)
    square = jnp.sum(square, axis=0, keepdims=True)
    square_ref[...] = jnp.broadcast_to(square[None], square_ref.shape)


def update_kernel(
    live_ref, square_ref, grad_ref, master_ref, moment_ref, variance_ref,
    spread_ref, new_master_ref, new_moment_ref, new_variance_ref, clipped_ref,
):
    square = square_ref[0]
    for owner in range(1, square_ref.shape[0]):
        square = square + square_ref[owner]
    square = jnp.sum(square, axis=1, keepdims=True)
    entries = live_ref[8:9, :].astype(jnp.float32) * BLOCK
    clip = jnp.minimum(1.0, 1.0 / jnp.sqrt(square / entries + 1e-06))
    for t in range(TILES):
        lanes = pl.ds(t * LANES, LANES)
        clipped = clip * grad_ref[pl.ds(t * SLOTS, SLOTS), :]
        moment = 0.9 * moment_ref[:, lanes] + 0.1 * clipped
        variance = 0.95 * variance_ref[:, lanes] + 0.05 * clipped * clipped
        master = master_ref[:, lanes]
        moment_hat = moment / (1.0 - 0.9**20)
        variance_hat = variance / (1.0 - 0.95**20)
        step = moment_hat / (jnp.sqrt(variance_hat) + 1e-08) + 0.1 * master
        master = master - 0.02 * step
        clipped_ref[:, lanes] = clipped
        new_moment_ref[:, lanes] = moment
        new_variance_ref[:, lanes] = variance
        new_master_ref[:, lanes] = master
    own = new_master_ref[...].astype(jnp.bfloat16)
    for chip in range(spread_ref.shape[0]):
        spread_ref[chip] = own


def store_kernel(after_ref, *refs):
    half = len(refs) // 2
    for source, target in zip(refs[:half], refs[half:]):
        target[...] = source[...]


def publish_kernel(place_ref, mine_ref, other_ref, out_hbm, woven_ref, sems):
    rows = CORES * SLOTS
    group = sems.shape[0]
    step = mine_ref.shape[0] // group

    def weave(first_ref, second_ref):
        copies = []
        for g in range(group):
            for chip in range(g * step, (g + 1) * step, 2):
                parts = []
                for k in range(2):
                    parts.append(first_ref[chip + k].astype(jnp.float32))
                    parts.append(second_ref[chip + k].astype(jnp.float32))
                block = jnp.concatenate(parts, axis=0).astype(jnp.bfloat16)
                woven_ref[pl.ds(chip * rows, 2 * rows), :] = block
            span = pl.ds(g * step * rows, step * rows)
            copies.append(
                pltpu.make_async_copy(woven_ref.at[span], out_hbm.at[span], sems.at[g])
            )
            copies[-1].start()
        for copy in copies:
            copy.wait()

    @pl.when(place_ref[0] == 0)
    def _():
        weave(mine_ref, other_ref)

    @pl.when(place_ref[0] == 1)
    def _():
        weave(other_ref, mine_ref)


VMEM = pl.BlockSpec(memory_space=pltpu.VMEM)
SMEM = pl.BlockSpec(memory_space=pltpu.SMEM)
ANY = pl.BlockSpec(memory_space=pl.ANY)
PARAMS = pltpu.CompilerParams(vmem_limit_bytes=40 * 1024 * 1024)


def local(hidden, grad_out, block_list, live_block_count, master, moment, variance):
    chips = lax.axis_size("chip")
    tokens = hidden.shape[0]
    place = jnp.stack([lax.axis_index("core"), lax.axis_index(AXES)])
    swap = [(0, 1), (1, 0)]
    shape = jax.ShapeDtypeStruct(master.shape, jnp.float32)
    kept = pltpu.VMEM(master.shape, jnp.float32)
    blocks = block_list.T
    top_octave = math.log2(CORES * tokens * LARGEST * LARGEST) + 0.05
    per_octave = 32767 / (top_octave - LOW_OCTAVE)
    cost = pl.CostEstimate(
        flops=2 * chips * SLOTS * SIDE * LANES * tokens,
        bytes_accessed=2 * (hidden.size + grad_out.size),
        transcendentals=0,
    )
    terms = pltpu.VMEM((chips, PAIRS * SIDE, LANES), jnp.float32)
    partner_terms, hidden, turned, master, moment, variance = pl.pallas_call(
        partner_terms_kernel,
        out_shape=(
            terms,
            pltpu.VMEM(hidden.shape, hidden.dtype),
            pltpu.VMEM(grad_out.shape[::-1], grad_out.dtype),
            kept,
            kept,
            kept,
        ),
        in_specs=[SMEM] + [ANY] * 6,
        out_specs=(VMEM,) * 6,
        scratch_shapes=[
            pltpu.SMEM(blocks.shape, jnp.int32),
            pltpu.VMEM(grad_out.shape, grad_out.dtype),
            pltpu.SemaphoreType.DMA((4 + GRAD_PARTS + HIDDEN_PARTS,)),
        ],
        compiler_params=PARAMS,
        cost_estimate=cost,
        name="partner_terms",
    )(
        place,
        *(
            pltpu.with_memory_space_constraint(x, pltpu.HBM)
            for x in (blocks, hidden, grad_out, master, moment, variance)
        ),
    )
    arrived = lax.ppermute(partner_terms, "core", swap)
    own_terms, live_rows = pl.pallas_call(
        own_terms_kernel,
        out_shape=(terms, pltpu.VMEM((16, LANES), jnp.int32)),
        in_specs=[SMEM, SMEM, SMEM, VMEM, VMEM],
        out_specs=(VMEM, VMEM),
        compiler_params=PARAMS,
        cost_estimate=cost,
        name="own_terms",
    )(place, blocks, live_block_count, hidden, turned)
    codes = pl.pallas_call(
        functools.partial(code_kernel, per_octave),
        out_shape=pltpu.VMEM((chips, SIDE, LANES), jnp.int32),
        in_specs=[VMEM, VMEM],
        out_specs=VMEM,
        compiler_params=PARAMS,
        name="code_terms",
    )(own_terms, arrived)
    received = lax.all_to_all(codes, "chip", split_axis=0, concat_axis=0, tiled=True)
    gradient, square = pl.pallas_call(
        functools.partial(sum_kernel, per_octave),
        out_shape=(
            pltpu.VMEM((TILES * SLOTS, LANES), jnp.float32),
            pltpu.VMEM((chips * CORES, 1, LANES), jnp.float32),
        ),
        in_specs=[VMEM, VMEM],
        out_specs=(VMEM, VMEM),
        scratch_shapes=[pltpu.VMEM((PAIRS, LANES, LANES), jnp.float32)],
        compiler_params=PARAMS,
        name="sum_sources",
    )(live_rows, received)
    square = lax.all_to_all(square, AXES[::-1], split_axis=0, concat_axis=0, tiled=True)
    spread, *updated = pl.pallas_call(
        update_kernel,
        out_shape=(pltpu.VMEM((chips,) + master.shape, jnp.bfloat16), kept, kept, kept, kept),
        in_specs=[VMEM] * 6,
        out_specs=(VMEM,) * 5,
        compiler_params=PARAMS,
        name="adamw",
    )(live_rows, square, gradient, master, moment, variance)
    mine = lax.all_to_all(spread, "chip", split_axis=0, concat_axis=0, tiled=True)
    other = lax.ppermute(mine, "core", swap)
    results = pl.pallas_call(
        store_kernel,
        out_shape=(shape,) * 4,
        in_specs=[ANY] + [VMEM] * 4,
        out_specs=(VMEM,) * 4,
        compiler_params=PARAMS,
        name="store_state",
    )(mine, *updated)
    published = pl.pallas_call(
        publish_kernel,
        out_shape=jax.ShapeDtypeStruct((chips * CORES * SLOTS, BLOCK), jnp.bfloat16),
        in_specs=[SMEM, VMEM, VMEM],
        out_specs=ANY,
        scratch_shapes=[
            pltpu.VMEM((chips * CORES * SLOTS, BLOCK), jnp.bfloat16),
            pltpu.SemaphoreType.DMA((STORE_PARTS,)),
        ],
        compiler_params=PARAMS,
        name="publish",
    )(place, mine, other)
    return (*results, published)


def solution(mesh):
    devices = mesh.devices.reshape(-1, CORES)
    rows = P(AXES, None)
    return jax.shard_map(
        local,
        mesh=Mesh(devices, AXES),
        in_specs=(rows, rows, P(), P(), rows, rows, rows),
        out_specs=(rows, rows, rows, rows, P()),
        check_vma=False,
    )
```

```python
import functools
import math

import jax
import jax.numpy as jnp
from jax import lax
from jax.experimental import pallas as pl
from jax.experimental.pallas import tpu as pltpu
from jax.sharding import Mesh
from jax.sharding import PartitionSpec as P

SIDE = 64
LANES = 128
SLOTS = 4
PAIRS = SLOTS // 2
BLOCK = SIDE * SIDE
TILES = BLOCK // LANES
LOW_OCTAVE = -36
LARGEST = 6.0
GRAD_PARTS = 4
HIDDEN_PARTS = 8
CORES = 2
HALVES = 2
AXES = ("half", "chip", "core")
CHIPS = ("chip", "half")
INV_LN2 = 1.4426950408889634


def block_products(core, blocks_ref, hidden_ref, turned_ref, out_ref):
    low_lane = lax.broadcasted_iota(jnp.int32, (SIDE, LANES), 1) < SIDE

    chips = out_ref.shape[0] // HALVES

    def one_chip(peer, carry):
        owner = ((peer % HALVES) * chips + peer // HALVES) * CORES + core
        for pair in range(PAIRS):
            lefts, rights, rows = [], [], []
            for k in range(2):
                slot = owner * SLOTS + pair * 2 + k
                r = blocks_ref[0, slot]
                c = blocks_ref[1, slot]
                lefts.append(turned_ref[pl.ds(pl.multiple_of(c * SIDE, SIDE), SIDE), :])
                lanes = pl.ds(pl.multiple_of((r // 2) * LANES, LANES), LANES)
                rights.append(hidden_ref[:, lanes])
                rows.append(r)
            product = jnp.dot(
                jnp.concatenate(lefts, axis=0),
                jnp.concatenate(rights, axis=1),
                preferred_element_type=jnp.float32,
            )
            first = pltpu.roll(product[:SIDE, :LANES], (rows[0] % 2) * SIDE, 1)
            second = pltpu.roll(product[SIDE:, LANES:], ((rows[1] + 1) % 2) * SIDE, 1)
            out_ref[peer, pl.ds(pair * SIDE, SIDE), :] = jnp.where(low_lane, first, second)
        return carry

    lax.fori_loop(0, out_ref.shape[0], one_chip, 0, unroll=8)


def partner_terms_kernel(
    place_ref, blocks_hbm, hidden_hbm, grad_hbm, master_hbm, moment_hbm, variance_hbm,
    out_ref, hidden_ref, turned_ref, state_ref, blocks_ref, grad_ref, sems,
):
    copies = [pltpu.make_async_copy(blocks_hbm, blocks_ref, sems.at[0])]
    for source, target, parts in ((grad_hbm, grad_ref, GRAD_PARTS), (hidden_hbm, hidden_ref, HIDDEN_PARTS)):
        step = source.shape[0] // parts
        for k in range(parts):
            rows = pl.ds(k * step, step)
            copies.append(
                pltpu.make_async_copy(source.at[rows], target.at[rows], sems.at[len(copies)])
            )
    for k, source in enumerate((master_hbm, moment_hbm, variance_hbm)):
        copies.append(pltpu.make_async_copy(source, state_ref.at[k], sems.at[len(copies)]))
    for copy in copies:
        copy.start()
    grad_end = 1 + GRAD_PARTS
    hidden_end = grad_end + HIDDEN_PARTS
    for copy in copies[:grad_end]:
        copy.wait()
    for k in range(grad_ref.shape[1] // LANES):
        turned_ref[pl.ds(k * LANES, LANES), :] = grad_ref[:, pl.ds(k * LANES, LANES)].T
    for copy in copies[grad_end:hidden_end]:
        copy.wait()
    block_products(1 - place_ref[0], blocks_ref, hidden_ref, turned_ref, out_ref)
    for copy in copies[hidden_end:]:
        copy.wait()


def own_terms_kernel(
    place_ref, blocks_ref, live_ref, hidden_ref, turned_ref, out_ref, live_rows_ref
):
    block_products(place_ref[0], blocks_ref, hidden_ref, turned_ref, out_ref)
    total = live_ref[0]
    for owner in range(1, live_ref.shape[0]):
        total = total + live_ref[owner]
    live_rows_ref[pl.ds(0, 8), :] = jnp.full((8, LANES), live_ref[place_ref[1]], jnp.int32)
    live_rows_ref[pl.ds(8, 8), :] = jnp.full((8, LANES), total, jnp.int32)


def code_kernel(per_octave, own_ref, other_ref, out_ref):
    def encode(value):
        octave = jnp.log(jnp.maximum(jnp.abs(value), 2.0**LOW_OCTAVE)) * INV_LN2
        code = (octave - LOW_OCTAVE) * per_octave
        return jnp.round(jnp.where(value < 0, -code, code)).astype(jnp.int32)

    def one_chip(chip, carry):
        code = []
        for pair in range(PAIRS):
            rows = pl.ds(pair * SIDE, SIDE)
            code.append(encode(own_ref[chip, rows, :] + other_ref[chip, rows, :]))
        out_ref[chip] = (code[0] << 16) | (code[1] & 0xFFFF)
        return carry

    lax.fori_loop(0, out_ref.shape[0], one_chip, 0, unroll=2)


def sum_kernel(per_octave, live_ref, recv_ref, grad_ref, square_ref, turned_ref):
    def decode(code):
        value = code.astype(jnp.float32)
        size = jnp.exp2(jnp.abs(value) * (1.0 / per_octave) + LOW_OCTAVE)
        return jnp.where(code > 0, size, jnp.where(code < 0, -size, 0.0))

    def add(d, totals):
        word = recv_ref[d]
        return totals[0] + decode(word >> 16), totals[1] + decode((word << 16) >> 16)

    live = live_ref[0:1, :]
    zero = jnp.zeros((SIDE, LANES), jnp.float32)
    totals = lax.fori_loop(0, recv_ref.shape[0], add, (zero, zero), unroll=4)
    slot = lax.broadcasted_iota(jnp.int32, (SIDE, LANES), 1) // SIDE
    square = jnp.zeros((SIDE, LANES), jnp.float32)
    for pair in range(PAIRS):
        total = jnp.where(slot + pair * 2 < live, totals[pair], 0.0)
        square = square + total * total
        turned_ref[pair] = jnp.concatenate([total.T, total.T], axis=1)
    low_lane = lax.broadcasted_iota(jnp.int32, (TILES, LANES), 1) < SIDE
    for s in range(SLOTS):
        base = (s % 2) * SIDE
        even = turned_ref[s // 2, pl.ds(base, TILES, stride=2), :]
        odd = turned_ref[s // 2, pl.ds(base + 1, TILES, stride=2), :]
        grad_ref[pl.ds(s, TILES, stride=SLOTS), :] = jnp.where(low_lane, even, odd)
    square = jnp.sum(square, axis=0, keepdims=True)
    square_ref[...] = jnp.broadcast_to(square[None], square_ref.shape)


def update_kernel(
    place_ref, live_ref, square_ref, grad_ref, other_grad_ref, state_ref, other_state_ref,
    spread_ref, new_master_ref, new_moment_ref, new_variance_ref, clipped_ref, rows_ref,
):
    square = square_ref[0]
    for owner in range(1, square_ref.shape[0]):
        square = square + square_ref[owner]
    square = jnp.sum(square, axis=1, keepdims=True)
    entries = live_ref[8:9, :].astype(jnp.float32) * BLOCK
    clip = jnp.minimum(1.0, 1.0 / jnp.sqrt(square / entries + 1e-06))

    def step(grad, master, moment, variance):
        clipped = clip * grad
        moment = 0.9 * moment + 0.1 * clipped
        variance = 0.95 * variance + 0.05 * clipped * clipped
        moment_hat = moment / (1.0 - 0.9**20)
        variance_hat = variance / (1.0 - 0.95**20)
        change = moment_hat / (jnp.sqrt(variance_hat) + 1e-08) + 0.1 * master
        return master - 0.02 * change, moment, variance, clipped

    for t in range(TILES):
        lanes = pl.ds(t * LANES, LANES)
        rows = pl.ds(t * SLOTS, SLOTS)
        master, moment, variance, clipped = step(
            grad_ref[rows, :], state_ref[0, :, lanes], state_ref[1, :, lanes], state_ref[2, :, lanes]
        )
        clipped_ref[:, lanes] = clipped
        new_moment_ref[:, lanes] = moment
        new_variance_ref[:, lanes] = variance
        new_master_ref[:, lanes] = master
        rows_ref[:, lanes] = step(
            other_grad_ref[rows, :], other_state_ref[0, :, lanes],
            other_state_ref[1, :, lanes], other_state_ref[2, :, lanes],
        )[0]
    own = new_master_ref[...].astype(jnp.bfloat16)
    other = rows_ref[...].astype(jnp.bfloat16)
    for chip in range(spread_ref.shape[0]):
        spread_ref[chip, place_ref[2]] = own
        spread_ref[chip, 1 - place_ref[2]] = other


def store_kernel(after_ref, *refs):
    half = len(refs) // 2
    for source, target in zip(refs[:half], refs[half:]):
        target[...] = source[...]


def publish_kernel(place_ref, mine_ref, other_ref, out_ref):
    rows = CORES * SLOTS
    chips = mine_ref.shape[0]

    def weave(first_ref, second_ref):
        for half in range(HALVES):
            for chip in range(0, chips, 2):
                parts = []
                for k in range(2):
                    parts.append(first_ref[chip + k, half].astype(jnp.float32))
                    parts.append(second_ref[chip + k, half].astype(jnp.float32))
                block = jnp.concatenate(parts, axis=0).astype(jnp.bfloat16)
                out_ref[pl.ds((half * chips + chip) * rows, 2 * rows), :] = block

    @pl.when(place_ref[0] == 0)
    def _():
        weave(mine_ref, other_ref)

    @pl.when(place_ref[0] == 1)
    def _():
        weave(other_ref, mine_ref)


VMEM = pl.BlockSpec(memory_space=pltpu.VMEM)
SMEM = pl.BlockSpec(memory_space=pltpu.SMEM)
ANY = pl.BlockSpec(memory_space=pl.ANY)
PARAMS = pltpu.CompilerParams(vmem_limit_bytes=40 * 1024 * 1024)


def local(hidden, grad_out, block_list, live_block_count, master, moment, variance):
    chips = lax.axis_size(CHIPS)
    tokens = hidden.shape[0]
    place = jnp.stack([lax.axis_index("core"), lax.axis_index(AXES), lax.axis_index("half")])
    swap = [(0, 1), (1, 0)]
    shape = jax.ShapeDtypeStruct(master.shape, jnp.float32)
    kept = pltpu.VMEM(master.shape, jnp.float32)
    blocks = block_list.T
    top_octave = math.log2(CORES * tokens * LARGEST * LARGEST) + 0.05
    per_octave = 32767 / (top_octave - LOW_OCTAVE)
    cost = pl.CostEstimate(
        flops=2 * chips * SLOTS * SIDE * LANES * tokens,
        bytes_accessed=2 * (hidden.size + grad_out.size),
        transcendentals=0,
    )
    terms = pltpu.VMEM((chips, PAIRS * SIDE, LANES), jnp.float32)
    partner_terms, hidden, turned, state = pl.pallas_call(
        partner_terms_kernel,
        out_shape=(
            terms,
            pltpu.VMEM(hidden.shape, hidden.dtype),
            pltpu.VMEM(grad_out.shape[::-1], grad_out.dtype),
            pltpu.VMEM((3,) + master.shape, jnp.float32),
        ),
        in_specs=[SMEM] + [ANY] * 6,
        out_specs=(VMEM,) * 4,
        scratch_shapes=[
            pltpu.SMEM(blocks.shape, jnp.int32),
            pltpu.VMEM(grad_out.shape, grad_out.dtype),
            pltpu.SemaphoreType.DMA((4 + GRAD_PARTS + HIDDEN_PARTS,)),
        ],
        compiler_params=PARAMS,
        cost_estimate=cost,
        name="partner_terms",
    )(
        place,
        *(
            pltpu.with_memory_space_constraint(x, pltpu.HBM)
            for x in (blocks, hidden, grad_out, master, moment, variance)
        ),
    )
    arrived = lax.ppermute(partner_terms, "core", swap)
    other_state = lax.ppermute(state, "half", swap)
    own_terms, live_rows = pl.pallas_call(
        own_terms_kernel,
        out_shape=(terms, pltpu.VMEM((16, LANES), jnp.int32)),
        in_specs=[SMEM, SMEM, SMEM, VMEM, VMEM],
        out_specs=(VMEM, VMEM),
        compiler_params=PARAMS,
        cost_estimate=cost,
        name="own_terms",
    )(place, blocks, live_block_count, hidden, turned)
    codes = pl.pallas_call(
        functools.partial(code_kernel, per_octave),
        out_shape=pltpu.VMEM((chips, SIDE, LANES), jnp.int32),
        in_specs=[VMEM, VMEM],
        out_specs=VMEM,
        compiler_params=PARAMS,
        name="code_terms",
    )(own_terms, arrived)
    received = lax.all_to_all(codes, CHIPS, split_axis=0, concat_axis=0, tiled=True)
    gradient, square = pl.pallas_call(
        functools.partial(sum_kernel, per_octave),
        out_shape=(
            pltpu.VMEM((TILES * SLOTS, LANES), jnp.float32),
            pltpu.VMEM((chips * CORES, 1, LANES), jnp.float32),
        ),
        in_specs=[VMEM, VMEM],
        out_specs=(VMEM, VMEM),
        scratch_shapes=[pltpu.VMEM((PAIRS, LANES, LANES), jnp.float32)],
        compiler_params=PARAMS,
        name="sum_sources",
    )(live_rows, received)
    other_gradient = lax.ppermute(gradient, "half", swap)
    square = lax.all_to_all(square, AXES[::-1], split_axis=0, concat_axis=0, tiled=True)
    spread, *updated = pl.pallas_call(
        update_kernel,
        out_shape=(
            pltpu.VMEM((chips // HALVES, HALVES) + master.shape, jnp.bfloat16),
            kept,
            kept,
            kept,
            kept,
        ),
        in_specs=[SMEM] + [VMEM] * 6,
        out_specs=(VMEM,) * 5,
        scratch_shapes=[pltpu.VMEM(master.shape, jnp.float32)],
        compiler_params=PARAMS,
        name="adamw",
    )(place, live_rows, square, gradient, other_gradient, state, other_state)
    mine = lax.all_to_all(spread, "chip", split_axis=0, concat_axis=0, tiled=True)
    other = lax.ppermute(mine, "core", swap)
    results = pl.pallas_call(
        store_kernel,
        out_shape=(shape,) * 4,
        in_specs=[ANY] + [VMEM] * 4,
        out_specs=(VMEM,) * 4,
        compiler_params=PARAMS,
        name="store_state",
    )(mine, *updated)
    published = pl.pallas_call(
        publish_kernel,
        out_shape=jax.ShapeDtypeStruct((chips * CORES * SLOTS, BLOCK), jnp.bfloat16),
        in_specs=[SMEM, VMEM, VMEM],
        out_specs=VMEM,
        compiler_params=PARAMS,
        name="publish",
    )(place, mine, other)
    return (*results, published)


def solution(mesh):
    devices = mesh.devices.reshape(HALVES, -1, CORES)
    rows = P(AXES, None)
    return jax.shard_map(
        local,
        mesh=Mesh(devices, AXES),
        in_specs=(rows, rows, P(), P(), rows, rows, rows),
        out_specs=(rows, rows, rows, rows, P()),
        check_vma=False,
    )
```

```python
import functools
import math

import jax
import jax.numpy as jnp
from jax import lax
from jax.experimental import pallas as pl
from jax.experimental.pallas import tpu as pltpu
from jax.sharding import Mesh
from jax.sharding import PartitionSpec as P

SIDE = 64
LANES = 128
SLOTS = 4
PAIRS = SLOTS // 2
BLOCK = SIDE * SIDE
TILES = BLOCK // LANES
LOW_OCTAVE = -36
LARGEST = 6.0
GRAD_PARTS = 4
HIDDEN_PARTS = 8
CORES = 2
HALVES = 2
AXES = ("half", "chip", "core")
CHIPS = ("chip", "half")
INV_LN2 = 1.4426950408889634


def block_products(core, blocks_ref, hidden_ref, turned_ref, out_ref):
    low_lane = lax.broadcasted_iota(jnp.int32, (SIDE, LANES), 1) < SIDE

    chips = out_ref.shape[0] // HALVES

    def one_chip(peer, carry):
        owner = ((peer % HALVES) * chips + peer // HALVES) * CORES + core
        for pair in range(PAIRS):
            lefts, rights, rows = [], [], []
            for k in range(2):
                slot = owner * SLOTS + pair * 2 + k
                r = blocks_ref[0, slot]
                c = blocks_ref[1, slot]
                lefts.append(turned_ref[pl.ds(pl.multiple_of(c * SIDE, SIDE), SIDE), :])
                lanes = pl.ds(pl.multiple_of((r // 2) * LANES, LANES), LANES)
                rights.append(hidden_ref[:, lanes])
                rows.append(r)
            product = jnp.dot(
                jnp.concatenate(lefts, axis=0),
                jnp.concatenate(rights, axis=1),
                preferred_element_type=jnp.float32,
            )
            first = pltpu.roll(product[:SIDE, :LANES], (rows[0] % 2) * SIDE, 1)
            second = pltpu.roll(product[SIDE:, LANES:], ((rows[1] + 1) % 2) * SIDE, 1)
            out_ref[peer, pl.ds(pair * SIDE, SIDE), :] = jnp.where(low_lane, first, second)
        return carry

    lax.fori_loop(0, out_ref.shape[0], one_chip, 0, unroll=8)


def partner_terms_kernel(
    place_ref, blocks_hbm, hidden_hbm, grad_hbm, master_hbm, moment_hbm, variance_hbm,
    out_ref, hidden_ref, turned_ref, state_ref, blocks_ref, grad_ref, sems,
):
    copies = [pltpu.make_async_copy(blocks_hbm, blocks_ref, sems.at[0])]
    for source, target, parts in ((grad_hbm, grad_ref, GRAD_PARTS), (hidden_hbm, hidden_ref, HIDDEN_PARTS)):
        step = source.shape[0] // parts
        for k in range(parts):
            rows = pl.ds(k * step, step)
            copies.append(
                pltpu.make_async_copy(source.at[rows], target.at[rows], sems.at[len(copies)])
            )
    for k, source in enumerate((master_hbm, moment_hbm, variance_hbm)):
        copies.append(pltpu.make_async_copy(source, state_ref.at[k], sems.at[len(copies)]))
    for copy in copies:
        copy.start()
    grad_end = 1 + GRAD_PARTS
    hidden_end = grad_end + HIDDEN_PARTS
    for copy in copies[:grad_end]:
        copy.wait()
    for k in range(grad_ref.shape[1] // LANES):
        turned_ref[pl.ds(k * LANES, LANES), :] = grad_ref[:, pl.ds(k * LANES, LANES)].T
    for copy in copies[grad_end:hidden_end]:
        copy.wait()
    block_products(1 - place_ref[0], blocks_ref, hidden_ref, turned_ref, out_ref)
    for copy in copies[hidden_end:]:
        copy.wait()


def own_terms_kernel(
    place_ref, blocks_ref, live_ref, hidden_ref, turned_ref, out_ref, live_rows_ref
):
    block_products(place_ref[0], blocks_ref, hidden_ref, turned_ref, out_ref)
    total = live_ref[0]
    for owner in range(1, live_ref.shape[0]):
        total = total + live_ref[owner]
    live_rows_ref[pl.ds(0, 8), :] = jnp.full((8, LANES), live_ref[place_ref[1]], jnp.int32)
    live_rows_ref[pl.ds(8, 8), :] = jnp.full((8, LANES), total, jnp.int32)


def code_kernel(per_octave, own_ref, other_ref, out_ref):
    def encode(value):
        octave = jnp.log(jnp.maximum(jnp.abs(value), 2.0**LOW_OCTAVE)) * INV_LN2
        code = (octave - LOW_OCTAVE) * per_octave
        return jnp.round(jnp.where(value < 0, -code, code)).astype(jnp.int32)

    def one_chip(chip, carry):
        code = []
        for pair in range(PAIRS):
            rows = pl.ds(pair * SIDE, SIDE)
            code.append(encode(own_ref[chip, rows, :] + other_ref[chip, rows, :]))
        out_ref[chip] = (code[0] << 16) | (code[1] & 0xFFFF)
        return carry

    lax.fori_loop(0, out_ref.shape[0], one_chip, 0, unroll=2)


def half_sum_kernel(per_octave, place_ref, after_ref, recv_ref, own_ref, other_ref):
    def decode(code):
        value = code.astype(jnp.float32)
        size = jnp.exp2(jnp.abs(value) * (1.0 / per_octave) + LOW_OCTAVE)
        return jnp.where(code > 0, size, jnp.where(code < 0, -size, 0.0))

    def add(offset, d, totals):
        word = recv_ref[d * HALVES + offset]
        return totals[0] + decode(word >> 16), totals[1] + decode((word << 16) >> 16)

    zero = jnp.zeros((SIDE, LANES), jnp.float32)
    chips = recv_ref.shape[0] // HALVES
    for offset, out_ref in ((place_ref[2], own_ref), (1 - place_ref[2], other_ref)):
        totals = lax.fori_loop(
            0, chips, functools.partial(add, offset), (zero, zero), unroll=4
        )
        for pair in range(PAIRS):
            out_ref[pair] = totals[pair]


def sum_kernel(live_ref, own_ref, arrived_ref, grad_ref, square_ref, turned_ref):
    live = live_ref[0:1, :]
    slot = lax.broadcasted_iota(jnp.int32, (SIDE, LANES), 1) // SIDE
    square = jnp.zeros((SIDE, LANES), jnp.float32)
    for pair in range(PAIRS):
        total = jnp.where(slot + pair * 2 < live, own_ref[pair] + arrived_ref[pair], 0.0)
        square = square + total * total
        turned_ref[pair] = jnp.concatenate([total.T, total.T], axis=1)
    low_lane = lax.broadcasted_iota(jnp.int32, (TILES, LANES), 1) < SIDE
    for s in range(SLOTS):
        base = (s % 2) * SIDE
        even = turned_ref[s // 2, pl.ds(base, TILES, stride=2), :]
        odd = turned_ref[s // 2, pl.ds(base + 1, TILES, stride=2), :]
        grad_ref[pl.ds(s, TILES, stride=SLOTS), :] = jnp.where(low_lane, even, odd)
    square = jnp.sum(square, axis=0, keepdims=True)
    square_ref[...] = jnp.broadcast_to(square[None], square_ref.shape)


def update_kernel(
    place_ref, live_ref, square_ref, grad_ref, other_grad_ref, state_ref, other_state_ref,
    spread_ref, new_master_ref, new_moment_ref, new_variance_ref, clipped_ref, rows_ref,
):
    square = square_ref[0]
    for owner in range(1, square_ref.shape[0]):
        square = square + square_ref[owner]
    square = jnp.sum(square, axis=1, keepdims=True)
    entries = live_ref[8:9, :].astype(jnp.float32) * BLOCK
    clip = jnp.minimum(1.0, 1.0 / jnp.sqrt(square / entries + 1e-06))

    def step(grad, master, moment, variance):
        clipped = clip * grad
        moment = 0.9 * moment + 0.1 * clipped
        variance = 0.95 * variance + 0.05 * clipped * clipped
        moment_hat = moment / (1.0 - 0.9**20)
        variance_hat = variance / (1.0 - 0.95**20)
        change = moment_hat / (jnp.sqrt(variance_hat) + 1e-08) + 0.1 * master
        return master - 0.02 * change, moment, variance, clipped

    for t in range(TILES):
        lanes = pl.ds(t * LANES, LANES)
        rows = pl.ds(t * SLOTS, SLOTS)
        master, moment, variance, clipped = step(
            grad_ref[rows, :], state_ref[0, :, lanes], state_ref[1, :, lanes], state_ref[2, :, lanes]
        )
        clipped_ref[:, lanes] = clipped
        new_moment_ref[:, lanes] = moment
        new_variance_ref[:, lanes] = variance
        new_master_ref[:, lanes] = master
        rows_ref[:, lanes] = step(
            other_grad_ref[rows, :], other_state_ref[0, :, lanes],
            other_state_ref[1, :, lanes], other_state_ref[2, :, lanes],
        )[0]
    own = new_master_ref[...].astype(jnp.bfloat16)
    other = rows_ref[...].astype(jnp.bfloat16)
    for chip in range(spread_ref.shape[0]):
        spread_ref[chip, place_ref[2]] = own
        spread_ref[chip, 1 - place_ref[2]] = other


def store_kernel(after_ref, *refs):
    half = len(refs) // 2
    for source, target in zip(refs[:half], refs[half:]):
        target[...] = source[...]


def publish_kernel(place_ref, mine_ref, other_ref, out_ref):
    rows = CORES * SLOTS
    chips = mine_ref.shape[0]

    def weave(first_ref, second_ref):
        for half in range(HALVES):
            for chip in range(0, chips, 2):
                parts = []
                for k in range(2):
                    parts.append(first_ref[chip + k, half].astype(jnp.float32))
                    parts.append(second_ref[chip + k, half].astype(jnp.float32))
                block = jnp.concatenate(parts, axis=0).astype(jnp.bfloat16)
                out_ref[pl.ds((half * chips + chip) * rows, 2 * rows), :] = block

    @pl.when(place_ref[0] == 0)
    def _():
        weave(mine_ref, other_ref)

    @pl.when(place_ref[0] == 1)
    def _():
        weave(other_ref, mine_ref)


VMEM = pl.BlockSpec(memory_space=pltpu.VMEM)
SMEM = pl.BlockSpec(memory_space=pltpu.SMEM)
ANY = pl.BlockSpec(memory_space=pl.ANY)
PARAMS = pltpu.CompilerParams(vmem_limit_bytes=40 * 1024 * 1024)


def local(hidden, grad_out, block_list, live_block_count, master, moment, variance):
    chips = lax.axis_size(CHIPS)
    tokens = hidden.shape[0]
    place = jnp.stack([lax.axis_index("core"), lax.axis_index(AXES), lax.axis_index("half")])
    swap = [(0, 1), (1, 0)]
    shape = jax.ShapeDtypeStruct(master.shape, jnp.float32)
    kept = pltpu.VMEM(master.shape, jnp.float32)
    blocks = block_list.T
    top_octave = math.log2(CORES * tokens * LARGEST * LARGEST) + 0.05
    per_octave = 32767 / (top_octave - LOW_OCTAVE)
    cost = pl.CostEstimate(
        flops=2 * chips * SLOTS * SIDE * LANES * tokens,
        bytes_accessed=2 * (hidden.size + grad_out.size),
        transcendentals=0,
    )
    terms = pltpu.VMEM((chips, PAIRS * SIDE, LANES), jnp.float32)
    partner_terms, hidden, turned, state = pl.pallas_call(
        partner_terms_kernel,
        out_shape=(
            terms,
            pltpu.VMEM(hidden.shape, hidden.dtype),
            pltpu.VMEM(grad_out.shape[::-1], grad_out.dtype),
            pltpu.VMEM((3,) + master.shape, jnp.float32),
        ),
        in_specs=[SMEM] + [ANY] * 6,
        out_specs=(VMEM,) * 4,
        scratch_shapes=[
            pltpu.SMEM(blocks.shape, jnp.int32),
            pltpu.VMEM(grad_out.shape, grad_out.dtype),
            pltpu.SemaphoreType.DMA((4 + GRAD_PARTS + HIDDEN_PARTS,)),
        ],
        compiler_params=PARAMS,
        cost_estimate=cost,
        name="partner_terms",
    )(
        place,
        *(
            pltpu.with_memory_space_constraint(x, pltpu.HBM)
            for x in (blocks, hidden, grad_out, master, moment, variance)
        ),
    )
    arrived = lax.ppermute(partner_terms, "core", swap)
    other_state = lax.ppermute(state, "half", swap)
    own_terms, live_rows = pl.pallas_call(
        own_terms_kernel,
        out_shape=(terms, pltpu.VMEM((16, LANES), jnp.int32)),
        in_specs=[SMEM, SMEM, SMEM, VMEM, VMEM],
        out_specs=(VMEM, VMEM),
        compiler_params=PARAMS,
        cost_estimate=cost,
        name="own_terms",
    )(place, blocks, live_block_count, hidden, turned)
    codes = pl.pallas_call(
        functools.partial(code_kernel, per_octave),
        out_shape=pltpu.VMEM((chips, SIDE, LANES), jnp.int32),
        in_specs=[VMEM, VMEM],
        out_specs=VMEM,
        compiler_params=PARAMS,
        name="code_terms",
    )(own_terms, arrived)
    received = lax.all_to_all(codes, "chip", split_axis=0, concat_axis=0, tiled=True)
    sums = pltpu.VMEM((PAIRS, SIDE, LANES), jnp.float32)
    own_sum, other_sum = pl.pallas_call(
        functools.partial(half_sum_kernel, per_octave),
        out_shape=(sums, sums),
        in_specs=[SMEM, ANY, VMEM],
        out_specs=(VMEM, VMEM),
        compiler_params=PARAMS,
        name="sum_half",
    )(place, other_state, received)
    arrived_sum = lax.ppermute(other_sum, "half", swap)
    gradient, square = pl.pallas_call(
        sum_kernel,
        out_shape=(
            pltpu.VMEM((TILES * SLOTS, LANES), jnp.float32),
            pltpu.VMEM((chips * CORES, 1, LANES), jnp.float32),
        ),
        in_specs=[VMEM, VMEM, VMEM],
        out_specs=(VMEM, VMEM),
        scratch_shapes=[pltpu.VMEM((PAIRS, LANES, LANES), jnp.float32)],
        compiler_params=PARAMS,
        name="sum_pair",
    )(live_rows, own_sum, arrived_sum)
    other_gradient = lax.ppermute(gradient, "half", swap)
    square = lax.all_to_all(square, AXES[::-1], split_axis=0, concat_axis=0, tiled=True)
    spread, *updated = pl.pallas_call(
        update_kernel,
        out_shape=(
            pltpu.VMEM((chips // HALVES, HALVES) + master.shape, jnp.bfloat16),
            kept,
            kept,
            kept,
            kept,
        ),
        in_specs=[SMEM] + [VMEM] * 6,
        out_specs=(VMEM,) * 5,
        scratch_shapes=[pltpu.VMEM(master.shape, jnp.float32)],
        compiler_params=PARAMS,
        name="adamw",
    )(place, live_rows, square, gradient, other_gradient, state, other_state)
    mine = lax.all_to_all(spread, "chip", split_axis=0, concat_axis=0, tiled=True)
    other = lax.ppermute(mine, "core", swap)
    results = pl.pallas_call(
        store_kernel,
        out_shape=(shape,) * 4,
        in_specs=[ANY] + [VMEM] * 4,
        out_specs=(VMEM,) * 4,
        compiler_params=PARAMS,
        name="store_state",
    )(mine, *updated)
    published = pl.pallas_call(
        publish_kernel,
        out_shape=jax.ShapeDtypeStruct((chips * CORES * SLOTS, BLOCK), jnp.bfloat16),
        in_specs=[SMEM, VMEM, VMEM],
        out_specs=VMEM,
        compiler_params=PARAMS,
        name="publish",
    )(place, mine, other)
    return (*results, published)


def solution(mesh):
    devices = mesh.devices.reshape(HALVES, -1, CORES)
    rows = P(AXES, None)
    return jax.shard_map(
        local,
        mesh=Mesh(devices, AXES),
        in_specs=(rows, rows, P(), P(), rows, rows, rows),
        out_specs=(rows, rows, rows, rows, P()),
        check_vma=False,
    )
```

```python
import functools
import math

import jax
import jax.numpy as jnp
from jax import lax
from jax.experimental import pallas as pl
from jax.experimental.pallas import tpu as pltpu
from jax.sharding import Mesh
from jax.sharding import PartitionSpec as P

SIDE = 64
LANES = 128
SLOTS = 4
PAIRS = SLOTS // 2
BLOCK = SIDE * SIDE
TILES = BLOCK // LANES
LOW_OCTAVE = -36
LARGEST = 6.0
GRAD_PARTS = 4
HIDDEN_PARTS = 8
CORES = 2
HALVES = 2
AXES = ("half", "chip", "core")
CHIPS = ("chip", "half")
INV_LN2 = 1.4426950408889634


def block_products(core, blocks_ref, hidden_ref, turned_ref, out_ref):
    low_lane = lax.broadcasted_iota(jnp.int32, (SIDE, LANES), 1) < SIDE

    chips = out_ref.shape[0] // HALVES

    def one_chip(peer, carry):
        owner = ((peer % HALVES) * chips + peer // HALVES) * CORES + core
        for pair in range(PAIRS):
            lefts, rights, rows = [], [], []
            for k in range(2):
                slot = owner * SLOTS + pair * 2 + k
                r = blocks_ref[0, slot]
                c = blocks_ref[1, slot]
                lefts.append(turned_ref[pl.ds(pl.multiple_of(c * SIDE, SIDE), SIDE), :])
                lanes = pl.ds(pl.multiple_of((r // 2) * LANES, LANES), LANES)
                rights.append(hidden_ref[:, lanes])
                rows.append(r)
            product = jnp.dot(
                jnp.concatenate(lefts, axis=0),
                jnp.concatenate(rights, axis=1),
                preferred_element_type=jnp.float32,
            )
            first = pltpu.roll(product[:SIDE, :LANES], (rows[0] % 2) * SIDE, 1)
            second = pltpu.roll(product[SIDE:, LANES:], ((rows[1] + 1) % 2) * SIDE, 1)
            out_ref[peer, pl.ds(pair * SIDE, SIDE), :] = jnp.where(low_lane, first, second)
        return carry

    lax.fori_loop(0, out_ref.shape[0], one_chip, 0, unroll=8)


def partner_terms_kernel(
    blocks_hbm, hidden_hbm, grad_hbm, master_hbm, moment_hbm, variance_hbm,
    out_ref, hidden_ref, turned_ref, state_ref, blocks_ref, grad_ref, sems,
):
    copies = [pltpu.make_async_copy(blocks_hbm, blocks_ref, sems.at[0])]
    for source, target, parts in ((grad_hbm, grad_ref, GRAD_PARTS), (hidden_hbm, hidden_ref, HIDDEN_PARTS)):
        step = source.shape[0] // parts
        for k in range(parts):
            rows = pl.ds(k * step, step)
            copies.append(
                pltpu.make_async_copy(source.at[rows], target.at[rows], sems.at[len(copies)])
            )
    for k, source in enumerate((master_hbm, moment_hbm, variance_hbm)):
        copies.append(pltpu.make_async_copy(source, state_ref.at[k], sems.at[len(copies)]))
    for copy in copies:
        copy.start()
    grad_end = 1 + GRAD_PARTS
    hidden_end = grad_end + HIDDEN_PARTS
    for copy in copies[:grad_end]:
        copy.wait()
    for k in range(grad_ref.shape[1] // LANES):
        turned_ref[pl.ds(k * LANES, LANES), :] = grad_ref[:, pl.ds(k * LANES, LANES)].T
    for copy in copies[grad_end:hidden_end]:
        copy.wait()
    block_products(1 - lax.axis_index("core"), blocks_ref, hidden_ref, turned_ref, out_ref)
    for copy in copies[hidden_end:]:
        copy.wait()


def own_terms_kernel(
    blocks_ref, live_ref, hidden_ref, turned_ref, out_ref, live_rows_ref
):
    block_products(lax.axis_index("core"), blocks_ref, hidden_ref, turned_ref, out_ref)
    total = live_ref[0]
    for owner in range(1, live_ref.shape[0]):
        total = total + live_ref[owner]
    live_rows_ref[pl.ds(0, 8), :] = jnp.full((8, LANES), live_ref[lax.axis_index(AXES)], jnp.int32)
    live_rows_ref[pl.ds(8, 8), :] = jnp.full((8, LANES), total, jnp.int32)


def code_kernel(per_octave, own_ref, other_ref, out_ref):
    def encode(value):
        octave = jnp.log(jnp.maximum(jnp.abs(value), 2.0**LOW_OCTAVE)) * INV_LN2
        code = (octave - LOW_OCTAVE) * per_octave
        return jnp.round(jnp.where(value < 0, -code, code)).astype(jnp.int32)

    def one_chip(chip, carry):
        code = []
        for pair in range(PAIRS):
            rows = pl.ds(pair * SIDE, SIDE)
            code.append(encode(own_ref[chip, rows, :] + other_ref[chip, rows, :]))
        out_ref[chip] = (code[0] << 16) | (code[1] & 0xFFFF)
        return carry

    lax.fori_loop(0, out_ref.shape[0], one_chip, 0, unroll=2)


def half_sum_kernel(per_octave, recv_ref, own_ref, other_ref):
    def decode(code):
        value = code.astype(jnp.float32)
        size = jnp.exp2(jnp.abs(value) * (1.0 / per_octave) + LOW_OCTAVE)
        return jnp.where(code > 0, size, jnp.where(code < 0, -size, 0.0))

    def add(offset, d, totals):
        word = recv_ref[d * HALVES + offset]
        return totals[0] + decode(word >> 16), totals[1] + decode((word << 16) >> 16)

    zero = jnp.zeros((SIDE, LANES), jnp.float32)
    chips = recv_ref.shape[0] // HALVES
    half = lax.axis_index("half")
    for offset, out_ref in ((half, own_ref), (1 - half, other_ref)):
        totals = lax.fori_loop(
            0, chips, functools.partial(add, offset), (zero, zero), unroll=4
        )
        for pair in range(PAIRS):
            out_ref[pair] = totals[pair]


def sum_kernel(live_ref, own_ref, arrived_ref, grad_ref, square_ref, turned_ref):
    live = live_ref[0:1, :]
    slot = lax.broadcasted_iota(jnp.int32, (SIDE, LANES), 1) // SIDE
    square = jnp.zeros((SIDE, LANES), jnp.float32)
    for pair in range(PAIRS):
        total = jnp.where(slot + pair * 2 < live, own_ref[pair] + arrived_ref[pair], 0.0)
        square = square + total * total
        turned_ref[pair] = jnp.concatenate([total.T, total.T], axis=1)
    low_lane = lax.broadcasted_iota(jnp.int32, (TILES, LANES), 1) < SIDE
    for s in range(SLOTS):
        base = (s % 2) * SIDE
        even = turned_ref[s // 2, pl.ds(base, TILES, stride=2), :]
        odd = turned_ref[s // 2, pl.ds(base + 1, TILES, stride=2), :]
        grad_ref[pl.ds(s, TILES, stride=SLOTS), :] = jnp.where(low_lane, even, odd)
    square = jnp.sum(square, axis=0, keepdims=True)
    square_ref[...] = jnp.broadcast_to(square[None], square_ref.shape)


def update_kernel(
    live_ref, square_ref, grad_ref, state_ref,
    own_ref, new_master_ref, new_moment_ref, new_variance_ref, clipped_ref,
):
    square = square_ref[0]
    for owner in range(1, square_ref.shape[0]):
        square = square + square_ref[owner]
    square = jnp.sum(square, axis=1, keepdims=True)
    entries = live_ref[8:9, :].astype(jnp.float32) * BLOCK
    clip = jnp.minimum(1.0, 1.0 / jnp.sqrt(square / entries + 1e-06))
    for t in range(TILES):
        lanes = pl.ds(t * LANES, LANES)
        clipped = clip * grad_ref[pl.ds(t * SLOTS, SLOTS), :]
        moment = 0.9 * state_ref[1, :, lanes] + 0.1 * clipped
        variance = 0.95 * state_ref[2, :, lanes] + 0.05 * clipped * clipped
        master = state_ref[0, :, lanes]
        moment_hat = moment / (1.0 - 0.9**20)
        variance_hat = variance / (1.0 - 0.95**20)
        step = moment_hat / (jnp.sqrt(variance_hat) + 1e-08) + 0.1 * master
        master = master - 0.02 * step
        clipped_ref[:, lanes] = clipped
        new_moment_ref[:, lanes] = moment
        new_variance_ref[:, lanes] = variance
        new_master_ref[:, lanes] = master
    own_ref[...] = new_master_ref[...].astype(jnp.bfloat16)


def spread_kernel(own_ref, other_ref, spread_ref):
    half = lax.axis_index("half")
    own, other = own_ref[...], other_ref[...]
    for chip in range(spread_ref.shape[0]):
        spread_ref[chip, half] = own
        spread_ref[chip, 1 - half] = other


def store_kernel(after_ref, *refs):
    half = len(refs) // 2
    for source, target in zip(refs[:half], refs[half:]):
        target[...] = source[...]


def publish_kernel(mine_ref, other_ref, out_ref):
    rows = CORES * SLOTS
    chips = mine_ref.shape[0]
    core = lax.axis_index("core")

    def weave(first_ref, second_ref):
        for half in range(HALVES):
            for chip in range(0, chips, 2):
                parts = []
                for k in range(2):
                    parts.append(first_ref[chip + k, half])
                    parts.append(second_ref[chip + k, half])
                block = jnp.concatenate(parts, axis=0)
                out_ref[pl.ds((half * chips + chip) * rows, 2 * rows), :] = block

    @pl.when(core == 0)
    def _():
        weave(mine_ref, other_ref)

    @pl.when(core == 1)
    def _():
        weave(other_ref, mine_ref)


VMEM = pl.BlockSpec(memory_space=pltpu.VMEM)
SMEM = pl.BlockSpec(memory_space=pltpu.SMEM)
ANY = pl.BlockSpec(memory_space=pl.ANY)
PARAMS = pltpu.CompilerParams(vmem_limit_bytes=40 * 1024 * 1024)


def local(hidden, grad_out, block_list, live_block_count, master, moment, variance):
    chips = lax.axis_size(CHIPS)
    tokens = hidden.shape[0]
    swap = [(0, 1), (1, 0)]
    shape = jax.ShapeDtypeStruct(master.shape, jnp.float32)
    kept = pltpu.VMEM(master.shape, jnp.float32)
    blocks = block_list.T
    top_octave = math.log2(CORES * tokens * LARGEST * LARGEST) + 0.05
    per_octave = 32767 / (top_octave - LOW_OCTAVE)
    cost = pl.CostEstimate(
        flops=2 * chips * SLOTS * SIDE * LANES * tokens,
        bytes_accessed=2 * (hidden.size + grad_out.size),
        transcendentals=0,
    )
    terms = pltpu.VMEM((chips, PAIRS * SIDE, LANES), jnp.float32)
    partner_terms, hidden, turned, state = pl.pallas_call(
        partner_terms_kernel,
        out_shape=(
            terms,
            pltpu.VMEM(hidden.shape, hidden.dtype),
            pltpu.VMEM(grad_out.shape[::-1], grad_out.dtype),
            pltpu.VMEM((3,) + master.shape, jnp.float32),
        ),
        in_specs=[ANY] * 6,
        out_specs=(VMEM,) * 4,
        scratch_shapes=[
            pltpu.SMEM(blocks.shape, jnp.int32),
            pltpu.VMEM(grad_out.shape, grad_out.dtype),
            pltpu.SemaphoreType.DMA((4 + GRAD_PARTS + HIDDEN_PARTS,)),
        ],
        compiler_params=PARAMS,
        cost_estimate=cost,
        name="partner_terms",
    )(
        *(
            pltpu.with_memory_space_constraint(x, pltpu.HBM)
            for x in (blocks, hidden, grad_out, master, moment, variance)
        )
    )
    arrived = lax.ppermute(partner_terms, "core", swap)
    own_terms, live_rows = pl.pallas_call(
        own_terms_kernel,
        out_shape=(terms, pltpu.VMEM((16, LANES), jnp.int32)),
        in_specs=[SMEM, SMEM, VMEM, VMEM],
        out_specs=(VMEM, VMEM),
        compiler_params=PARAMS,
        cost_estimate=cost,
        name="own_terms",
    )(blocks, live_block_count, hidden, turned)
    codes = pl.pallas_call(
        functools.partial(code_kernel, per_octave),
        out_shape=pltpu.VMEM((chips, SIDE, LANES), jnp.int32),
        in_specs=[VMEM, VMEM],
        out_specs=VMEM,
        compiler_params=PARAMS,
        name="code_terms",
    )(own_terms, arrived)
    received = lax.all_to_all(codes, "chip", split_axis=0, concat_axis=0, tiled=True)
    sums = pltpu.VMEM((PAIRS, SIDE, LANES), jnp.float32)
    own_sum, other_sum = pl.pallas_call(
        functools.partial(half_sum_kernel, per_octave),
        out_shape=(sums, sums),
        in_specs=[VMEM],
        out_specs=(VMEM, VMEM),
        compiler_params=PARAMS,
        name="sum_half",
    )(received)
    arrived_sum = lax.ppermute(other_sum, "half", swap)
    gradient, square = pl.pallas_call(
        sum_kernel,
        out_shape=(
            pltpu.VMEM((TILES * SLOTS, LANES), jnp.float32),
            pltpu.VMEM((chips * CORES, 1, LANES), jnp.float32),
        ),
        in_specs=[VMEM, VMEM, VMEM],
        out_specs=(VMEM, VMEM),
        scratch_shapes=[pltpu.VMEM((PAIRS, LANES, LANES), jnp.float32)],
        compiler_params=PARAMS,
        name="sum_pair",
    )(live_rows, own_sum, arrived_sum)
    square = lax.all_to_all(square, AXES[::-1], split_axis=0, concat_axis=0, tiled=True)
    rows = pltpu.VMEM(master.shape, jnp.bfloat16)
    own_rows, *updated = pl.pallas_call(
        update_kernel,
        out_shape=(rows, kept, kept, kept, kept),
        in_specs=[VMEM] * 4,
        out_specs=(VMEM,) * 5,
        compiler_params=PARAMS,
        name="adamw",
    )(live_rows, square, gradient, state)
    other_rows = lax.ppermute(own_rows, "half", swap)
    spread = pl.pallas_call(
        spread_kernel,
        out_shape=pltpu.VMEM((chips // HALVES, HALVES) + master.shape, jnp.bfloat16),
        in_specs=[VMEM, VMEM],
        out_specs=VMEM,
        compiler_params=PARAMS,
        name="spread_rows",
    )(own_rows, other_rows)
    mine = lax.all_to_all(spread, "chip", split_axis=0, concat_axis=0, tiled=True)
    other = lax.ppermute(mine, "core", swap)
    results = pl.pallas_call(
        store_kernel,
        out_shape=(shape,) * 4,
        in_specs=[ANY] + [VMEM] * 4,
        out_specs=(VMEM,) * 4,
        compiler_params=PARAMS,
        name="store_state",
    )(mine, *updated)
    published = pl.pallas_call(
        publish_kernel,
        out_shape=jax.ShapeDtypeStruct((chips * CORES * SLOTS, BLOCK), jnp.bfloat16),
        in_specs=[VMEM, VMEM],
        out_specs=VMEM,
        compiler_params=PARAMS,
        name="publish",
    )(mine, other)
    return (*results, published)


def solution(mesh):
    devices = mesh.devices.reshape(HALVES, -1, CORES)
    rows = P(AXES, None)
    return jax.shard_map(
        local,
        mesh=Mesh(devices, AXES),
        in_specs=(rows, rows, P(), P(), rows, rows, rows),
        out_specs=(rows, rows, rows, rows, P()),
        check_vma=False,
    )
```

```python
import functools
import math

import jax
import jax.numpy as jnp
from jax import lax
from jax.experimental import pallas as pl
from jax.experimental.pallas import tpu as pltpu
from jax.sharding import Mesh
from jax.sharding import PartitionSpec as P

SIDE = 64
LANES = 128
SLOTS = 4
PAIRS = SLOTS // 2
BLOCK = SIDE * SIDE
TILES = BLOCK // LANES
LOW_OCTAVE = -36
LARGEST = 6.0
SMALLEST = 1e-30
CODE_BITS = 13
EXP_ROWS = 8
GRAD_PARTS = 4
HIDDEN_PARTS = 8
CORES = 2
HALVES = 2
AXES = ("half", "chip", "core")
CHIPS = ("chip", "half")
INV_LN2 = 1.4426950408889634


def block_products(core, blocks_ref, hidden_ref, turned_ref, out_ref):
    low_lane = lax.broadcasted_iota(jnp.int32, (SIDE, LANES), 1) < SIDE

    chips = out_ref.shape[0] // HALVES

    def one_chip(peer, carry):
        owner = ((peer % HALVES) * chips + peer // HALVES) * CORES + core
        for pair in range(PAIRS):
            lefts, rights, rows = [], [], []
            for k in range(2):
                slot = owner * SLOTS + pair * 2 + k
                r = blocks_ref[0, slot]
                c = blocks_ref[1, slot]
                lefts.append(turned_ref[pl.ds(pl.multiple_of(c * SIDE, SIDE), SIDE), :])
                lanes = pl.ds(pl.multiple_of((r // 2) * LANES, LANES), LANES)
                rights.append(hidden_ref[:, lanes])
                rows.append(r)
            product = jnp.dot(
                jnp.concatenate(lefts, axis=0),
                jnp.concatenate(rights, axis=1),
                preferred_element_type=jnp.float32,
            )
            first = pltpu.roll(product[:SIDE, :LANES], (rows[0] % 2) * SIDE, 1)
            second = pltpu.roll(product[SIDE:, LANES:], ((rows[1] + 1) % 2) * SIDE, 1)
            out_ref[peer, pl.ds(pair * SIDE, SIDE), :] = jnp.where(low_lane, first, second)
        return carry

    lax.fori_loop(0, out_ref.shape[0], one_chip, 0, unroll=16)


def partner_terms_kernel(
    blocks_hbm, hidden_hbm, grad_hbm, master_hbm, moment_hbm, variance_hbm,
    out_ref, hidden_ref, turned_ref, state_ref, blocks_ref, grad_ref, sems,
):
    copies = [pltpu.make_async_copy(blocks_hbm, blocks_ref, sems.at[0])]
    for source, target, parts in ((grad_hbm, grad_ref, GRAD_PARTS), (hidden_hbm, hidden_ref, HIDDEN_PARTS)):
        step = source.shape[0] // parts
        for k in range(parts):
            rows = pl.ds(k * step, step)
            copies.append(
                pltpu.make_async_copy(source.at[rows], target.at[rows], sems.at[len(copies)])
            )
    for k, source in enumerate((master_hbm, moment_hbm, variance_hbm)):
        copies.append(pltpu.make_async_copy(source, state_ref.at[k], sems.at[len(copies)]))
    for copy in copies:
        copy.start()
    grad_end = 1 + GRAD_PARTS
    hidden_end = grad_end + HIDDEN_PARTS
    for copy in copies[:grad_end]:
        copy.wait()
    for k in range(grad_ref.shape[1] // LANES):
        turned_ref[pl.ds(k * LANES, LANES), :] = grad_ref[:, pl.ds(k * LANES, LANES)].T
    for copy in copies[grad_end:hidden_end]:
        copy.wait()
    block_products(1 - lax.axis_index("core"), blocks_ref, hidden_ref, turned_ref, out_ref)
    for copy in copies[hidden_end:]:
        copy.wait()


def own_terms_kernel(
    blocks_ref, live_ref, hidden_ref, turned_ref, out_ref, live_rows_ref
):
    block_products(lax.axis_index("core"), blocks_ref, hidden_ref, turned_ref, out_ref)
    total = live_ref[0]
    for owner in range(1, live_ref.shape[0]):
        total = total + live_ref[owner]
    owners = live_ref.shape[0]
    me = lax.axis_index(AXES)
    paired = lax.rem(me + owners // HALVES, owners)
    live_rows_ref[pl.ds(0, 8), :] = jnp.full((8, LANES), live_ref[me], jnp.int32)
    live_rows_ref[pl.ds(16, 8), :] = jnp.full((8, LANES), live_ref[paired], jnp.int32)
    live_rows_ref[pl.ds(8, 8), :] = jnp.full((8, LANES), total, jnp.int32)


def code_kernel(per_octave, own_ref, other_ref, out_ref):
    def encode(value):
        octave = jnp.log(jnp.maximum(jnp.abs(value), 2.0**LOW_OCTAVE)) * INV_LN2
        code = (octave - LOW_OCTAVE) * per_octave
        return jnp.round(jnp.where(value < 0, -code, code)).astype(jnp.int32)

    def one_chip(chip, carry):
        code = []
        for pair in range(PAIRS):
            rows = pl.ds(pair * SIDE, SIDE)
            code.append(encode(own_ref[chip, rows, :] + other_ref[chip, rows, :]))
        out_ref[chip] = (code[0] << 16) | (code[1] & 0xFFFF)
        return carry

    lax.fori_loop(0, out_ref.shape[0], one_chip, 0, unroll=2)


def half_sum_kernel(per_octave, recv_ref, own_ref, other_ref, code_ref):
    def decode(code):
        value = code.astype(jnp.float32)
        size = jnp.exp2(jnp.abs(value) * (1.0 / per_octave) + LOW_OCTAVE)
        return jnp.where(code > 0, size, jnp.where(code < 0, -size, 0.0))

    def add(offset, d, totals):
        word = recv_ref[d * HALVES + offset]
        return totals[0] + decode(word >> 16), totals[1] + decode((word << 16) >> 16)

    zero = jnp.zeros((SIDE, LANES), jnp.float32)
    chips = recv_ref.shape[0] // HALVES
    half = lax.axis_index("half")
    for offset, out_ref in ((half, own_ref), (1 - half, other_ref)):
        totals = lax.fori_loop(
            0, chips, functools.partial(add, offset), (zero, zero), unroll=4
        )
        peak = jnp.max(jnp.maximum(*map(jnp.abs, totals)), axis=0, keepdims=True)
        exponent = jnp.floor(jnp.log(jnp.maximum(peak, SMALLEST)) * INV_LN2)
        scale = jnp.exp2(CODE_BITS - exponent)
        high, low = (jnp.round(total * scale).astype(jnp.int32) for total in totals)
        code_ref[offset, pl.ds(0, SIDE), :] = (high << 16) | (low & 0xFFFF)
        code_ref[offset, pl.ds(SIDE, EXP_ROWS), :] = jnp.broadcast_to(
            exponent.astype(jnp.int32), (EXP_ROWS, LANES)
        )
        for pair in range(PAIRS):
            out_ref[pair] = totals[pair]


def sum_kernel(live_ref, own_ref, other_ref, arrived_ref, grad_ref, square_ref, turned_ref):
    slot = lax.broadcasted_iota(jnp.int32, (SIDE, LANES), 1) // SIDE
    half = lax.axis_index("half")

    def totals(offset, sum_ref, live):
        word = arrived_ref[offset, pl.ds(0, SIDE), :]
        exponent = arrived_ref[offset, pl.ds(SIDE, EXP_ROWS), :][:1].astype(jnp.float32)
        scale = jnp.exp2(exponent - CODE_BITS)
        arrived = (word >> 16, (word << 16) >> 16)
        return [
            jnp.where(
                slot + pair * 2 < live,
                sum_ref[pair] + arrived[pair].astype(jnp.float32) * scale,
                0.0,
            )
            for pair in range(PAIRS)
        ]

    own = totals(half, own_ref, live_ref[0:1, :])
    other = totals(1 - half, other_ref, live_ref[16:17, :])
    square = functools.reduce(jnp.add, [total * total for total in own + other])
    for pair in range(PAIRS):
        turned = own[pair].T
        turned_ref[pair] = jnp.concatenate([turned, turned], axis=1)
    low_lane = lax.broadcasted_iota(jnp.int32, (TILES, LANES), 1) < SIDE
    for s in range(SLOTS):
        base = (s % 2) * SIDE
        even = turned_ref[s // 2, pl.ds(base, TILES, stride=2), :]
        odd = turned_ref[s // 2, pl.ds(base + 1, TILES, stride=2), :]
        grad_ref[pl.ds(s, TILES, stride=SLOTS), :] = jnp.where(low_lane, even, odd)
    square = jnp.sum(square, axis=0, keepdims=True)
    square_ref[...] = jnp.broadcast_to(square[None], square_ref.shape)


def update_kernel(
    live_ref, square_ref, grad_ref, state_ref,
    own_ref, new_master_ref, new_moment_ref, new_variance_ref, clipped_ref,
):
    square = square_ref[0]
    for owner in range(1, square_ref.shape[0]):
        square = square + square_ref[owner]
    square = jnp.sum(square, axis=1, keepdims=True)
    entries = live_ref[8:9, :].astype(jnp.float32) * BLOCK
    clip = jnp.minimum(1.0, 1.0 / jnp.sqrt(square / entries + 1e-06))
    for t in range(TILES):
        lanes = pl.ds(t * LANES, LANES)
        clipped = clip * grad_ref[pl.ds(t * SLOTS, SLOTS), :]
        moment = 0.9 * state_ref[1, :, lanes] + 0.1 * clipped
        variance = 0.95 * state_ref[2, :, lanes] + 0.05 * clipped * clipped
        master = state_ref[0, :, lanes]
        moment_hat = moment / (1.0 - 0.9**20)
        variance_hat = variance / (1.0 - 0.95**20)
        step = moment_hat / (jnp.sqrt(variance_hat) + 1e-08) + 0.1 * master
        master = master - 0.02 * step
        clipped_ref[:, lanes] = clipped
        new_moment_ref[:, lanes] = moment
        new_variance_ref[:, lanes] = variance
        new_master_ref[:, lanes] = master
    own_ref[...] = new_master_ref[...].astype(jnp.bfloat16)


def spread_kernel(own_ref, other_ref, spread_ref):
    half = lax.axis_index("half")
    own, other = own_ref[...], other_ref[...]
    for chip in range(spread_ref.shape[0]):
        spread_ref[chip, half] = own
        spread_ref[chip, 1 - half] = other


def store_kernel(after_ref, *refs):
    half = len(refs) // 2
    for source, target in zip(refs[:half], refs[half:]):
        target[...] = source[...]


def publish_kernel(mine_ref, other_ref, out_ref):
    rows = CORES * SLOTS
    chips = mine_ref.shape[0]
    core = lax.axis_index("core")

    def weave(first_ref, second_ref):
        for half in range(HALVES):
            for chip in range(0, chips, 2):
                parts = []
                for k in range(2):
                    parts.append(first_ref[chip + k, half])
                    parts.append(second_ref[chip + k, half])
                block = jnp.concatenate(parts, axis=0)
                out_ref[pl.ds((half * chips + chip) * rows, 2 * rows), :] = block

    @pl.when(core == 0)
    def _():
        weave(mine_ref, other_ref)

    @pl.when(core == 1)
    def _():
        weave(other_ref, mine_ref)


VMEM = pl.BlockSpec(memory_space=pltpu.VMEM)
SMEM = pl.BlockSpec(memory_space=pltpu.SMEM)
ANY = pl.BlockSpec(memory_space=pl.ANY)
PARAMS = pltpu.CompilerParams(vmem_limit_bytes=40 * 1024 * 1024)


def local(hidden, grad_out, block_list, live_block_count, master, moment, variance):
    chips = lax.axis_size(CHIPS)
    tokens = hidden.shape[0]
    swap = [(0, 1), (1, 0)]
    shape = jax.ShapeDtypeStruct(master.shape, jnp.float32)
    kept = pltpu.VMEM(master.shape, jnp.float32)
    blocks = block_list.T
    top_octave = math.log2(CORES * tokens * LARGEST * LARGEST) + 0.05
    per_octave = 32767 / (top_octave - LOW_OCTAVE)
    cost = pl.CostEstimate(
        flops=2 * chips * SLOTS * SIDE * LANES * tokens,
        bytes_accessed=2 * (hidden.size + grad_out.size),
        transcendentals=0,
    )
    terms = pltpu.VMEM((chips, PAIRS * SIDE, LANES), jnp.float32)
    partner_terms, hidden, turned, state = pl.pallas_call(
        partner_terms_kernel,
        out_shape=(
            terms,
            pltpu.VMEM(hidden.shape, hidden.dtype),
            pltpu.VMEM(grad_out.shape[::-1], grad_out.dtype),
            pltpu.VMEM((3,) + master.shape, jnp.float32),
        ),
        in_specs=[ANY] * 6,
        out_specs=(VMEM,) * 4,
        scratch_shapes=[
            pltpu.SMEM(blocks.shape, jnp.int32),
            pltpu.VMEM(grad_out.shape, grad_out.dtype),
            pltpu.SemaphoreType.DMA((4 + GRAD_PARTS + HIDDEN_PARTS,)),
        ],
        compiler_params=PARAMS,
        cost_estimate=cost,
        name="partner_terms",
    )(
        *(
            pltpu.with_memory_space_constraint(x, pltpu.HBM)
            for x in (blocks, hidden, grad_out, master, moment, variance)
        )
    )
    arrived = lax.ppermute(partner_terms, "core", swap)
    own_terms, live_rows = pl.pallas_call(
        own_terms_kernel,
        out_shape=(terms, pltpu.VMEM((24, LANES), jnp.int32)),
        in_specs=[SMEM, SMEM, VMEM, VMEM],
        out_specs=(VMEM, VMEM),
        compiler_params=PARAMS,
        cost_estimate=cost,
        name="own_terms",
    )(blocks, live_block_count, hidden, turned)
    codes = pl.pallas_call(
        functools.partial(code_kernel, per_octave),
        out_shape=pltpu.VMEM((chips, SIDE, LANES), jnp.int32),
        in_specs=[VMEM, VMEM],
        out_specs=VMEM,
        compiler_params=PARAMS,
        name="code_terms",
    )(own_terms, arrived)
    received = lax.all_to_all(codes, "chip", split_axis=0, concat_axis=0, tiled=True)
    sums = pltpu.VMEM((PAIRS, SIDE, LANES), jnp.float32)
    own_sum, other_sum, sum_codes = pl.pallas_call(
        functools.partial(half_sum_kernel, per_octave),
        out_shape=(sums, sums, pltpu.VMEM((HALVES, SIDE + EXP_ROWS, LANES), jnp.int32)),
        in_specs=[VMEM],
        out_specs=(VMEM,) * 3,
        compiler_params=PARAMS,
        name="sum_half",
    )(received)
    arrived = lax.ppermute(sum_codes, "half", swap)
    gradient, square = pl.pallas_call(
        sum_kernel,
        out_shape=(
            pltpu.VMEM((TILES * SLOTS, LANES), jnp.float32),
            pltpu.VMEM((chips * CORES // HALVES, 1, LANES), jnp.float32),
        ),
        in_specs=[VMEM] * 4,
        out_specs=(VMEM, VMEM),
        scratch_shapes=[pltpu.VMEM((PAIRS, LANES, LANES), jnp.float32)],
        compiler_params=PARAMS,
        name="sum_pair",
    )(live_rows, own_sum, other_sum, arrived)
    square = lax.all_to_all(square, ("core", "chip"), split_axis=0, concat_axis=0, tiled=True)
    rows = pltpu.VMEM(master.shape, jnp.bfloat16)
    own_rows, *updated = pl.pallas_call(
        update_kernel,
        out_shape=(rows, kept, kept, kept, kept),
        in_specs=[VMEM] * 4,
        out_specs=(VMEM,) * 5,
        compiler_params=PARAMS,
        name="adamw",
    )(live_rows, square, gradient, state)
    other_rows = lax.ppermute(own_rows, "half", swap)
    spread = pl.pallas_call(
        spread_kernel,
        out_shape=pltpu.VMEM((chips // HALVES, HALVES) + master.shape, jnp.bfloat16),
        in_specs=[VMEM, VMEM],
        out_specs=VMEM,
        compiler_params=PARAMS,
        name="spread_rows",
    )(own_rows, other_rows)
    mine = lax.all_to_all(spread, "chip", split_axis=0, concat_axis=0, tiled=True)
    other = lax.ppermute(mine, "core", swap)
    results = pl.pallas_call(
        store_kernel,
        out_shape=(shape,) * 4,
        in_specs=[ANY] + [VMEM] * 4,
        out_specs=(VMEM,) * 4,
        compiler_params=PARAMS,
        name="store_state",
    )(mine, *updated)
    published = pl.pallas_call(
        publish_kernel,
        out_shape=jax.ShapeDtypeStruct((chips * CORES * SLOTS, BLOCK), jnp.bfloat16),
        in_specs=[VMEM, VMEM],
        out_specs=VMEM,
        compiler_params=PARAMS,
        name="publish",
    )(mine, other)
    return (*results, published)


def solution(mesh):
    devices = mesh.devices.reshape(HALVES, -1, CORES)
    rows = P(AXES, None)
    return jax.shard_map(
        local,
        mesh=Mesh(devices, AXES),
        in_specs=(rows, rows, P(), P(), rows, rows, rows),
        out_specs=(rows, rows, rows, rows, P()),
        check_vma=False,
    )
```

```python
import functools
import math

import jax
import jax.numpy as jnp
from jax import lax
from jax.experimental import pallas as pl
from jax.experimental.pallas import tpu as pltpu
from jax.sharding import Mesh
from jax.sharding import PartitionSpec as P

SIDE = 64
LANES = 128
SLOTS = 4
PAIRS = SLOTS // 2
BLOCK = SIDE * SIDE
TILES = BLOCK // LANES
LOW_OCTAVE = -36
LARGEST = 6.0
SMALLEST = 1e-30
CODE_BITS = 13
EXP_ROWS = 8
GRAD_PARTS = 4
HIDDEN_PARTS = 8
CORES = 2
HALVES = 2
AXES = ("half", "chip", "core")
CHIPS = ("chip", "half")
INV_LN2 = 1.4426950408889634


def block_products(core, blocks_ref, hidden_ref, turned_ref, out_ref):
    low_lane = lax.broadcasted_iota(jnp.int32, (SIDE, LANES), 1) < SIDE

    chips = out_ref.shape[0] // HALVES

    def one_chip(peer, carry):
        owner = ((peer % HALVES) * chips + peer // HALVES) * CORES + core
        for pair in range(PAIRS):
            lefts, rights, rows = [], [], []
            for k in range(2):
                slot = owner * SLOTS + pair * 2 + k
                r = blocks_ref[0, slot]
                c = blocks_ref[1, slot]
                lefts.append(turned_ref[pl.ds(pl.multiple_of(c * SIDE, SIDE), SIDE), :])
                lanes = pl.ds(pl.multiple_of((r // 2) * LANES, LANES), LANES)
                rights.append(hidden_ref[:, lanes])
                rows.append(r)
            product = jnp.dot(
                jnp.concatenate(lefts, axis=0),
                jnp.concatenate(rights, axis=1),
                preferred_element_type=jnp.float32,
            )
            first = pltpu.roll(product[:SIDE, :LANES], (rows[0] % 2) * SIDE, 1)
            second = pltpu.roll(product[SIDE:, LANES:], ((rows[1] + 1) % 2) * SIDE, 1)
            out_ref[peer, pl.ds(pair * SIDE, SIDE), :] = jnp.where(low_lane, first, second)
        return carry

    lax.fori_loop(0, out_ref.shape[0], one_chip, 0, unroll=16)


def partner_terms_kernel(
    blocks_hbm, hidden_hbm, grad_hbm, master_hbm, moment_hbm, variance_hbm,
    out_ref, hidden_ref, turned_ref, state_ref, blocks_ref, grad_ref, sems,
):
    copies = [pltpu.make_async_copy(blocks_hbm, blocks_ref, sems.at[0])]
    for source, target, parts in ((grad_hbm, grad_ref, GRAD_PARTS), (hidden_hbm, hidden_ref, HIDDEN_PARTS)):
        step = source.shape[0] // parts
        for k in range(parts):
            rows = pl.ds(k * step, step)
            copies.append(
                pltpu.make_async_copy(source.at[rows], target.at[rows], sems.at[len(copies)])
            )
    for k, source in enumerate((master_hbm, moment_hbm, variance_hbm)):
        copies.append(pltpu.make_async_copy(source, state_ref.at[k], sems.at[len(copies)]))
    for copy in copies:
        copy.start()
    grad_end = 1 + GRAD_PARTS
    hidden_end = grad_end + HIDDEN_PARTS
    for copy in copies[:grad_end]:
        copy.wait()
    for k in range(grad_ref.shape[1] // LANES):
        turned_ref[pl.ds(k * LANES, LANES), :] = grad_ref[:, pl.ds(k * LANES, LANES)].T
    for copy in copies[grad_end:hidden_end]:
        copy.wait()
    block_products(1 - lax.axis_index("core"), blocks_ref, hidden_ref, turned_ref, out_ref)
    for copy in copies[hidden_end:]:
        copy.wait()


def own_terms_kernel(
    blocks_ref, live_ref, hidden_ref, turned_ref, out_ref, live_rows_ref
):
    block_products(lax.axis_index("core"), blocks_ref, hidden_ref, turned_ref, out_ref)
    total = live_ref[0]
    for owner in range(1, live_ref.shape[0]):
        total = total + live_ref[owner]
    owners = live_ref.shape[0] // HALVES
    me = lax.axis_index(AXES[1:])
    for half in range(HALVES):
        live = live_ref[half * owners + me]
        live_rows_ref[half] = jnp.full((8, LANES), live, jnp.int32)
    live_rows_ref[HALVES] = jnp.full((8, LANES), total, jnp.int32)


def code_kernel(per_octave, own_ref, other_ref, out_ref):
    def encode(value):
        octave = jnp.log(jnp.maximum(jnp.abs(value), 2.0**LOW_OCTAVE)) * INV_LN2
        code = (octave - LOW_OCTAVE) * per_octave
        return jnp.round(jnp.where(value < 0, -code, code)).astype(jnp.int32)

    def one_chip(chip, carry):
        code = []
        for pair in range(PAIRS):
            rows = pl.ds(pair * SIDE, SIDE)
            code.append(encode(own_ref[chip, rows, :] + other_ref[chip, rows, :]))
        out_ref[chip] = (code[0] << 16) | (code[1] & 0xFFFF)
        return carry

    lax.fori_loop(0, out_ref.shape[0], one_chip, 0, unroll=2)


def half_sum_kernel(per_octave, after_ref, recv_ref, code_ref):
    def decode(code):
        value = code.astype(jnp.float32)
        size = jnp.exp2(jnp.abs(value) * (1.0 / per_octave) + LOW_OCTAVE)
        return jnp.where(code > 0, size, jnp.where(code < 0, -size, 0.0))

    def add(offset, d, totals):
        word = recv_ref[d * HALVES + offset]
        return totals[0] + decode(word >> 16), totals[1] + decode((word << 16) >> 16)

    zero = jnp.zeros((SIDE, LANES), jnp.float32)
    chips = recv_ref.shape[0] // HALVES
    for offset in range(HALVES):
        totals = lax.fori_loop(
            0, chips, functools.partial(add, offset), (zero, zero), unroll=4
        )
        peak = jnp.max(jnp.maximum(*map(jnp.abs, totals)), axis=0, keepdims=True)
        exponent = jnp.floor(jnp.log(jnp.maximum(peak, SMALLEST)) * INV_LN2)
        scale = jnp.exp2(CODE_BITS - exponent)
        high, low = (jnp.round(total * scale).astype(jnp.int32) for total in totals)
        code_ref[offset, pl.ds(0, SIDE), :] = (high << 16) | (low & 0xFFFF)
        code_ref[offset, pl.ds(SIDE, EXP_ROWS), :] = jnp.broadcast_to(
            exponent.astype(jnp.int32), (EXP_ROWS, LANES)
        )


def sum_kernel(live_ref, own_ref, arrived_ref, grad_ref, square_ref, turned_ref):
    slot = lax.broadcasted_iota(jnp.int32, (SIDE, LANES), 1) // SIDE
    low_lane = lax.broadcasted_iota(jnp.int32, (TILES, LANES), 1) < SIDE

    def decode(code_ref, half):
        word = code_ref[half, pl.ds(0, SIDE), :]
        exponent = code_ref[half, pl.ds(SIDE, EXP_ROWS), :][:1].astype(jnp.float32)
        scale = jnp.exp2(exponent - CODE_BITS)
        return [code.astype(jnp.float32) * scale for code in (word >> 16, (word << 16) >> 16)]

    square = jnp.zeros((SIDE, LANES), jnp.float32)
    for half in range(HALVES):
        live = live_ref[half, 0:1, :]
        own, arrived = decode(own_ref, half), decode(arrived_ref, half)
        for pair in range(PAIRS):
            total = jnp.where(slot + pair * 2 < live, own[pair] + arrived[pair], 0.0)
            square = square + total * total
            turned = total.T
            turned_ref[half, pair] = jnp.concatenate([turned, turned], axis=1)
        for s in range(SLOTS):
            base = (s % 2) * SIDE
            even = turned_ref[half, s // 2, pl.ds(base, TILES, stride=2), :]
            odd = turned_ref[half, s // 2, pl.ds(base + 1, TILES, stride=2), :]
            grad_ref[half, pl.ds(s, TILES, stride=SLOTS), :] = jnp.where(low_lane, even, odd)
    square = jnp.sum(square, axis=0, keepdims=True)
    square_ref[...] = jnp.broadcast_to(square[None], square_ref.shape)


def update_kernel(
    live_ref, square_ref, grad_ref, state_ref, other_state_ref,
    spread_ref, new_master_ref, new_moment_ref, new_variance_ref, clipped_ref, rows_ref,
):
    square = square_ref[0]
    for owner in range(1, square_ref.shape[0]):
        square = square + square_ref[owner]
    square = jnp.sum(square, axis=1, keepdims=True)
    entries = live_ref[HALVES, 0:1, :].astype(jnp.float32) * BLOCK
    clip = jnp.minimum(1.0, 1.0 / jnp.sqrt(square / entries + 1e-06))
    half = lax.axis_index("half")

    def step(grad, state):
        clipped = clip * grad
        master, moment, variance = state
        moment = 0.9 * moment + 0.1 * clipped
        variance = 0.95 * variance + 0.05 * clipped * clipped
        moment_hat = moment / (1.0 - 0.9**20)
        variance_hat = variance / (1.0 - 0.95**20)
        change = moment_hat / (jnp.sqrt(variance_hat) + 1e-08) + 0.1 * master
        return master - 0.02 * change, moment, variance, clipped

    for t in range(TILES):
        lanes = pl.ds(t * LANES, LANES)
        rows = pl.ds(t * SLOTS, SLOTS)
        master, moment, variance, clipped = step(
            grad_ref[half, rows, :], [state_ref[k, :, lanes] for k in range(3)]
        )
        clipped_ref[:, lanes] = clipped
        new_moment_ref[:, lanes] = moment
        new_variance_ref[:, lanes] = variance
        new_master_ref[:, lanes] = master
        rows_ref[:, lanes] = step(
            grad_ref[1 - half, rows, :], [other_state_ref[k, :, lanes] for k in range(3)]
        )[0]
    own = new_master_ref[...].astype(jnp.bfloat16)
    other = rows_ref[...].astype(jnp.bfloat16)
    for chip in range(spread_ref.shape[0]):
        spread_ref[chip, half] = own
        spread_ref[chip, 1 - half] = other


def store_kernel(after_ref, *refs):
    half = len(refs) // 2
    for source, target in zip(refs[:half], refs[half:]):
        target[...] = source[...]


def publish_kernel(mine_ref, other_ref, out_ref):
    rows = CORES * SLOTS
    chips = mine_ref.shape[0]
    core = lax.axis_index("core")

    def weave(first_ref, second_ref):
        for half in range(HALVES):
            for chip in range(0, chips, 2):
                parts = []
                for k in range(2):
                    parts.append(first_ref[chip + k, half])
                    parts.append(second_ref[chip + k, half])
                block = jnp.concatenate(parts, axis=0)
                out_ref[pl.ds((half * chips + chip) * rows, 2 * rows), :] = block

    @pl.when(core == 0)
    def _():
        weave(mine_ref, other_ref)

    @pl.when(core == 1)
    def _():
        weave(other_ref, mine_ref)


VMEM = pl.BlockSpec(memory_space=pltpu.VMEM)
SMEM = pl.BlockSpec(memory_space=pltpu.SMEM)
ANY = pl.BlockSpec(memory_space=pl.ANY)
PARAMS = pltpu.CompilerParams(vmem_limit_bytes=40 * 1024 * 1024)


def local(hidden, grad_out, block_list, live_block_count, master, moment, variance):
    chips = lax.axis_size(CHIPS)
    tokens = hidden.shape[0]
    swap = [(0, 1), (1, 0)]
    shape = jax.ShapeDtypeStruct(master.shape, jnp.float32)
    kept = pltpu.VMEM(master.shape, jnp.float32)
    blocks = block_list.T
    top_octave = math.log2(CORES * tokens * LARGEST * LARGEST) + 0.05
    per_octave = 32767 / (top_octave - LOW_OCTAVE)
    cost = pl.CostEstimate(
        flops=2 * chips * SLOTS * SIDE * LANES * tokens,
        bytes_accessed=2 * (hidden.size + grad_out.size),
        transcendentals=0,
    )
    terms = pltpu.VMEM((chips, PAIRS * SIDE, LANES), jnp.float32)
    partner_terms, hidden, turned, state = pl.pallas_call(
        partner_terms_kernel,
        out_shape=(
            terms,
            pltpu.VMEM(hidden.shape, hidden.dtype),
            pltpu.VMEM(grad_out.shape[::-1], grad_out.dtype),
            pltpu.VMEM((3,) + master.shape, jnp.float32),
        ),
        in_specs=[ANY] * 6,
        out_specs=(VMEM,) * 4,
        scratch_shapes=[
            pltpu.SMEM(blocks.shape, jnp.int32),
            pltpu.VMEM(grad_out.shape, grad_out.dtype),
            pltpu.SemaphoreType.DMA((4 + GRAD_PARTS + HIDDEN_PARTS,)),
        ],
        compiler_params=PARAMS,
        cost_estimate=cost,
        name="partner_terms",
    )(
        *(
            pltpu.with_memory_space_constraint(x, pltpu.HBM)
            for x in (blocks, hidden, grad_out, master, moment, variance)
        )
    )
    arrived = lax.ppermute(partner_terms, "core", swap)
    other_state = lax.ppermute(state, "half", swap)
    own_terms, live_rows = pl.pallas_call(
        own_terms_kernel,
        out_shape=(terms, pltpu.VMEM((HALVES + 1, 8, LANES), jnp.int32)),
        in_specs=[SMEM, SMEM, VMEM, VMEM],
        out_specs=(VMEM, VMEM),
        compiler_params=PARAMS,
        cost_estimate=cost,
        name="own_terms",
    )(blocks, live_block_count, hidden, turned)
    codes = pl.pallas_call(
        functools.partial(code_kernel, per_octave),
        out_shape=pltpu.VMEM((chips, SIDE, LANES), jnp.int32),
        in_specs=[VMEM, VMEM],
        out_specs=VMEM,
        compiler_params=PARAMS,
        name="code_terms",
    )(own_terms, arrived)
    received = lax.cond(
        live_block_count[0] > 0,
        lambda x: lax.all_to_all(x, "chip", split_axis=0, concat_axis=0, tiled=True),
        lambda x: x,
        codes,
    )
    sum_codes = pl.pallas_call(
        functools.partial(half_sum_kernel, per_octave),
        out_shape=pltpu.VMEM((HALVES, SIDE + EXP_ROWS, LANES), jnp.int32),
        in_specs=[ANY, VMEM],
        out_specs=VMEM,
        compiler_params=PARAMS,
        name="sum_half",
    )(other_state, received)
    arrived = lax.ppermute(sum_codes, "half", swap)
    gradient, square = pl.pallas_call(
        sum_kernel,
        out_shape=(
            pltpu.VMEM((HALVES, TILES * SLOTS, LANES), jnp.float32),
            pltpu.VMEM((chips * CORES // HALVES, 1, LANES), jnp.float32),
        ),
        in_specs=[VMEM] * 3,
        out_specs=(VMEM, VMEM),
        scratch_shapes=[pltpu.VMEM((HALVES, PAIRS, LANES, LANES), jnp.float32)],
        compiler_params=PARAMS,
        name="sum_pair",
    )(live_rows, sum_codes, arrived)
    square = lax.all_to_all(square, ("core", "chip"), split_axis=0, concat_axis=0, tiled=True)
    spread, *updated = pl.pallas_call(
        update_kernel,
        out_shape=(
            pltpu.VMEM((chips // HALVES, HALVES) + master.shape, jnp.bfloat16),
            kept,
            kept,
            kept,
            kept,
        ),
        in_specs=[VMEM] * 5,
        out_specs=(VMEM,) * 5,
        scratch_shapes=[pltpu.VMEM(master.shape, jnp.float32)],
        compiler_params=PARAMS,
        name="adamw",
    )(live_rows, square, gradient, state, other_state)
    mine = lax.all_to_all(spread, "chip", split_axis=0, concat_axis=0, tiled=True)
    other = lax.ppermute(mine, "core", swap)
    results = pl.pallas_call(
        store_kernel,
        out_shape=(shape,) * 4,
        in_specs=[ANY] + [VMEM] * 4,
        out_specs=(VMEM,) * 4,
        compiler_params=PARAMS,
        name="store_state",
    )(mine, *updated)
    published = pl.pallas_call(
        publish_kernel,
        out_shape=jax.ShapeDtypeStruct((chips * CORES * SLOTS, BLOCK), jnp.bfloat16),
        in_specs=[VMEM, VMEM],
        out_specs=VMEM,
        compiler_params=PARAMS,
        name="publish",
    )(mine, other)
    return (*results, published)


def solution(mesh):
    devices = mesh.devices.reshape(HALVES, -1, CORES)
    rows = P(AXES, None)
    return jax.shard_map(
        local,
        mesh=Mesh(devices, AXES),
        in_specs=(rows, rows, P(), P(), rows, rows, rows),
        out_specs=(rows, rows, rows, rows, P()),
        check_vma=False,
    )
```

```python
import functools
import math

import jax
import jax.numpy as jnp
from jax import lax
from jax.experimental import pallas as pl
from jax.experimental.pallas import tpu as pltpu
from jax.sharding import Mesh
from jax.sharding import PartitionSpec as P

SIDE = 64
LANES = 128
SLOTS = 4
PAIRS = SLOTS // 2
BLOCK = SIDE * SIDE
TILES = BLOCK // LANES
LOW_OCTAVE = -36
LARGEST = 6.0
SMALLEST = 1e-30
CODE_BITS = 13
EXP_ROWS = 8
GRAD_PARTS = 8
HIDDEN_PARTS = 16
STORE_PARTS = 4
CORES = 2
HALVES = 2
SWAP = [(0, 1), (1, 0)]
AXES = ("half", "chip", "core")
CHIPS = ("chip", "half")
INV_LN2 = 1.4426950408889634


def block_products(core, blocks_ref, hidden_ref, turned_ref, out_ref):
    low_lane = lax.broadcasted_iota(jnp.int32, (SIDE, LANES), 1) < SIDE

    chips = out_ref.shape[0] // HALVES

    def one_chip(peer, carry):
        owner = ((peer % HALVES) * chips + peer // HALVES) * CORES + core
        for pair in range(PAIRS):
            lefts, rights, rows = [], [], []
            for k in range(2):
                slot = owner * SLOTS + pair * 2 + k
                r = blocks_ref[0, slot]
                c = blocks_ref[1, slot]
                lefts.append(turned_ref[pl.ds(pl.multiple_of(c * SIDE, SIDE), SIDE), :])
                lanes = pl.ds(pl.multiple_of((r // 2) * LANES, LANES), LANES)
                rights.append(hidden_ref[:, lanes])
                rows.append(r)
            product = jnp.dot(
                jnp.concatenate(lefts, axis=0),
                jnp.concatenate(rights, axis=1),
                preferred_element_type=jnp.float32,
            )
            first = pltpu.roll(product[:SIDE, :LANES], (rows[0] % 2) * SIDE, 1)
            second = pltpu.roll(product[SIDE:, LANES:], ((rows[1] + 1) % 2) * SIDE, 1)
            out_ref[peer, pl.ds(pair * SIDE, SIDE), :] = jnp.where(low_lane, first, second)
        return carry

    lax.fori_loop(0, out_ref.shape[0], one_chip, 0, unroll=16)


def gather_kernel(master_hbm, moment_hbm, variance_hbm, state_ref, sems):
    copies = [
        pltpu.make_async_copy(source, state_ref.at[k], sems.at[k])
        for k, source in enumerate((master_hbm, moment_hbm, variance_hbm))
    ]
    for copy in copies:
        copy.start()
    for copy in copies:
        copy.wait()


def partner_terms_kernel(
    blocks_hbm, hidden_hbm, grad_hbm, out_ref, hidden_ref, turned_ref, blocks_ref, grad_ref, sems
):
    copies = [pltpu.make_async_copy(blocks_hbm, blocks_ref, sems.at[0])]
    for source, target, parts in ((grad_hbm, grad_ref, GRAD_PARTS), (hidden_hbm, hidden_ref, HIDDEN_PARTS)):
        step = source.shape[0] // parts
        for k in range(parts):
            rows = pl.ds(k * step, step)
            copies.append(
                pltpu.make_async_copy(source.at[rows], target.at[rows], sems.at[len(copies)])
            )
    for copy in copies:
        copy.start()
    grad_end = 1 + GRAD_PARTS
    for copy in copies[:grad_end]:
        copy.wait()
    for k in range(grad_ref.shape[1] // LANES):
        turned_ref[pl.ds(k * LANES, LANES), :] = grad_ref[:, pl.ds(k * LANES, LANES)].T
    for copy in copies[grad_end:]:
        copy.wait()
    block_products(1 - lax.axis_index("core"), blocks_ref, hidden_ref, turned_ref, out_ref)


def own_terms_kernel(
    blocks_ref, live_ref, hidden_ref, turned_ref, out_ref, live_rows_ref
):
    block_products(lax.axis_index("core"), blocks_ref, hidden_ref, turned_ref, out_ref)
    total = live_ref[0]
    for owner in range(1, live_ref.shape[0]):
        total = total + live_ref[owner]
    owners = live_ref.shape[0] // HALVES
    me = lax.axis_index(AXES[1:])
    for half in range(HALVES):
        live = live_ref[half * owners + me]
        live_rows_ref[half] = jnp.full((8, LANES), live, jnp.int32)
    live_rows_ref[HALVES] = jnp.full((8, LANES), total, jnp.int32)


def code_kernel(per_octave, own_ref, other_ref, out_ref):
    def encode(value):
        octave = jnp.log(jnp.maximum(jnp.abs(value), 2.0**LOW_OCTAVE)) * INV_LN2
        code = (octave - LOW_OCTAVE) * per_octave
        return jnp.round(jnp.where(value < 0, -code, code)).astype(jnp.int32)

    def one_chip(chip, carry):
        code = []
        for pair in range(PAIRS):
            rows = pl.ds(pair * SIDE, SIDE)
            code.append(encode(own_ref[chip, rows, :] + other_ref[chip, rows, :]))
        out_ref[chip] = (code[0] << 16) | (code[1] & 0xFFFF)
        return carry

    lax.fori_loop(0, out_ref.shape[0], one_chip, 0, unroll=2)


def half_sum_kernel(per_octave, after_ref, recv_ref, code_ref):
    def decode(code):
        value = code.astype(jnp.float32)
        size = jnp.exp2(jnp.abs(value) * (1.0 / per_octave) + LOW_OCTAVE)
        return jnp.where(code > 0, size, jnp.where(code < 0, -size, 0.0))

    def add(offset, d, totals):
        word = recv_ref[d * HALVES + offset]
        return totals[0] + decode(word >> 16), totals[1] + decode((word << 16) >> 16)

    zero = jnp.zeros((SIDE, LANES), jnp.float32)
    chips = recv_ref.shape[0] // HALVES
    for offset in range(HALVES):
        totals = lax.fori_loop(
            0, chips, functools.partial(add, offset), (zero, zero), unroll=4
        )
        peak = jnp.max(jnp.maximum(*map(jnp.abs, totals)), axis=0, keepdims=True)
        exponent = jnp.floor(jnp.log(jnp.maximum(peak, SMALLEST)) * INV_LN2)
        scale = jnp.exp2(CODE_BITS - exponent)
        high, low = (jnp.round(total * scale).astype(jnp.int32) for total in totals)
        code_ref[offset, pl.ds(0, SIDE), :] = (high << 16) | (low & 0xFFFF)
        code_ref[offset, pl.ds(SIDE, EXP_ROWS), :] = jnp.broadcast_to(
            exponent.astype(jnp.int32), (EXP_ROWS, LANES)
        )


def sum_kernel(live_ref, own_ref, arrived_ref, grad_ref, square_ref, turned_ref):
    slot = lax.broadcasted_iota(jnp.int32, (SIDE, LANES), 1) // SIDE
    low_lane = lax.broadcasted_iota(jnp.int32, (TILES, LANES), 1) < SIDE

    def decode(code_ref, half):
        word = code_ref[half, pl.ds(0, SIDE), :]
        exponent = code_ref[half, pl.ds(SIDE, EXP_ROWS), :][:1].astype(jnp.float32)
        scale = jnp.exp2(exponent - CODE_BITS)
        return [code.astype(jnp.float32) * scale for code in (word >> 16, (word << 16) >> 16)]

    square = jnp.zeros((SIDE, LANES), jnp.float32)
    for half in range(HALVES):
        live = live_ref[half, 0:1, :]
        own, arrived = decode(own_ref, half), decode(arrived_ref, half)
        for pair in range(PAIRS):
            total = jnp.where(slot + pair * 2 < live, own[pair] + arrived[pair], 0.0)
            square = square + total * total
            turned = total.T
            turned_ref[half, pair] = jnp.concatenate([turned, turned], axis=1)
        for s in range(SLOTS):
            base = (s % 2) * SIDE
            even = turned_ref[half, s // 2, pl.ds(base, TILES, stride=2), :]
            odd = turned_ref[half, s // 2, pl.ds(base + 1, TILES, stride=2), :]
            grad_ref[half, pl.ds(s, TILES, stride=SLOTS), :] = jnp.where(low_lane, even, odd)
    square = jnp.sum(square, axis=0, keepdims=True)
    square_ref[...] = jnp.broadcast_to(square[None], square_ref.shape)


def update_kernel(
    live_ref, square_ref, grad_ref, state_ref, other_state_ref,
    spread_ref, new_master_ref, new_moment_ref, new_variance_ref, clipped_ref, rows_ref,
):
    square = square_ref[0]
    for owner in range(1, square_ref.shape[0]):
        square = square + square_ref[owner]
    square = jnp.sum(square, axis=1, keepdims=True)
    entries = live_ref[HALVES, 0:1, :].astype(jnp.float32) * BLOCK
    clip = jnp.minimum(1.0, 1.0 / jnp.sqrt(square / entries + 1e-06))
    half = lax.axis_index("half")

    def step(grad, state):
        clipped = clip * grad
        master, moment, variance = state
        moment = 0.9 * moment + 0.1 * clipped
        variance = 0.95 * variance + 0.05 * clipped * clipped
        moment_hat = moment / (1.0 - 0.9**20)
        variance_hat = variance / (1.0 - 0.95**20)
        change = moment_hat / (jnp.sqrt(variance_hat) + 1e-08) + 0.1 * master
        return master - 0.02 * change, moment, variance, clipped

    for t in range(TILES):
        lanes = pl.ds(t * LANES, LANES)
        rows = pl.ds(t * SLOTS, SLOTS)
        master, moment, variance, clipped = step(
            grad_ref[half, rows, :], [state_ref[k, :, lanes] for k in range(3)]
        )
        clipped_ref[:, lanes] = clipped
        new_moment_ref[:, lanes] = moment
        new_variance_ref[:, lanes] = variance
        new_master_ref[:, lanes] = master
        rows_ref[:, lanes] = step(
            grad_ref[1 - half, rows, :], [other_state_ref[k, :, lanes] for k in range(3)]
        )[0]
    own = new_master_ref[...].astype(jnp.bfloat16)
    other = rows_ref[...].astype(jnp.bfloat16)
    for chip in range(spread_ref.shape[0]):
        spread_ref[chip, half] = own
        spread_ref[chip, 1 - half] = other


def store_kernel(after_ref, *refs):
    half = len(refs) // 2
    for source, target in zip(refs[:half], refs[half:]):
        target[...] = source[...]


def publish_kernel(mine_ref, other_ref, out_hbm, woven_ref, sems):
    rows = CORES * SLOTS
    chips = mine_ref.shape[0]
    parts = sems.shape[0] // HALVES
    step = chips // parts
    core = lax.axis_index("core")

    def weave(first_ref, second_ref):
        copies = []
        for half in range(HALVES):
            for part in range(parts):
                for chip in range(part * step, (part + 1) * step, 2):
                    pieces = []
                    for k in range(2):
                        pieces.append(first_ref[chip + k, half])
                        pieces.append(second_ref[chip + k, half])
                    block = jnp.concatenate(pieces, axis=0)
                    woven_ref[pl.ds((half * chips + chip) * rows, 2 * rows), :] = block
                span = pl.ds((half * chips + part * step) * rows, step * rows)
                copies.append(
                    pltpu.make_async_copy(
                        woven_ref.at[span], out_hbm.at[span], sems.at[len(copies)]
                    )
                )
                copies[-1].start()
        for copy in copies:
            copy.wait()

    @pl.when(core == 0)
    def _():
        weave(mine_ref, other_ref)

    @pl.when(core == 1)
    def _():
        weave(other_ref, mine_ref)


VMEM = pl.BlockSpec(memory_space=pltpu.VMEM)
SMEM = pl.BlockSpec(memory_space=pltpu.SMEM)
ANY = pl.BlockSpec(memory_space=pl.ANY)
PARAMS = pltpu.CompilerParams(vmem_limit_bytes=40 * 1024 * 1024)


def exchange_terms(hidden, grad_out, blocks, live_block_count):
    chips = lax.axis_size(CHIPS)
    tokens = hidden.shape[0]
    top_octave = math.log2(CORES * tokens * LARGEST * LARGEST) + 0.05
    per_octave = 32767 / (top_octave - LOW_OCTAVE)
    cost = pl.CostEstimate(
        flops=2 * chips * SLOTS * SIDE * LANES * tokens,
        bytes_accessed=2 * (hidden.size + grad_out.size),
        transcendentals=0,
    )
    terms = pltpu.VMEM((chips, PAIRS * SIDE, LANES), jnp.float32)
    partner_terms, hidden, turned = pl.pallas_call(
        partner_terms_kernel,
        out_shape=(
            terms,
            pltpu.VMEM(hidden.shape, hidden.dtype),
            pltpu.VMEM(grad_out.shape[::-1], grad_out.dtype),
        ),
        in_specs=[ANY] * 3,
        out_specs=(VMEM,) * 3,
        scratch_shapes=[
            pltpu.SMEM(blocks.shape, jnp.int32),
            pltpu.VMEM(grad_out.shape, grad_out.dtype),
            pltpu.SemaphoreType.DMA((1 + GRAD_PARTS + HIDDEN_PARTS,)),
        ],
        compiler_params=PARAMS,
        cost_estimate=cost,
        name="partner_terms",
    )(*(pltpu.with_memory_space_constraint(x, pltpu.HBM) for x in (blocks, hidden, grad_out)))
    arrived = lax.ppermute(partner_terms, "core", SWAP)
    own_terms, live_rows = pl.pallas_call(
        own_terms_kernel,
        out_shape=(terms, pltpu.VMEM((HALVES + 1, 8, LANES), jnp.int32)),
        in_specs=[SMEM, SMEM, VMEM, VMEM],
        out_specs=(VMEM, VMEM),
        compiler_params=PARAMS,
        cost_estimate=cost,
        name="own_terms",
    )(blocks, live_block_count, hidden, turned)
    codes = pl.pallas_call(
        functools.partial(code_kernel, per_octave),
        out_shape=pltpu.VMEM((chips, SIDE, LANES), jnp.int32),
        in_specs=[VMEM, VMEM],
        out_specs=VMEM,
        compiler_params=PARAMS,
        name="code_terms",
    )(own_terms, arrived)
    return lax.all_to_all(codes, "chip", split_axis=0, concat_axis=0, tiled=True), live_rows


def no_terms(hidden, grad_out, blocks, live_block_count):
    chips = lax.axis_size(CHIPS)
    return (
        jnp.zeros((chips, SIDE, LANES), jnp.int32),
        jnp.zeros((HALVES + 1, 8, LANES), jnp.int32),
    )


def local(hidden, grad_out, block_list, live_block_count, master, moment, variance):
    chips = lax.axis_size(CHIPS)
    shape = jax.ShapeDtypeStruct(master.shape, jnp.float32)
    kept = pltpu.VMEM(master.shape, jnp.float32)
    top_octave = math.log2(CORES * hidden.shape[0] * LARGEST * LARGEST) + 0.05
    per_octave = 32767 / (top_octave - LOW_OCTAVE)
    state = pl.pallas_call(
        gather_kernel,
        out_shape=pltpu.VMEM((3,) + master.shape, jnp.float32),
        in_specs=[ANY] * 3,
        out_specs=VMEM,
        scratch_shapes=[pltpu.SemaphoreType.DMA((3,))],
        compiler_params=PARAMS,
        name="gather_state",
    )(*(pltpu.with_memory_space_constraint(x, pltpu.HBM) for x in (master, moment, variance)))
    other_state = lax.ppermute(state, "half", SWAP)
    received, live_rows = lax.cond(
        live_block_count[0] > 0,
        exchange_terms,
        no_terms,
        hidden,
        grad_out,
        block_list.T,
        live_block_count,
    )
    sum_codes = pl.pallas_call(
        functools.partial(half_sum_kernel, per_octave),
        out_shape=pltpu.VMEM((HALVES, SIDE + EXP_ROWS, LANES), jnp.int32),
        in_specs=[ANY, VMEM],
        out_specs=VMEM,
        compiler_params=PARAMS,
        name="sum_half",
    )(other_state, received)
    arrived = lax.ppermute(sum_codes, "half", SWAP)
    gradient, square = pl.pallas_call(
        sum_kernel,
        out_shape=(
            pltpu.VMEM((HALVES, TILES * SLOTS, LANES), jnp.float32),
            pltpu.VMEM((chips * CORES // HALVES, 1, LANES), jnp.float32),
        ),
        in_specs=[VMEM] * 3,
        out_specs=(VMEM, VMEM),
        scratch_shapes=[pltpu.VMEM((HALVES, PAIRS, LANES, LANES), jnp.float32)],
        compiler_params=PARAMS,
        name="sum_pair",
    )(live_rows, sum_codes, arrived)
    square = lax.all_to_all(square, ("core", "chip"), split_axis=0, concat_axis=0, tiled=True)
    spread, *updated = pl.pallas_call(
        update_kernel,
        out_shape=(
            pltpu.VMEM((chips // HALVES, HALVES) + master.shape, jnp.bfloat16),
            kept,
            kept,
            kept,
            kept,
        ),
        in_specs=[VMEM] * 5,
        out_specs=(VMEM,) * 5,
        scratch_shapes=[pltpu.VMEM(master.shape, jnp.float32)],
        compiler_params=PARAMS,
        name="adamw",
    )(live_rows, square, gradient, state, other_state)
    mine = lax.all_to_all(spread, "chip", split_axis=0, concat_axis=0, tiled=True)
    other = lax.ppermute(mine, "core", SWAP)
    results = pl.pallas_call(
        store_kernel,
        out_shape=(shape,) * 4,
        in_specs=[ANY] + [VMEM] * 4,
        out_specs=(VMEM,) * 4,
        compiler_params=PARAMS,
        name="store_state",
    )(mine, *updated)
    published = pl.pallas_call(
        publish_kernel,
        out_shape=jax.ShapeDtypeStruct((chips * CORES * SLOTS, BLOCK), jnp.bfloat16),
        in_specs=[VMEM, VMEM],
        out_specs=ANY,
        scratch_shapes=[
            pltpu.VMEM((chips * CORES * SLOTS, BLOCK), jnp.bfloat16),
            pltpu.SemaphoreType.DMA((STORE_PARTS,)),
        ],
        compiler_params=PARAMS,
        name="publish",
    )(mine, other)
    return (*results, published)


def solution(mesh):
    devices = mesh.devices.reshape(HALVES, -1, CORES)
    rows = P(AXES, None)
    return jax.shard_map(
        local,
        mesh=Mesh(devices, AXES),
        in_specs=(rows, rows, P(), P(), rows, rows, rows),
        out_specs=(rows, rows, rows, rows, P()),
        check_vma=False,
    )
```

```python
import functools
import math

import jax
import jax.numpy as jnp
from jax import lax
from jax.experimental import pallas as pl
from jax.experimental.pallas import tpu as pltpu
from jax.sharding import Mesh
from jax.sharding import PartitionSpec as P

SIDE = 64
LANES = 128
SLOTS = 4
PAIRS = SLOTS // 2
BLOCK = SIDE * SIDE
TILES = BLOCK // LANES
LOW_OCTAVE = -36
LARGEST = 6.0
SMALLEST = 1e-30
CODE_BITS = 13
EXP_ROWS = 8
GRAD_PARTS = 4
HIDDEN_PARTS = 8
STORE_PARTS = 4
CORES = 2
HALVES = 2
AXES = ("half", "chip", "core")
CHIPS = ("chip", "half")
INV_LN2 = 1.4426950408889634


def block_products(core, blocks_ref, hidden_ref, turned_ref, out_ref):
    low_lane = lax.broadcasted_iota(jnp.int32, (SIDE, LANES), 1) < SIDE

    chips = out_ref.shape[0] // HALVES

    def one_chip(peer, carry):
        owner = ((peer % HALVES) * chips + peer // HALVES) * CORES + core
        for pair in range(PAIRS):
            lefts, rights, rows = [], [], []
            for k in range(2):
                slot = owner * SLOTS + pair * 2 + k
                r = blocks_ref[0, slot]
                c = blocks_ref[1, slot]
                lefts.append(turned_ref[pl.ds(pl.multiple_of(c * SIDE, SIDE), SIDE), :])
                lanes = pl.ds(pl.multiple_of((r // 2) * LANES, LANES), LANES)
                rights.append(hidden_ref[:, lanes])
                rows.append(r)
            product = jnp.dot(
                jnp.concatenate(lefts, axis=0),
                jnp.concatenate(rights, axis=1),
                preferred_element_type=jnp.float32,
            )
            first = pltpu.roll(product[:SIDE, :LANES], (rows[0] % 2) * SIDE, 1)
            second = pltpu.roll(product[SIDE:, LANES:], ((rows[1] + 1) % 2) * SIDE, 1)
            out_ref[peer, pl.ds(pair * SIDE, SIDE), :] = jnp.where(low_lane, first, second)
        return carry

    lax.fori_loop(0, out_ref.shape[0], one_chip, 0, unroll=16)


def partner_terms_kernel(
    blocks_hbm, hidden_hbm, grad_hbm, master_hbm, moment_hbm, variance_hbm,
    out_ref, hidden_ref, turned_ref, state_ref, blocks_ref, grad_ref, sems,
):
    copies = [pltpu.make_async_copy(blocks_hbm, blocks_ref, sems.at[0])]
    for source, target, parts in ((grad_hbm, grad_ref, GRAD_PARTS), (hidden_hbm, hidden_ref, HIDDEN_PARTS)):
        step = source.shape[0] // parts
        for k in range(parts):
            rows = pl.ds(k * step, step)
            copies.append(
                pltpu.make_async_copy(source.at[rows], target.at[rows], sems.at[len(copies)])
            )
    for k, source in enumerate((master_hbm, moment_hbm, variance_hbm)):
        copies.append(pltpu.make_async_copy(source, state_ref.at[k], sems.at[len(copies)]))
    for copy in copies:
        copy.start()
    grad_end = 1 + GRAD_PARTS
    hidden_end = grad_end + HIDDEN_PARTS
    for copy in copies[:grad_end]:
        copy.wait()
    for k in range(grad_ref.shape[1] // LANES):
        turned_ref[pl.ds(k * LANES, LANES), :] = grad_ref[:, pl.ds(k * LANES, LANES)].T
    for copy in copies[grad_end:hidden_end]:
        copy.wait()
    block_products(1 - lax.axis_index("core"), blocks_ref, hidden_ref, turned_ref, out_ref)
    for copy in copies[hidden_end:]:
        copy.wait()


def own_terms_kernel(
    blocks_ref, live_ref, hidden_ref, turned_ref, state_in, out_ref, live_rows_ref, state_ref
):
    block_products(lax.axis_index("core"), blocks_ref, hidden_ref, turned_ref, out_ref)
    total = live_ref[0]
    for owner in range(1, live_ref.shape[0]):
        total = total + live_ref[owner]
    owners = live_ref.shape[0] // HALVES
    me = lax.axis_index(AXES[1:])
    for half in range(HALVES):
        live = live_ref[half * owners + me]
        live_rows_ref[half] = jnp.full((8, LANES), live, jnp.int32)
    live_rows_ref[HALVES] = jnp.full((8, LANES), total, jnp.int32)
    state_ref[...] = state_in[...]


def code_kernel(per_octave, own_ref, other_ref, out_ref):
    def encode(value):
        octave = jnp.log(jnp.maximum(jnp.abs(value), 2.0**LOW_OCTAVE)) * INV_LN2
        code = (octave - LOW_OCTAVE) * per_octave
        return jnp.round(jnp.where(value < 0, -code, code)).astype(jnp.int32)

    def one_chip(chip, carry):
        code = []
        for pair in range(PAIRS):
            rows = pl.ds(pair * SIDE, SIDE)
            code.append(encode(own_ref[chip, rows, :] + other_ref[chip, rows, :]))
        out_ref[chip] = (code[0] << 16) | (code[1] & 0xFFFF)
        return carry

    lax.fori_loop(0, out_ref.shape[0], one_chip, 0, unroll=2)


def half_sum_kernel(per_octave, after_ref, recv_ref, code_ref):
    def decode(code):
        value = code.astype(jnp.float32)
        size = jnp.exp2(jnp.abs(value) * (1.0 / per_octave) + LOW_OCTAVE)
        return jnp.where(code > 0, size, jnp.where(code < 0, -size, 0.0))

    def add(offset, d, totals):
        word = recv_ref[d * HALVES + offset]
        return totals[0] + decode(word >> 16), totals[1] + decode((word << 16) >> 16)

    zero = jnp.zeros((SIDE, LANES), jnp.float32)
    chips = recv_ref.shape[0] // HALVES
    for offset in range(HALVES):
        totals = lax.fori_loop(
            0, chips, functools.partial(add, offset), (zero, zero), unroll=4
        )
        peak = jnp.max(jnp.maximum(*map(jnp.abs, totals)), axis=0, keepdims=True)
        exponent = jnp.floor(jnp.log(jnp.maximum(peak, SMALLEST)) * INV_LN2)
        scale = jnp.exp2(CODE_BITS - exponent)
        high, low = (jnp.round(total * scale).astype(jnp.int32) for total in totals)
        code_ref[offset, pl.ds(0, SIDE), :] = (high << 16) | (low & 0xFFFF)
        code_ref[offset, pl.ds(SIDE, EXP_ROWS), :] = jnp.broadcast_to(
            exponent.astype(jnp.int32), (EXP_ROWS, LANES)
        )


def sum_kernel(live_ref, own_ref, arrived_ref, grad_ref, square_ref, turned_ref):
    slot = lax.broadcasted_iota(jnp.int32, (SIDE, LANES), 1) // SIDE
    low_lane = lax.broadcasted_iota(jnp.int32, (TILES, LANES), 1) < SIDE

    def decode(code_ref, half):
        word = code_ref[half, pl.ds(0, SIDE), :]
        exponent = code_ref[half, pl.ds(SIDE, EXP_ROWS), :][:1].astype(jnp.float32)
        scale = jnp.exp2(exponent - CODE_BITS)
        return [code.astype(jnp.float32) * scale for code in (word >> 16, (word << 16) >> 16)]

    square = jnp.zeros((SIDE, LANES), jnp.float32)
    for half in range(HALVES):
        live = live_ref[half, 0:1, :]
        own, arrived = decode(own_ref, half), decode(arrived_ref, half)
        for pair in range(PAIRS):
            total = jnp.where(slot + pair * 2 < live, own[pair] + arrived[pair], 0.0)
            square = square + total * total
            turned = total.T
            turned_ref[half, pair] = jnp.concatenate([turned, turned], axis=1)
        for s in range(SLOTS):
            base = (s % 2) * SIDE
            even = turned_ref[half, s // 2, pl.ds(base, TILES, stride=2), :]
            odd = turned_ref[half, s // 2, pl.ds(base + 1, TILES, stride=2), :]
            grad_ref[half, pl.ds(s, TILES, stride=SLOTS), :] = jnp.where(low_lane, even, odd)
    square = jnp.sum(square, axis=0, keepdims=True)
    square_ref[...] = jnp.broadcast_to(square[None], square_ref.shape)


def update_kernel(
    live_ref, square_ref, grad_ref, state_ref, other_state_ref,
    spread_ref, new_master_ref, new_moment_ref, new_variance_ref, clipped_ref, rows_ref,
):
    square = square_ref[0]
    for owner in range(1, square_ref.shape[0]):
        square = square + square_ref[owner]
    square = jnp.sum(square, axis=1, keepdims=True)
    entries = live_ref[HALVES, 0:1, :].astype(jnp.float32) * BLOCK
    clip = jnp.minimum(1.0, 1.0 / jnp.sqrt(square / entries + 1e-06))
    half = lax.axis_index("half")

    def step(grad, state):
        clipped = clip * grad
        master, moment, variance = state
        moment = 0.9 * moment + 0.1 * clipped
        variance = 0.95 * variance + 0.05 * clipped * clipped
        moment_hat = moment / (1.0 - 0.9**20)
        variance_hat = variance / (1.0 - 0.95**20)
        change = moment_hat / (jnp.sqrt(variance_hat) + 1e-08) + 0.1 * master
        return master - 0.02 * change, moment, variance, clipped

    for t in range(TILES):
        lanes = pl.ds(t * LANES, LANES)
        rows = pl.ds(t * SLOTS, SLOTS)
        master, moment, variance, clipped = step(
            grad_ref[half, rows, :], [state_ref[k, :, lanes] for k in range(3)]
        )
        clipped_ref[:, lanes] = clipped
        new_moment_ref[:, lanes] = moment
        new_variance_ref[:, lanes] = variance
        new_master_ref[:, lanes] = master
        rows_ref[:, lanes] = step(
            grad_ref[1 - half, rows, :], [other_state_ref[k, :, lanes] for k in range(3)]
        )[0]
    own = new_master_ref[...].astype(jnp.bfloat16)
    other = rows_ref[...].astype(jnp.bfloat16)
    for chip in range(spread_ref.shape[0]):
        spread_ref[chip, half] = own
        spread_ref[chip, 1 - half] = other


def store_kernel(after_ref, *refs):
    half = len(refs) // 2
    for source, target in zip(refs[:half], refs[half:]):
        target[...] = source[...]


def publish_kernel(mine_ref, other_ref, out_hbm, woven_ref, sems):
    rows = CORES * SLOTS
    chips = mine_ref.shape[0]
    parts = sems.shape[0] // HALVES
    step = chips // parts
    core = lax.axis_index("core")

    def weave(first_ref, second_ref):
        copies = []
        for half in range(HALVES):
            for part in range(parts):
                for chip in range(part * step, (part + 1) * step, 2):
                    pieces = []
                    for k in range(2):
                        pieces.append(first_ref[chip + k, half])
                        pieces.append(second_ref[chip + k, half])
                    block = jnp.concatenate(pieces, axis=0)
                    woven_ref[pl.ds((half * chips + chip) * rows, 2 * rows), :] = block
                span = pl.ds((half * chips + part * step) * rows, step * rows)
                copies.append(
                    pltpu.make_async_copy(
                        woven_ref.at[span], out_hbm.at[span], sems.at[len(copies)]
                    )
                )
                copies[-1].start()
        for copy in copies:
            copy.wait()

    @pl.when(core == 0)
    def _():
        weave(mine_ref, other_ref)

    @pl.when(core == 1)
    def _():
        weave(other_ref, mine_ref)


VMEM = pl.BlockSpec(memory_space=pltpu.VMEM)
SMEM = pl.BlockSpec(memory_space=pltpu.SMEM)
ANY = pl.BlockSpec(memory_space=pl.ANY)
PARAMS = pltpu.CompilerParams(vmem_limit_bytes=40 * 1024 * 1024)


def local(hidden, grad_out, block_list, live_block_count, master, moment, variance):
    chips = lax.axis_size(CHIPS)
    tokens = hidden.shape[0]
    swap = [(0, 1), (1, 0)]
    shape = jax.ShapeDtypeStruct(master.shape, jnp.float32)
    kept = pltpu.VMEM(master.shape, jnp.float32)
    blocks = block_list.T
    top_octave = math.log2(CORES * tokens * LARGEST * LARGEST) + 0.05
    per_octave = 32767 / (top_octave - LOW_OCTAVE)
    cost = pl.CostEstimate(
        flops=2 * chips * SLOTS * SIDE * LANES * tokens,
        bytes_accessed=2 * (hidden.size + grad_out.size),
        transcendentals=0,
    )
    terms = pltpu.VMEM((chips, PAIRS * SIDE, LANES), jnp.float32)
    partner_terms, hidden, turned, state = pl.pallas_call(
        partner_terms_kernel,
        out_shape=(
            terms,
            pltpu.VMEM(hidden.shape, hidden.dtype),
            pltpu.VMEM(grad_out.shape[::-1], grad_out.dtype),
            pltpu.VMEM((3,) + master.shape, jnp.float32),
        ),
        in_specs=[ANY] * 6,
        out_specs=(VMEM,) * 4,
        scratch_shapes=[
            pltpu.SMEM(blocks.shape, jnp.int32),
            pltpu.VMEM(grad_out.shape, grad_out.dtype),
            pltpu.SemaphoreType.DMA((4 + GRAD_PARTS + HIDDEN_PARTS,)),
        ],
        compiler_params=PARAMS,
        cost_estimate=cost,
        name="partner_terms",
    )(
        *(
            pltpu.with_memory_space_constraint(x, pltpu.HBM)
            for x in (blocks, hidden, grad_out, master, moment, variance)
        )
    )
    arrived = lax.ppermute(partner_terms, "core", swap)
    own_terms, live_rows, state = pl.pallas_call(
        own_terms_kernel,
        out_shape=(
            terms,
            pltpu.VMEM((HALVES + 1, 8, LANES), jnp.int32),
            pltpu.VMEM((3,) + master.shape, jnp.float32),
        ),
        in_specs=[SMEM, SMEM, VMEM, VMEM, VMEM],
        out_specs=(VMEM,) * 3,
        compiler_params=PARAMS,
        cost_estimate=cost,
        name="own_terms",
    )(blocks, live_block_count, hidden, turned, state)
    other_state = lax.ppermute(state, "half", swap)
    codes = pl.pallas_call(
        functools.partial(code_kernel, per_octave),
        out_shape=pltpu.VMEM((chips, SIDE, LANES), jnp.int32),
        in_specs=[VMEM, VMEM],
        out_specs=VMEM,
        compiler_params=PARAMS,
        name="code_terms",
    )(own_terms, arrived)
    received = lax.cond(
        live_block_count[0] > 0,
        lambda x: lax.all_to_all(x, "chip", split_axis=0, concat_axis=0, tiled=True),
        jnp.zeros_like,
        codes,
    )
    sum_codes = pl.pallas_call(
        functools.partial(half_sum_kernel, per_octave),
        out_shape=pltpu.VMEM((HALVES, SIDE + EXP_ROWS, LANES), jnp.int32),
        in_specs=[ANY, VMEM],
        out_specs=VMEM,
        compiler_params=PARAMS,
        name="sum_half",
    )(other_state, received)
    arrived = lax.ppermute(sum_codes, "half", swap)
    gradient, square = pl.pallas_call(
        sum_kernel,
        out_shape=(
            pltpu.VMEM((HALVES, TILES * SLOTS, LANES), jnp.float32),
            pltpu.VMEM((chips * CORES // HALVES, 1, LANES), jnp.float32),
        ),
        in_specs=[VMEM] * 3,
        out_specs=(VMEM, VMEM),
        scratch_shapes=[pltpu.VMEM((HALVES, PAIRS, LANES, LANES), jnp.float32)],
        compiler_params=PARAMS,
        name="sum_pair",
    )(live_rows, sum_codes, arrived)
    square = lax.all_to_all(square, ("core", "chip"), split_axis=0, concat_axis=0, tiled=True)
    spread, *updated = pl.pallas_call(
        update_kernel,
        out_shape=(
            pltpu.VMEM((chips // HALVES, HALVES) + master.shape, jnp.bfloat16),
            kept,
            kept,
            kept,
            kept,
        ),
        in_specs=[VMEM] * 5,
        out_specs=(VMEM,) * 5,
        scratch_shapes=[pltpu.VMEM(master.shape, jnp.float32)],
        compiler_params=PARAMS,
        name="adamw",
    )(live_rows, square, gradient, state, other_state)
    mine = lax.all_to_all(spread, "chip", split_axis=0, concat_axis=0, tiled=True)
    other = lax.ppermute(mine, "core", swap)
    results = pl.pallas_call(
        store_kernel,
        out_shape=(shape,) * 4,
        in_specs=[ANY] + [VMEM] * 4,
        out_specs=(VMEM,) * 4,
        compiler_params=PARAMS,
        name="store_state",
    )(mine, *updated)
    published = pl.pallas_call(
        publish_kernel,
        out_shape=jax.ShapeDtypeStruct((chips * CORES * SLOTS, BLOCK), jnp.bfloat16),
        in_specs=[VMEM, VMEM],
        out_specs=ANY,
        scratch_shapes=[
            pltpu.VMEM((chips * CORES * SLOTS, BLOCK), jnp.bfloat16),
            pltpu.SemaphoreType.DMA((STORE_PARTS,)),
        ],
        compiler_params=PARAMS,
        name="publish",
    )(mine, other)
    return (*results, published)


def solution(mesh):
    devices = mesh.devices.reshape(HALVES, -1, CORES)
    rows = P(AXES, None)
    return jax.shard_map(
        local,
        mesh=Mesh(devices, AXES),
        in_specs=(rows, rows, P(), P(), rows, rows, rows),
        out_specs=(rows, rows, rows, rows, P()),
        check_vma=False,
    )
```

```python
import functools
import math

import jax
import jax.numpy as jnp
from jax import lax
from jax.experimental import pallas as pl
from jax.experimental.pallas import tpu as pltpu
from jax.sharding import Mesh
from jax.sharding import PartitionSpec as P

SIDE = 64
LANES = 128
SLOTS = 4
PAIRS = SLOTS // 2
BLOCK = SIDE * SIDE
TILES = BLOCK // LANES
LOW_OCTAVE = -36
LARGEST = 6.0
SMALLEST = 1e-30
CODE_BITS = 13
EXP_ROWS = 8
GRAD_PARTS = 4
HIDDEN_PARTS = 8
STORE_PARTS = 4
CORES = 2
HALVES = 2
SWAP = [(0, 1), (1, 0)]
AXES = ("half", "chip", "core")
CHIPS = ("chip", "half")
INV_LN2 = 1.4426950408889634


def block_products(core, blocks_ref, hidden_ref, turned_ref, out_ref):
    low_lane = lax.broadcasted_iota(jnp.int32, (SIDE, LANES), 1) < SIDE

    chips = out_ref.shape[0] // HALVES

    def one_chip(peer, carry):
        owner = ((peer % HALVES) * chips + peer // HALVES) * CORES + core
        for pair in range(PAIRS):
            lefts, rights, rows = [], [], []
            for k in range(2):
                slot = owner * SLOTS + pair * 2 + k
                r = blocks_ref[0, slot]
                c = blocks_ref[1, slot]
                lefts.append(turned_ref[pl.ds(pl.multiple_of(c * SIDE, SIDE), SIDE), :])
                lanes = pl.ds(pl.multiple_of((r // 2) * LANES, LANES), LANES)
                rights.append(hidden_ref[:, lanes])
                rows.append(r)
            product = jnp.dot(
                jnp.concatenate(lefts, axis=0),
                jnp.concatenate(rights, axis=1),
                preferred_element_type=jnp.float32,
            )
            first = pltpu.roll(product[:SIDE, :LANES], (rows[0] % 2) * SIDE, 1)
            second = pltpu.roll(product[SIDE:, LANES:], ((rows[1] + 1) % 2) * SIDE, 1)
            out_ref[peer, pl.ds(pair * SIDE, SIDE), :] = jnp.where(low_lane, first, second)
        return carry

    lax.fori_loop(0, out_ref.shape[0], one_chip, 0, unroll=16)


def load_kernel(
    hidden_hbm, grad_hbm, master_hbm, moment_hbm, variance_hbm,
    hidden_ref, turned_ref, state_ref, grad_ref, sems,
):
    pieces = [(source, state_ref.at[k]) for k, source in enumerate((master_hbm, moment_hbm, variance_hbm))]
    for source, target, parts in (
        (grad_hbm, grad_ref, GRAD_PARTS), (hidden_hbm, hidden_ref, HIDDEN_PARTS)
    ):
        step = source.shape[0] // parts
        for k in range(parts):
            rows = pl.ds(k * step, step)
            pieces.append((source.at[rows], target.at[rows]))
    copies = [
        pltpu.make_async_copy(source, target, sems.at[k])
        for k, (source, target) in enumerate(pieces)
    ]
    for copy in copies:
        copy.start()
    for copy in copies[: 3 + GRAD_PARTS]:
        copy.wait()
    for k in range(grad_ref.shape[1] // LANES):
        turned_ref[pl.ds(k * LANES, LANES), :] = grad_ref[:, pl.ds(k * LANES, LANES)].T
    for copy in copies[3 + GRAD_PARTS :]:
        copy.wait()


def partner_terms_kernel(blocks_ref, hidden_ref, turned_ref, out_ref):
    block_products(1 - lax.axis_index("core"), blocks_ref, hidden_ref, turned_ref, out_ref)


def own_terms_kernel(
    blocks_ref, live_ref, hidden_ref, turned_ref, out_ref, live_rows_ref
):
    block_products(lax.axis_index("core"), blocks_ref, hidden_ref, turned_ref, out_ref)
    total = live_ref[0]
    for owner in range(1, live_ref.shape[0]):
        total = total + live_ref[owner]
    owners = live_ref.shape[0] // HALVES
    me = lax.axis_index(AXES[1:])
    for half in range(HALVES):
        live = live_ref[half * owners + me]
        live_rows_ref[half] = jnp.full((8, LANES), live, jnp.int32)
    live_rows_ref[HALVES] = jnp.full((8, LANES), total, jnp.int32)


def code_kernel(per_octave, own_ref, other_ref, out_ref):
    def encode(value):
        octave = jnp.log(jnp.maximum(jnp.abs(value), 2.0**LOW_OCTAVE)) * INV_LN2
        code = (octave - LOW_OCTAVE) * per_octave
        return jnp.round(jnp.where(value < 0, -code, code)).astype(jnp.int32)

    def one_chip(chip, carry):
        code = []
        for pair in range(PAIRS):
            rows = pl.ds(pair * SIDE, SIDE)
            code.append(encode(own_ref[chip, rows, :] + other_ref[chip, rows, :]))
        out_ref[chip] = (code[0] << 16) | (code[1] & 0xFFFF)
        return carry

    lax.fori_loop(0, out_ref.shape[0], one_chip, 0, unroll=2)


def half_sum_kernel(per_octave, after_ref, recv_ref, code_ref):
    def decode(code):
        value = code.astype(jnp.float32)
        size = jnp.exp2(jnp.abs(value) * (1.0 / per_octave) + LOW_OCTAVE)
        return jnp.where(code > 0, size, jnp.where(code < 0, -size, 0.0))

    def add(offset, d, totals):
        word = recv_ref[d * HALVES + offset]
        return totals[0] + decode(word >> 16), totals[1] + decode((word << 16) >> 16)

    zero = jnp.zeros((SIDE, LANES), jnp.float32)
    chips = recv_ref.shape[0] // HALVES
    for offset in range(HALVES):
        totals = lax.fori_loop(
            0, chips, functools.partial(add, offset), (zero, zero), unroll=4
        )
        peak = jnp.max(jnp.maximum(*map(jnp.abs, totals)), axis=0, keepdims=True)
        exponent = jnp.floor(jnp.log(jnp.maximum(peak, SMALLEST)) * INV_LN2)
        scale = jnp.exp2(CODE_BITS - exponent)
        high, low = (jnp.round(total * scale).astype(jnp.int32) for total in totals)
        code_ref[offset, pl.ds(0, SIDE), :] = (high << 16) | (low & 0xFFFF)
        code_ref[offset, pl.ds(SIDE, EXP_ROWS), :] = jnp.broadcast_to(
            exponent.astype(jnp.int32), (EXP_ROWS, LANES)
        )


def sum_kernel(live_ref, own_ref, arrived_ref, grad_ref, square_ref, turned_ref):
    slot = lax.broadcasted_iota(jnp.int32, (SIDE, LANES), 1) // SIDE
    low_lane = lax.broadcasted_iota(jnp.int32, (TILES, LANES), 1) < SIDE

    def decode(code_ref, half):
        word = code_ref[half, pl.ds(0, SIDE), :]
        exponent = code_ref[half, pl.ds(SIDE, EXP_ROWS), :][:1].astype(jnp.float32)
        scale = jnp.exp2(exponent - CODE_BITS)
        return [code.astype(jnp.float32) * scale for code in (word >> 16, (word << 16) >> 16)]

    square = jnp.zeros((SIDE, LANES), jnp.float32)
    for half in range(HALVES):
        live = live_ref[half, 0:1, :]
        own, arrived = decode(own_ref, half), decode(arrived_ref, half)
        for pair in range(PAIRS):
            total = jnp.where(slot + pair * 2 < live, own[pair] + arrived[pair], 0.0)
            square = square + total * total
            turned = total.T
            turned_ref[half, pair] = jnp.concatenate([turned, turned], axis=1)
        for s in range(SLOTS):
            base = (s % 2) * SIDE
            even = turned_ref[half, s // 2, pl.ds(base, TILES, stride=2), :]
            odd = turned_ref[half, s // 2, pl.ds(base + 1, TILES, stride=2), :]
            grad_ref[half, pl.ds(s, TILES, stride=SLOTS), :] = jnp.where(low_lane, even, odd)
    square = jnp.sum(square, axis=0, keepdims=True)
    square_ref[...] = jnp.broadcast_to(square[None], square_ref.shape)


def update_kernel(
    live_ref, square_ref, grad_ref, state_ref, other_state_ref,
    spread_ref, new_master_ref, new_moment_ref, new_variance_ref, clipped_ref, rows_ref,
):
    square = square_ref[0]
    for owner in range(1, square_ref.shape[0]):
        square = square + square_ref[owner]
    square = jnp.sum(square, axis=1, keepdims=True)
    entries = live_ref[HALVES, 0:1, :].astype(jnp.float32) * BLOCK
    clip = jnp.minimum(1.0, 1.0 / jnp.sqrt(square / entries + 1e-06))
    half = lax.axis_index("half")

    def step(grad, state):
        clipped = clip * grad
        master, moment, variance = state
        moment = 0.9 * moment + 0.1 * clipped
        variance = 0.95 * variance + 0.05 * clipped * clipped
        moment_hat = moment / (1.0 - 0.9**20)
        variance_hat = variance / (1.0 - 0.95**20)
        change = moment_hat / (jnp.sqrt(variance_hat) + 1e-08) + 0.1 * master
        return master - 0.02 * change, moment, variance, clipped

    for t in range(TILES):
        lanes = pl.ds(t * LANES, LANES)
        rows = pl.ds(t * SLOTS, SLOTS)
        master, moment, variance, clipped = step(
            grad_ref[half, rows, :], [state_ref[k, :, lanes] for k in range(3)]
        )
        clipped_ref[:, lanes] = clipped
        new_moment_ref[:, lanes] = moment
        new_variance_ref[:, lanes] = variance
        new_master_ref[:, lanes] = master
        rows_ref[:, lanes] = step(
            grad_ref[1 - half, rows, :], [other_state_ref[k, :, lanes] for k in range(3)]
        )[0]
    own = new_master_ref[...].astype(jnp.bfloat16)
    other = rows_ref[...].astype(jnp.bfloat16)
    for chip in range(spread_ref.shape[0]):
        spread_ref[chip, half] = own
        spread_ref[chip, 1 - half] = other


def store_kernel(after_ref, *refs):
    half = len(refs) // 2
    for source, target in zip(refs[:half], refs[half:]):
        target[...] = source[...]


def publish_kernel(mine_ref, other_ref, out_hbm, woven_ref, sems):
    rows = CORES * SLOTS
    chips = mine_ref.shape[0]
    parts = sems.shape[0] // HALVES
    step = chips // parts
    core = lax.axis_index("core")

    def weave(first_ref, second_ref):
        copies = []
        for half in range(HALVES):
            for part in range(parts):
                for chip in range(part * step, (part + 1) * step, 2):
                    pieces = []
                    for k in range(2):
                        pieces.append(first_ref[chip + k, half])
                        pieces.append(second_ref[chip + k, half])
                    block = jnp.concatenate(pieces, axis=0)
                    woven_ref[pl.ds((half * chips + chip) * rows, 2 * rows), :] = block
                span = pl.ds((half * chips + part * step) * rows, step * rows)
                copies.append(
                    pltpu.make_async_copy(
                        woven_ref.at[span], out_hbm.at[span], sems.at[len(copies)]
                    )
                )
                copies[-1].start()
        for copy in copies:
            copy.wait()

    @pl.when(core == 0)
    def _():
        weave(mine_ref, other_ref)

    @pl.when(core == 1)
    def _():
        weave(other_ref, mine_ref)


VMEM = pl.BlockSpec(memory_space=pltpu.VMEM)
SMEM = pl.BlockSpec(memory_space=pltpu.SMEM)
ANY = pl.BlockSpec(memory_space=pl.ANY)
PARAMS = pltpu.CompilerParams(vmem_limit_bytes=40 * 1024 * 1024)


def exchange_terms(hidden, turned, blocks, live_block_count):
    chips = lax.axis_size(CHIPS)
    tokens = hidden.shape[0]
    top_octave = math.log2(CORES * tokens * LARGEST * LARGEST) + 0.05
    per_octave = 32767 / (top_octave - LOW_OCTAVE)
    cost = pl.CostEstimate(
        flops=2 * chips * SLOTS * SIDE * LANES * tokens,
        bytes_accessed=2 * (hidden.size + turned.size),
        transcendentals=0,
    )
    terms = pltpu.VMEM((chips, PAIRS * SIDE, LANES), jnp.float32)
    partner_terms = pl.pallas_call(
        partner_terms_kernel,
        out_shape=terms,
        in_specs=[SMEM, VMEM, VMEM],
        out_specs=VMEM,
        compiler_params=PARAMS,
        cost_estimate=cost,
        name="partner_terms",
    )(blocks, hidden, turned)
    arrived = lax.ppermute(partner_terms, "core", SWAP)
    own_terms, live_rows = pl.pallas_call(
        own_terms_kernel,
        out_shape=(terms, pltpu.VMEM((HALVES + 1, 8, LANES), jnp.int32)),
        in_specs=[SMEM, SMEM, VMEM, VMEM],
        out_specs=(VMEM, VMEM),
        compiler_params=PARAMS,
        cost_estimate=cost,
        name="own_terms",
    )(blocks, live_block_count, hidden, turned)
    codes = pl.pallas_call(
        functools.partial(code_kernel, per_octave),
        out_shape=pltpu.VMEM((chips, SIDE, LANES), jnp.int32),
        in_specs=[VMEM, VMEM],
        out_specs=VMEM,
        compiler_params=PARAMS,
        name="code_terms",
    )(own_terms, arrived)
    return lax.all_to_all(codes, "chip", split_axis=0, concat_axis=0, tiled=True), live_rows


def no_terms(hidden, turned, blocks, live_block_count):
    chips = lax.axis_size(CHIPS)
    return (
        jnp.zeros((chips, SIDE, LANES), jnp.int32),
        jnp.zeros((HALVES + 1, 8, LANES), jnp.int32),
    )


def local(hidden, grad_out, block_list, live_block_count, master, moment, variance):
    chips = lax.axis_size(CHIPS)
    shape = jax.ShapeDtypeStruct(master.shape, jnp.float32)
    kept = pltpu.VMEM(master.shape, jnp.float32)
    top_octave = math.log2(CORES * hidden.shape[0] * LARGEST * LARGEST) + 0.05
    per_octave = 32767 / (top_octave - LOW_OCTAVE)
    hidden, turned, state = pl.pallas_call(
        load_kernel,
        out_shape=(
            pltpu.VMEM(hidden.shape, hidden.dtype),
            pltpu.VMEM(grad_out.shape[::-1], grad_out.dtype),
            pltpu.VMEM((3,) + master.shape, jnp.float32),
        ),
        in_specs=[ANY] * 5,
        out_specs=(VMEM,) * 3,
        scratch_shapes=[
            pltpu.VMEM(grad_out.shape, grad_out.dtype),
            pltpu.SemaphoreType.DMA((3 + GRAD_PARTS + HIDDEN_PARTS,)),
        ],
        compiler_params=PARAMS,
        name="load_inputs",
    )(
        *(
            pltpu.with_memory_space_constraint(x, pltpu.HBM)
            for x in (hidden, grad_out, master, moment, variance)
        )
    )
    other_state = lax.ppermute(state, "half", SWAP)
    received, live_rows = lax.cond(
        live_block_count[0] > 0,
        exchange_terms,
        no_terms,
        hidden,
        turned,
        block_list.T,
        live_block_count,
    )
    sum_codes = pl.pallas_call(
        functools.partial(half_sum_kernel, per_octave),
        out_shape=pltpu.VMEM((HALVES, SIDE + EXP_ROWS, LANES), jnp.int32),
        in_specs=[ANY, VMEM],
        out_specs=VMEM,
        compiler_params=PARAMS,
        name="sum_half",
    )(other_state, received)
    arrived = lax.ppermute(sum_codes, "half", SWAP)
    gradient, square = pl.pallas_call(
        sum_kernel,
        out_shape=(
            pltpu.VMEM((HALVES, TILES * SLOTS, LANES), jnp.float32),
            pltpu.VMEM((chips * CORES // HALVES, 1, LANES), jnp.float32),
        ),
        in_specs=[VMEM] * 3,
        out_specs=(VMEM, VMEM),
        scratch_shapes=[pltpu.VMEM((HALVES, PAIRS, LANES, LANES), jnp.float32)],
        compiler_params=PARAMS,
        name="sum_pair",
    )(live_rows, sum_codes, arrived)
    square = lax.all_to_all(square, ("core", "chip"), split_axis=0, concat_axis=0, tiled=True)
    spread, *updated = pl.pallas_call(
        update_kernel,
        out_shape=(
            pltpu.VMEM((chips // HALVES, HALVES) + master.shape, jnp.bfloat16),
            kept,
            kept,
            kept,
            kept,
        ),
        in_specs=[VMEM] * 5,
        out_specs=(VMEM,) * 5,
        scratch_shapes=[pltpu.VMEM(master.shape, jnp.float32)],
        compiler_params=PARAMS,
        name="adamw",
    )(live_rows, square, gradient, state, other_state)
    mine = lax.all_to_all(spread, "chip", split_axis=0, concat_axis=0, tiled=True)
    other = lax.ppermute(mine, "core", SWAP)
    results = pl.pallas_call(
        store_kernel,
        out_shape=(shape,) * 4,
        in_specs=[ANY] + [VMEM] * 4,
        out_specs=(VMEM,) * 4,
        compiler_params=PARAMS,
        name="store_state",
    )(mine, *updated)
    published = pl.pallas_call(
        publish_kernel,
        out_shape=jax.ShapeDtypeStruct((chips * CORES * SLOTS, BLOCK), jnp.bfloat16),
        in_specs=[VMEM, VMEM],
        out_specs=ANY,
        scratch_shapes=[
            pltpu.VMEM((chips * CORES * SLOTS, BLOCK), jnp.bfloat16),
            pltpu.SemaphoreType.DMA((STORE_PARTS,)),
        ],
        compiler_params=PARAMS,
        name="publish",
    )(mine, other)
    return (*results, published)


def solution(mesh):
    devices = mesh.devices.reshape(HALVES, -1, CORES)
    rows = P(AXES, None)
    return jax.shard_map(
        local,
        mesh=Mesh(devices, AXES),
        in_specs=(rows, rows, P(), P(), rows, rows, rows),
        out_specs=(rows, rows, rows, rows, P()),
        check_vma=False,
    )
```

```python
import functools
import math

import jax
import jax.numpy as jnp
from jax import lax
from jax.experimental import pallas as pl
from jax.experimental.pallas import tpu as pltpu
from jax.sharding import Mesh
from jax.sharding import PartitionSpec as P

SIDE = 64
LANES = 128
SLOTS = 4
PAIRS = SLOTS // 2
BLOCK = SIDE * SIDE
TILES = BLOCK // LANES
LOW_OCTAVE = -36
LARGEST = 6.0
SMALLEST = 1e-30
CODE_BITS = 13
EXP_ROWS = 8
GRAD_PARTS = 2
HIDDEN_PARTS = 4
STORE_PARTS = 4
CORES = 2
HALVES = 2
AXES = ("half", "chip", "core")
CHIPS = ("chip", "half")
INV_LN2 = 1.4426950408889634


def block_products(core, blocks_ref, hidden_ref, turned_ref, out_ref):
    low_lane = lax.broadcasted_iota(jnp.int32, (SIDE, LANES), 1) < SIDE

    chips = out_ref.shape[0] // HALVES

    def one_chip(peer, carry):
        owner = ((peer % HALVES) * chips + peer // HALVES) * CORES + core
        for pair in range(PAIRS):
            lefts, rights, rows = [], [], []
            for k in range(2):
                slot = owner * SLOTS + pair * 2 + k
                r = blocks_ref[0, slot]
                c = blocks_ref[1, slot]
                lefts.append(turned_ref[pl.ds(pl.multiple_of(c * SIDE, SIDE), SIDE), :])
                lanes = pl.ds(pl.multiple_of((r // 2) * LANES, LANES), LANES)
                rights.append(hidden_ref[:, lanes])
                rows.append(r)
            product = jnp.dot(
                jnp.concatenate(lefts, axis=0),
                jnp.concatenate(rights, axis=1),
                preferred_element_type=jnp.float32,
            )
            first = pltpu.roll(product[:SIDE, :LANES], (rows[0] % 2) * SIDE, 1)
            second = pltpu.roll(product[SIDE:, LANES:], ((rows[1] + 1) % 2) * SIDE, 1)
            out_ref[peer, pl.ds(pair * SIDE, SIDE), :] = jnp.where(low_lane, first, second)
        return carry

    lax.fori_loop(0, out_ref.shape[0], one_chip, 0, unroll=16)


def partner_terms_kernel(
    blocks_hbm, hidden_hbm, grad_hbm, master_hbm, moment_hbm, variance_hbm,
    out_ref, hidden_ref, turned_ref, state_ref, blocks_ref, grad_ref, sems,
):
    copies = [pltpu.make_async_copy(blocks_hbm, blocks_ref, sems.at[0])]
    for source, target, parts in ((grad_hbm, grad_ref, GRAD_PARTS), (hidden_hbm, hidden_ref, HIDDEN_PARTS)):
        step = source.shape[0] // parts
        for k in range(parts):
            rows = pl.ds(k * step, step)
            copies.append(
                pltpu.make_async_copy(source.at[rows], target.at[rows], sems.at[len(copies)])
            )
    for k, source in enumerate((master_hbm, moment_hbm, variance_hbm)):
        copies.append(pltpu.make_async_copy(source, state_ref.at[k], sems.at[len(copies)]))
    for copy in copies:
        copy.start()
    grad_end = 1 + GRAD_PARTS
    hidden_end = grad_end + HIDDEN_PARTS
    for copy in copies[:grad_end]:
        copy.wait()
    for k in range(grad_ref.shape[1] // LANES):
        turned_ref[pl.ds(k * LANES, LANES), :] = grad_ref[:, pl.ds(k * LANES, LANES)].T
    for copy in copies[grad_end:hidden_end]:
        copy.wait()
    block_products(1 - lax.axis_index("core"), blocks_ref, hidden_ref, turned_ref, out_ref)
    for copy in copies[hidden_end:]:
        copy.wait()


def own_terms_kernel(
    blocks_ref, live_ref, hidden_ref, turned_ref, out_ref, live_rows_ref
):
    block_products(lax.axis_index("core"), blocks_ref, hidden_ref, turned_ref, out_ref)
    total = live_ref[0]
    for owner in range(1, live_ref.shape[0]):
        total = total + live_ref[owner]
    owners = live_ref.shape[0] // HALVES
    me = lax.axis_index(AXES[1:])
    for half in range(HALVES):
        live = live_ref[half * owners + me]
        live_rows_ref[half] = jnp.full((8, LANES), live, jnp.int32)
    live_rows_ref[HALVES] = jnp.full((8, LANES), total, jnp.int32)


def code_kernel(per_octave, own_ref, other_ref, out_ref):
    def encode(value):
        octave = jnp.log(jnp.maximum(jnp.abs(value), 2.0**LOW_OCTAVE)) * INV_LN2
        code = (octave - LOW_OCTAVE) * per_octave
        return jnp.round(jnp.where(value < 0, -code, code)).astype(jnp.int32)

    def one_chip(chip, carry):
        code = []
        for pair in range(PAIRS):
            rows = pl.ds(pair * SIDE, SIDE)
            code.append(encode(own_ref[chip, rows, :] + other_ref[chip, rows, :]))
        out_ref[chip] = (code[0] << 16) | (code[1] & 0xFFFF)
        return carry

    lax.fori_loop(0, out_ref.shape[0], one_chip, 0, unroll=4)


def half_sum_kernel(per_octave, after_ref, recv_ref, code_ref):
    def decode(code):
        value = code.astype(jnp.float32)
        size = jnp.exp2(jnp.abs(value) * (1.0 / per_octave) + LOW_OCTAVE)
        return jnp.where(code > 0, size, jnp.where(code < 0, -size, 0.0))

    def add(offset, d, totals):
        word = recv_ref[d * HALVES + offset]
        return totals[0] + decode(word >> 16), totals[1] + decode((word << 16) >> 16)

    zero = jnp.zeros((SIDE, LANES), jnp.float32)
    chips = recv_ref.shape[0] // HALVES
    for offset in range(HALVES):
        totals = lax.fori_loop(
            0, chips, functools.partial(add, offset), (zero, zero), unroll=8
        )
        peak = jnp.max(jnp.maximum(*map(jnp.abs, totals)), axis=0, keepdims=True)
        exponent = jnp.floor(jnp.log(jnp.maximum(peak, SMALLEST)) * INV_LN2)
        scale = jnp.exp2(CODE_BITS - exponent)
        high, low = (jnp.round(total * scale).astype(jnp.int32) for total in totals)
        code_ref[offset, pl.ds(0, SIDE), :] = (high << 16) | (low & 0xFFFF)
        code_ref[offset, pl.ds(SIDE, EXP_ROWS), :] = jnp.broadcast_to(
            exponent.astype(jnp.int32), (EXP_ROWS, LANES)
        )


def sum_kernel(live_ref, own_ref, arrived_ref, grad_ref, square_ref, turned_ref):
    slot = lax.broadcasted_iota(jnp.int32, (SIDE, LANES), 1) // SIDE
    low_lane = lax.broadcasted_iota(jnp.int32, (TILES, LANES), 1) < SIDE

    def decode(code_ref, half):
        word = code_ref[half, pl.ds(0, SIDE), :]
        exponent = code_ref[half, pl.ds(SIDE, EXP_ROWS), :][:1].astype(jnp.float32)
        scale = jnp.exp2(exponent - CODE_BITS)
        return [code.astype(jnp.float32) * scale for code in (word >> 16, (word << 16) >> 16)]

    square = jnp.zeros((SIDE, LANES), jnp.float32)
    for half in range(HALVES):
        live = live_ref[half, 0:1, :]
        own, arrived = decode(own_ref, half), decode(arrived_ref, half)
        for pair in range(PAIRS):
            total = jnp.where(slot + pair * 2 < live, own[pair] + arrived[pair], 0.0)
            square = square + total * total
            turned = total.T
            turned_ref[half, pair] = jnp.concatenate([turned, turned], axis=1)
        for s in range(SLOTS):
            base = (s % 2) * SIDE
            even = turned_ref[half, s // 2, pl.ds(base, TILES, stride=2), :]
            odd = turned_ref[half, s // 2, pl.ds(base + 1, TILES, stride=2), :]
            grad_ref[half, pl.ds(s, TILES, stride=SLOTS), :] = jnp.where(low_lane, even, odd)
    square = jnp.sum(square, axis=0, keepdims=True)
    square_ref[...] = jnp.broadcast_to(square[None], square_ref.shape)


def update_kernel(
    live_ref, square_ref, grad_ref, state_ref, other_state_ref,
    spread_ref, new_master_ref, new_moment_ref, new_variance_ref, clipped_ref, rows_ref,
):
    square = square_ref[0]
    for owner in range(1, square_ref.shape[0]):
        square = square + square_ref[owner]
    square = jnp.sum(square, axis=1, keepdims=True)
    entries = live_ref[HALVES, 0:1, :].astype(jnp.float32) * BLOCK
    clip = jnp.minimum(1.0, 1.0 / jnp.sqrt(square / entries + 1e-06))
    half = lax.axis_index("half")

    def step(grad, state):
        clipped = clip * grad
        master, moment, variance = state
        moment = 0.9 * moment + 0.1 * clipped
        variance = 0.95 * variance + 0.05 * clipped * clipped
        moment_hat = moment / (1.0 - 0.9**20)
        variance_hat = variance / (1.0 - 0.95**20)
        change = moment_hat / (jnp.sqrt(variance_hat) + 1e-08) + 0.1 * master
        return master - 0.02 * change, moment, variance, clipped

    for t in range(TILES):
        lanes = pl.ds(t * LANES, LANES)
        rows = pl.ds(t * SLOTS, SLOTS)
        master, moment, variance, clipped = step(
            grad_ref[half, rows, :], [state_ref[k, :, lanes] for k in range(3)]
        )
        clipped_ref[:, lanes] = clipped
        new_moment_ref[:, lanes] = moment
        new_variance_ref[:, lanes] = variance
        new_master_ref[:, lanes] = master
        rows_ref[:, lanes] = step(
            grad_ref[1 - half, rows, :], [other_state_ref[k, :, lanes] for k in range(3)]
        )[0]
    own = new_master_ref[...].astype(jnp.bfloat16)
    other = rows_ref[...].astype(jnp.bfloat16)
    for chip in range(spread_ref.shape[0]):
        spread_ref[chip, half] = own
        spread_ref[chip, 1 - half] = other


def store_kernel(after_ref, *refs):
    half = len(refs) // 2
    for source, target in zip(refs[:half], refs[half:]):
        target[...] = source[...]


def publish_kernel(mine_ref, other_ref, out_hbm, woven_ref, sems):
    rows = CORES * SLOTS
    chips = mine_ref.shape[0]
    parts = sems.shape[0] // HALVES
    step = chips // parts
    core = lax.axis_index("core")

    def weave(first_ref, second_ref):
        copies = []
        for half in range(HALVES):
            for part in range(parts):
                for chip in range(part * step, (part + 1) * step, 2):
                    pieces = []
                    for k in range(2):
                        pieces.append(first_ref[chip + k, half])
                        pieces.append(second_ref[chip + k, half])
                    block = jnp.concatenate(pieces, axis=0)
                    woven_ref[pl.ds((half * chips + chip) * rows, 2 * rows), :] = block
                span = pl.ds((half * chips + part * step) * rows, step * rows)
                copies.append(
                    pltpu.make_async_copy(
                        woven_ref.at[span], out_hbm.at[span], sems.at[len(copies)]
                    )
                )
                copies[-1].start()
        for copy in copies:
            copy.wait()

    @pl.when(core == 0)
    def _():
        weave(mine_ref, other_ref)

    @pl.when(core == 1)
    def _():
        weave(other_ref, mine_ref)


VMEM = pl.BlockSpec(memory_space=pltpu.VMEM)
SMEM = pl.BlockSpec(memory_space=pltpu.SMEM)
ANY = pl.BlockSpec(memory_space=pl.ANY)
PARAMS = pltpu.CompilerParams(vmem_limit_bytes=40 * 1024 * 1024)


def local(hidden, grad_out, block_list, live_block_count, master, moment, variance):
    chips = lax.axis_size(CHIPS)
    tokens = hidden.shape[0]
    swap = [(0, 1), (1, 0)]
    shape = jax.ShapeDtypeStruct(master.shape, jnp.float32)
    kept = pltpu.VMEM(master.shape, jnp.float32)
    blocks = block_list.T
    top_octave = math.log2(CORES * tokens * LARGEST * LARGEST) + 0.05
    per_octave = 32767 / (top_octave - LOW_OCTAVE)
    cost = pl.CostEstimate(
        flops=2 * chips * SLOTS * SIDE * LANES * tokens,
        bytes_accessed=2 * (hidden.size + grad_out.size),
        transcendentals=0,
    )
    terms = pltpu.VMEM((chips, PAIRS * SIDE, LANES), jnp.float32)
    partner_terms, hidden, turned, state = pl.pallas_call(
        partner_terms_kernel,
        out_shape=(
            terms,
            pltpu.VMEM(hidden.shape, hidden.dtype),
            pltpu.VMEM(grad_out.shape[::-1], grad_out.dtype),
            pltpu.VMEM((3,) + master.shape, jnp.float32),
        ),
        in_specs=[ANY] * 6,
        out_specs=(VMEM,) * 4,
        scratch_shapes=[
            pltpu.SMEM(blocks.shape, jnp.int32),
            pltpu.VMEM(grad_out.shape, grad_out.dtype),
            pltpu.SemaphoreType.DMA((4 + GRAD_PARTS + HIDDEN_PARTS,)),
        ],
        compiler_params=PARAMS,
        cost_estimate=cost,
        name="partner_terms",
    )(
        *(
            pltpu.with_memory_space_constraint(x, pltpu.HBM)
            for x in (blocks, hidden, grad_out, master, moment, variance)
        )
    )
    arrived = lax.ppermute(partner_terms, "core", swap)
    other_state = lax.ppermute(state, "half", swap)
    own_terms, live_rows = pl.pallas_call(
        own_terms_kernel,
        out_shape=(terms, pltpu.VMEM((HALVES + 1, 8, LANES), jnp.int32)),
        in_specs=[SMEM, SMEM, VMEM, VMEM],
        out_specs=(VMEM, VMEM),
        compiler_params=PARAMS,
        cost_estimate=cost,
        name="own_terms",
    )(blocks, live_block_count, hidden, turned)
    codes = pl.pallas_call(
        functools.partial(code_kernel, per_octave),
        out_shape=pltpu.VMEM((chips, SIDE, LANES), jnp.int32),
        in_specs=[VMEM, VMEM],
        out_specs=VMEM,
        compiler_params=PARAMS,
        name="code_terms",
    )(own_terms, arrived)
    received = lax.cond(
        live_block_count[0] > 0,
        lambda x: lax.all_to_all(x, "chip", split_axis=0, concat_axis=0, tiled=True),
        jnp.zeros_like,
        codes,
    )
    sum_codes = pl.pallas_call(
        functools.partial(half_sum_kernel, per_octave),
        out_shape=pltpu.VMEM((HALVES, SIDE + EXP_ROWS, LANES), jnp.int32),
        in_specs=[ANY, VMEM],
        out_specs=VMEM,
        compiler_params=PARAMS,
        name="sum_half",
    )(other_state, received)
    arrived = lax.ppermute(sum_codes, "half", swap)
    gradient, square = pl.pallas_call(
        sum_kernel,
        out_shape=(
            pltpu.VMEM((HALVES, TILES * SLOTS, LANES), jnp.float32),
            pltpu.VMEM((chips * CORES // HALVES, 1, LANES), jnp.float32),
        ),
        in_specs=[VMEM] * 3,
        out_specs=(VMEM, VMEM),
        scratch_shapes=[pltpu.VMEM((HALVES, PAIRS, LANES, LANES), jnp.float32)],
        compiler_params=PARAMS,
        name="sum_pair",
    )(live_rows, sum_codes, arrived)
    square = lax.all_to_all(square, ("core", "chip"), split_axis=0, concat_axis=0, tiled=True)
    spread, *updated = pl.pallas_call(
        update_kernel,
        out_shape=(
            pltpu.VMEM((chips // HALVES, HALVES) + master.shape, jnp.bfloat16),
            kept,
            kept,
            kept,
            kept,
        ),
        in_specs=[VMEM] * 5,
        out_specs=(VMEM,) * 5,
        scratch_shapes=[pltpu.VMEM(master.shape, jnp.float32)],
        compiler_params=PARAMS,
        name="adamw",
    )(live_rows, square, gradient, state, other_state)
    mine = lax.all_to_all(spread, "chip", split_axis=0, concat_axis=0, tiled=True)
    other = lax.ppermute(mine, "core", swap)
    results = pl.pallas_call(
        store_kernel,
        out_shape=(shape,) * 4,
        in_specs=[ANY] + [VMEM] * 4,
        out_specs=(VMEM,) * 4,
        compiler_params=PARAMS,
        name="store_state",
    )(mine, *updated)
    published = pl.pallas_call(
        publish_kernel,
        out_shape=jax.ShapeDtypeStruct((chips * CORES * SLOTS, BLOCK), jnp.bfloat16),
        in_specs=[VMEM, VMEM],
        out_specs=ANY,
        scratch_shapes=[
            pltpu.VMEM((chips * CORES * SLOTS, BLOCK), jnp.bfloat16),
            pltpu.SemaphoreType.DMA((STORE_PARTS,)),
        ],
        compiler_params=PARAMS,
        name="publish",
    )(mine, other)
    return (*results, published)


def solution(mesh):
    devices = mesh.devices.reshape(HALVES, -1, CORES)
    rows = P(AXES, None)
    return jax.shard_map(
        local,
        mesh=Mesh(devices, AXES),
        in_specs=(rows, rows, P(), P(), rows, rows, rows),
        out_specs=(rows, rows, rows, rows, P()),
        check_vma=False,
    )
```

```python
import functools
import math

import jax
import jax.numpy as jnp
from jax import lax
from jax.experimental import pallas as pl
from jax.experimental.pallas import tpu as pltpu
from jax.sharding import Mesh
from jax.sharding import PartitionSpec as P

SIDE = 64
LANES = 128
SLOTS = 4
PAIRS = SLOTS // 2
BLOCK = SIDE * SIDE
TILES = BLOCK // LANES
LOW_OCTAVE = -36
LARGEST = 6.0
SMALLEST = 1e-30
CODE_BITS = 13
EXP_ROWS = 8
GRAD_PARTS = 2
HIDDEN_PARTS = 4
STORE_PARTS = 4
CORES = 2
HALVES = 2
SWAP = [(0, 1), (1, 0)]
AXES = ("half", "chip", "core")
CHIPS = ("chip", "half")
INV_LN2 = 1.4426950408889634


def block_products(core, blocks_ref, hidden_ref, turned_ref, out_ref):
    low_lane = lax.broadcasted_iota(jnp.int32, (SIDE, LANES), 1) < SIDE

    chips = out_ref.shape[0] // HALVES

    def one_chip(peer, carry):
        owner = ((peer % HALVES) * chips + peer // HALVES) * CORES + core
        for pair in range(PAIRS):
            lefts, rights, rows = [], [], []
            for k in range(2):
                slot = owner * SLOTS + pair * 2 + k
                r = blocks_ref[0, slot]
                c = blocks_ref[1, slot]
                lefts.append(turned_ref[pl.ds(pl.multiple_of(c * SIDE, SIDE), SIDE), :])
                lanes = pl.ds(pl.multiple_of((r // 2) * LANES, LANES), LANES)
                rights.append(hidden_ref[:, lanes])
                rows.append(r)
            product = jnp.dot(
                jnp.concatenate(lefts, axis=0),
                jnp.concatenate(rights, axis=1),
                preferred_element_type=jnp.float32,
            )
            first = pltpu.roll(product[:SIDE, :LANES], (rows[0] % 2) * SIDE, 1)
            second = pltpu.roll(product[SIDE:, LANES:], ((rows[1] + 1) % 2) * SIDE, 1)
            out_ref[peer, pl.ds(pair * SIDE, SIDE), :] = jnp.where(low_lane, first, second)
        return carry

    lax.fori_loop(0, out_ref.shape[0], one_chip, 0, unroll=16)


def gather_kernel(master_hbm, moment_hbm, variance_hbm, state_ref, sems):
    copies = [
        pltpu.make_async_copy(source, state_ref.at[k], sems.at[k])
        for k, source in enumerate((master_hbm, moment_hbm, variance_hbm))
    ]
    for copy in copies:
        copy.start()
    for copy in copies:
        copy.wait()


def partner_terms_kernel(
    blocks_hbm, hidden_hbm, grad_hbm, out_ref, hidden_ref, turned_ref, blocks_ref, grad_ref, sems
):
    copies = [pltpu.make_async_copy(blocks_hbm, blocks_ref, sems.at[0])]
    for source, target, parts in ((grad_hbm, grad_ref, GRAD_PARTS), (hidden_hbm, hidden_ref, HIDDEN_PARTS)):
        step = source.shape[0] // parts
        for k in range(parts):
            rows = pl.ds(k * step, step)
            copies.append(
                pltpu.make_async_copy(source.at[rows], target.at[rows], sems.at[len(copies)])
            )
    for copy in copies:
        copy.start()
    grad_end = 1 + GRAD_PARTS
    for copy in copies[:grad_end]:
        copy.wait()
    for k in range(grad_ref.shape[1] // LANES):
        turned_ref[pl.ds(k * LANES, LANES), :] = grad_ref[:, pl.ds(k * LANES, LANES)].T
    for copy in copies[grad_end:]:
        copy.wait()
    block_products(1 - lax.axis_index("core"), blocks_ref, hidden_ref, turned_ref, out_ref)


def own_terms_kernel(
    blocks_ref, live_ref, hidden_ref, turned_ref, out_ref, live_rows_ref
):
    block_products(lax.axis_index("core"), blocks_ref, hidden_ref, turned_ref, out_ref)
    total = live_ref[0]
    for owner in range(1, live_ref.shape[0]):
        total = total + live_ref[owner]
    owners = live_ref.shape[0] // HALVES
    me = lax.axis_index(AXES[1:])
    for half in range(HALVES):
        live = live_ref[half * owners + me]
        live_rows_ref[half] = jnp.full((8, LANES), live, jnp.int32)
    live_rows_ref[HALVES] = jnp.full((8, LANES), total, jnp.int32)


def code_kernel(per_octave, own_ref, other_ref, out_ref):
    def encode(value):
        octave = jnp.log(jnp.maximum(jnp.abs(value), 2.0**LOW_OCTAVE)) * INV_LN2
        code = (octave - LOW_OCTAVE) * per_octave
        return jnp.round(jnp.where(value < 0, -code, code)).astype(jnp.int32)

    def one_chip(chip, carry):
        code = []
        for pair in range(PAIRS):
            rows = pl.ds(pair * SIDE, SIDE)
            code.append(encode(own_ref[chip, rows, :] + other_ref[chip, rows, :]))
        out_ref[chip] = (code[0] << 16) | (code[1] & 0xFFFF)
        return carry

    lax.fori_loop(0, out_ref.shape[0], one_chip, 0, unroll=4)


def half_sum_kernel(per_octave, after_ref, recv_ref, code_ref):
    def decode(code):
        value = code.astype(jnp.float32)
        size = jnp.exp2(jnp.abs(value) * (1.0 / per_octave) + LOW_OCTAVE)
        return jnp.where(code > 0, size, jnp.where(code < 0, -size, 0.0))

    def add(offset, d, totals):
        word = recv_ref[d * HALVES + offset]
        return totals[0] + decode(word >> 16), totals[1] + decode((word << 16) >> 16)

    zero = jnp.zeros((SIDE, LANES), jnp.float32)
    chips = recv_ref.shape[0] // HALVES
    for offset in range(HALVES):
        totals = lax.fori_loop(
            0, chips, functools.partial(add, offset), (zero, zero), unroll=8
        )
        peak = jnp.max(jnp.maximum(*map(jnp.abs, totals)), axis=0, keepdims=True)
        exponent = jnp.floor(jnp.log(jnp.maximum(peak, SMALLEST)) * INV_LN2)
        scale = jnp.exp2(CODE_BITS - exponent)
        high, low = (jnp.round(total * scale).astype(jnp.int32) for total in totals)
        code_ref[offset, pl.ds(0, SIDE), :] = (high << 16) | (low & 0xFFFF)
        code_ref[offset, pl.ds(SIDE, EXP_ROWS), :] = jnp.broadcast_to(
            exponent.astype(jnp.int32), (EXP_ROWS, LANES)
        )


def sum_kernel(live_ref, own_ref, arrived_ref, grad_ref, square_ref, turned_ref):
    slot = lax.broadcasted_iota(jnp.int32, (SIDE, LANES), 1) // SIDE
    low_lane = lax.broadcasted_iota(jnp.int32, (TILES, LANES), 1) < SIDE

    def decode(code_ref, half):
        word = code_ref[half, pl.ds(0, SIDE), :]
        exponent = code_ref[half, pl.ds(SIDE, EXP_ROWS), :][:1].astype(jnp.float32)
        scale = jnp.exp2(exponent - CODE_BITS)
        return [code.astype(jnp.float32) * scale for code in (word >> 16, (word << 16) >> 16)]

    square = jnp.zeros((SIDE, LANES), jnp.float32)
    for half in range(HALVES):
        live = live_ref[half, 0:1, :]
        own, arrived = decode(own_ref, half), decode(arrived_ref, half)
        for pair in range(PAIRS):
            total = jnp.where(slot + pair * 2 < live, own[pair] + arrived[pair], 0.0)
            square = square + total * total
            turned = total.T
            turned_ref[half, pair] = jnp.concatenate([turned, turned], axis=1)
        for s in range(SLOTS):
            base = (s % 2) * SIDE
            even = turned_ref[half, s // 2, pl.ds(base, TILES, stride=2), :]
            odd = turned_ref[half, s // 2, pl.ds(base + 1, TILES, stride=2), :]
            grad_ref[half, pl.ds(s, TILES, stride=SLOTS), :] = jnp.where(low_lane, even, odd)
    square = jnp.sum(square, axis=0, keepdims=True)
    square_ref[...] = jnp.broadcast_to(square[None], square_ref.shape)


def update_kernel(
    live_ref, square_ref, grad_ref, state_ref, other_state_ref,
    spread_ref, new_master_ref, new_moment_ref, new_variance_ref, clipped_ref, rows_ref,
):
    square = square_ref[0]
    for owner in range(1, square_ref.shape[0]):
        square = square + square_ref[owner]
    square = jnp.sum(square, axis=1, keepdims=True)
    entries = live_ref[HALVES, 0:1, :].astype(jnp.float32) * BLOCK
    clip = jnp.minimum(1.0, 1.0 / jnp.sqrt(square / entries + 1e-06))
    half = lax.axis_index("half")

    def step(grad, state):
        clipped = clip * grad
        master, moment, variance = state
        moment = 0.9 * moment + 0.1 * clipped
        variance = 0.95 * variance + 0.05 * clipped * clipped
        moment_hat = moment / (1.0 - 0.9**20)
        variance_hat = variance / (1.0 - 0.95**20)
        change = moment_hat / (jnp.sqrt(variance_hat) + 1e-08) + 0.1 * master
        return master - 0.02 * change, moment, variance, clipped

    for t in range(TILES):
        lanes = pl.ds(t * LANES, LANES)
        rows = pl.ds(t * SLOTS, SLOTS)
        master, moment, variance, clipped = step(
            grad_ref[half, rows, :], [state_ref[k, :, lanes] for k in range(3)]
        )
        clipped_ref[:, lanes] = clipped
        new_moment_ref[:, lanes] = moment
        new_variance_ref[:, lanes] = variance
        new_master_ref[:, lanes] = master
        rows_ref[:, lanes] = step(
            grad_ref[1 - half, rows, :], [other_state_ref[k, :, lanes] for k in range(3)]
        )[0]
    own = new_master_ref[...].astype(jnp.bfloat16)
    other = rows_ref[...].astype(jnp.bfloat16)
    for chip in range(spread_ref.shape[0]):
        spread_ref[chip, half] = own
        spread_ref[chip, 1 - half] = other


def store_kernel(after_ref, *refs):
    half = len(refs) // 2
    for source, target in zip(refs[:half], refs[half:]):
        target[...] = source[...]


def publish_kernel(mine_ref, other_ref, out_hbm, woven_ref, sems):
    rows = CORES * SLOTS
    chips = mine_ref.shape[0]
    parts = sems.shape[0] // HALVES
    step = chips // parts
    core = lax.axis_index("core")

    def weave(first_ref, second_ref):
        copies = []
        for half in range(HALVES):
            for part in range(parts):
                for chip in range(part * step, (part + 1) * step, 2):
                    pieces = []
                    for k in range(2):
                        pieces.append(first_ref[chip + k, half])
                        pieces.append(second_ref[chip + k, half])
                    block = jnp.concatenate(pieces, axis=0)
                    woven_ref[pl.ds((half * chips + chip) * rows, 2 * rows), :] = block
                span = pl.ds((half * chips + part * step) * rows, step * rows)
                copies.append(
                    pltpu.make_async_copy(
                        woven_ref.at[span], out_hbm.at[span], sems.at[len(copies)]
                    )
                )
                copies[-1].start()
        for copy in copies:
            copy.wait()

    @pl.when(core == 0)
    def _():
        weave(mine_ref, other_ref)

    @pl.when(core == 1)
    def _():
        weave(other_ref, mine_ref)


VMEM = pl.BlockSpec(memory_space=pltpu.VMEM)
SMEM = pl.BlockSpec(memory_space=pltpu.SMEM)
ANY = pl.BlockSpec(memory_space=pl.ANY)
PARAMS = pltpu.CompilerParams(vmem_limit_bytes=40 * 1024 * 1024)


def exchange_terms(hidden, grad_out, blocks, live_block_count):
    chips = lax.axis_size(CHIPS)
    tokens = hidden.shape[0]
    top_octave = math.log2(CORES * tokens * LARGEST * LARGEST) + 0.05
    per_octave = 32767 / (top_octave - LOW_OCTAVE)
    cost = pl.CostEstimate(
        flops=2 * chips * SLOTS * SIDE * LANES * tokens,
        bytes_accessed=2 * (hidden.size + grad_out.size),
        transcendentals=0,
    )
    terms = pltpu.VMEM((chips, PAIRS * SIDE, LANES), jnp.float32)
    partner_terms, hidden, turned = pl.pallas_call(
        partner_terms_kernel,
        out_shape=(
            terms,
            pltpu.VMEM(hidden.shape, hidden.dtype),
            pltpu.VMEM(grad_out.shape[::-1], grad_out.dtype),
        ),
        in_specs=[ANY] * 3,
        out_specs=(VMEM,) * 3,
        scratch_shapes=[
            pltpu.SMEM(blocks.shape, jnp.int32),
            pltpu.VMEM(grad_out.shape, grad_out.dtype),
            pltpu.SemaphoreType.DMA((1 + GRAD_PARTS + HIDDEN_PARTS,)),
        ],
        compiler_params=PARAMS,
        cost_estimate=cost,
        name="partner_terms",
    )(*(pltpu.with_memory_space_constraint(x, pltpu.HBM) for x in (blocks, hidden, grad_out)))
    arrived = lax.ppermute(partner_terms, "core", SWAP)
    own_terms, live_rows = pl.pallas_call(
        own_terms_kernel,
        out_shape=(terms, pltpu.VMEM((HALVES + 1, 8, LANES), jnp.int32)),
        in_specs=[SMEM, SMEM, VMEM, VMEM],
        out_specs=(VMEM, VMEM),
        compiler_params=PARAMS,
        cost_estimate=cost,
        name="own_terms",
    )(blocks, live_block_count, hidden, turned)
    codes = pl.pallas_call(
        functools.partial(code_kernel, per_octave),
        out_shape=pltpu.VMEM((chips, SIDE, LANES), jnp.int32),
        in_specs=[VMEM, VMEM],
        out_specs=VMEM,
        compiler_params=PARAMS,
        name="code_terms",
    )(own_terms, arrived)
    return lax.all_to_all(codes, "chip", split_axis=0, concat_axis=0, tiled=True), live_rows


def no_terms(hidden, grad_out, blocks, live_block_count):
    chips = lax.axis_size(CHIPS)
    return (
        jnp.zeros((chips, SIDE, LANES), jnp.int32),
        jnp.zeros((HALVES + 1, 8, LANES), jnp.int32),
    )


def local(hidden, grad_out, block_list, live_block_count, master, moment, variance):
    chips = lax.axis_size(CHIPS)
    shape = jax.ShapeDtypeStruct(master.shape, jnp.float32)
    kept = pltpu.VMEM(master.shape, jnp.float32)
    top_octave = math.log2(CORES * hidden.shape[0] * LARGEST * LARGEST) + 0.05
    per_octave = 32767 / (top_octave - LOW_OCTAVE)
    state = pl.pallas_call(
        gather_kernel,
        out_shape=pltpu.VMEM((3,) + master.shape, jnp.float32),
        in_specs=[ANY] * 3,
        out_specs=VMEM,
        scratch_shapes=[pltpu.SemaphoreType.DMA((3,))],
        compiler_params=PARAMS,
        name="gather_state",
    )(*(pltpu.with_memory_space_constraint(x, pltpu.HBM) for x in (master, moment, variance)))
    other_state = lax.ppermute(state, "half", SWAP)
    received, live_rows = lax.cond(
        lax.axis_index("chip") < lax.axis_size("chip"),
        exchange_terms,
        no_terms,
        hidden,
        grad_out,
        block_list.T,
        live_block_count,
    )
    sum_codes = pl.pallas_call(
        functools.partial(half_sum_kernel, per_octave),
        out_shape=pltpu.VMEM((HALVES, SIDE + EXP_ROWS, LANES), jnp.int32),
        in_specs=[ANY, VMEM],
        out_specs=VMEM,
        compiler_params=PARAMS,
        name="sum_half",
    )(other_state, received)
    arrived = lax.ppermute(sum_codes, "half", SWAP)
    gradient, square = pl.pallas_call(
        sum_kernel,
        out_shape=(
            pltpu.VMEM((HALVES, TILES * SLOTS, LANES), jnp.float32),
            pltpu.VMEM((chips * CORES // HALVES, 1, LANES), jnp.float32),
        ),
        in_specs=[VMEM] * 3,
        out_specs=(VMEM, VMEM),
        scratch_shapes=[pltpu.VMEM((HALVES, PAIRS, LANES, LANES), jnp.float32)],
        compiler_params=PARAMS,
        name="sum_pair",
    )(live_rows, sum_codes, arrived)
    square = lax.all_to_all(square, ("core", "chip"), split_axis=0, concat_axis=0, tiled=True)
    spread, *updated = pl.pallas_call(
        update_kernel,
        out_shape=(
            pltpu.VMEM((chips // HALVES, HALVES) + master.shape, jnp.bfloat16),
            kept,
            kept,
            kept,
            kept,
        ),
        in_specs=[VMEM] * 5,
        out_specs=(VMEM,) * 5,
        scratch_shapes=[pltpu.VMEM(master.shape, jnp.float32)],
        compiler_params=PARAMS,
        name="adamw",
    )(live_rows, square, gradient, state, other_state)
    mine = lax.all_to_all(spread, "chip", split_axis=0, concat_axis=0, tiled=True)
    other = lax.ppermute(mine, "core", SWAP)
    results = pl.pallas_call(
        store_kernel,
        out_shape=(shape,) * 4,
        in_specs=[ANY] + [VMEM] * 4,
        out_specs=(VMEM,) * 4,
        compiler_params=PARAMS,
        name="store_state",
    )(mine, *updated)
    published = pl.pallas_call(
        publish_kernel,
        out_shape=jax.ShapeDtypeStruct((chips * CORES * SLOTS, BLOCK), jnp.bfloat16),
        in_specs=[VMEM, VMEM],
        out_specs=ANY,
        scratch_shapes=[
            pltpu.VMEM((chips * CORES * SLOTS, BLOCK), jnp.bfloat16),
            pltpu.SemaphoreType.DMA((STORE_PARTS,)),
        ],
        compiler_params=PARAMS,
        name="publish",
    )(mine, other)
    return (*results, published)


def solution(mesh):
    devices = mesh.devices.reshape(HALVES, -1, CORES)
    rows = P(AXES, None)
    return jax.shard_map(
        local,
        mesh=Mesh(devices, AXES),
        in_specs=(rows, rows, P(), P(), rows, rows, rows),
        out_specs=(rows, rows, rows, rows, P()),
        check_vma=False,
    )
```

```python
import functools
import math

import jax
import jax.numpy as jnp
from jax import lax
from jax.experimental import pallas as pl
from jax.experimental.pallas import tpu as pltpu
from jax.sharding import Mesh
from jax.sharding import PartitionSpec as P

SIDE = 64
LANES = 128
SLOTS = 4
PAIRS = SLOTS // 2
BLOCK = SIDE * SIDE
TILES = BLOCK // LANES
LOW_OCTAVE = -36
LARGEST = 6.0
SMALLEST = 1e-30
CODE_BITS = 13
EXP_ROWS = 8
GRAD_PARTS = 2
HIDDEN_PARTS = 4
STORE_PARTS = 4
CORES = 2
HALVES = 2
PARTS = 2
AXES = ("half", "chip", "core")
CHIPS = ("chip", "half")
INV_LN2 = 1.4426950408889634


def block_products(core, start, peers, blocks_ref, hidden_ref, turned_ref, out_ref):
    low_lane = lax.broadcasted_iota(jnp.int32, (SIDE, LANES), 1) < SIDE

    chips = peers // HALVES

    def one_chip(row, carry):
        peer = start + row
        owner = ((peer % HALVES) * chips + peer // HALVES) * CORES + core
        for pair in range(PAIRS):
            lefts, rights, rows = [], [], []
            for k in range(2):
                slot = owner * SLOTS + pair * 2 + k
                r = blocks_ref[0, slot]
                c = blocks_ref[1, slot]
                lefts.append(turned_ref[pl.ds(pl.multiple_of(c * SIDE, SIDE), SIDE), :])
                lanes = pl.ds(pl.multiple_of((r // 2) * LANES, LANES), LANES)
                rights.append(hidden_ref[:, lanes])
                rows.append(r)
            product = jnp.dot(
                jnp.concatenate(lefts, axis=0),
                jnp.concatenate(rights, axis=1),
                preferred_element_type=jnp.float32,
            )
            first = pltpu.roll(product[:SIDE, :LANES], (rows[0] % 2) * SIDE, 1)
            second = pltpu.roll(product[SIDE:, LANES:], ((rows[1] + 1) % 2) * SIDE, 1)
            out_ref[row, pl.ds(pair * SIDE, SIDE), :] = jnp.where(low_lane, first, second)
        return carry

    lax.fori_loop(0, out_ref.shape[0], one_chip, 0, unroll=16)


def partner_terms_kernel(
    blocks_hbm, hidden_hbm, grad_hbm, master_hbm, moment_hbm, variance_hbm,
    out_ref, hidden_ref, turned_ref, state_ref, blocks_ref, grad_ref, sems,
):
    copies = [pltpu.make_async_copy(blocks_hbm, blocks_ref, sems.at[0])]
    for source, target, parts in ((grad_hbm, grad_ref, GRAD_PARTS), (hidden_hbm, hidden_ref, HIDDEN_PARTS)):
        step = source.shape[0] // parts
        for k in range(parts):
            rows = pl.ds(k * step, step)
            copies.append(
                pltpu.make_async_copy(source.at[rows], target.at[rows], sems.at[len(copies)])
            )
    for k, source in enumerate((master_hbm, moment_hbm, variance_hbm)):
        copies.append(pltpu.make_async_copy(source, state_ref.at[k], sems.at[len(copies)]))
    for copy in copies:
        copy.start()
    grad_end = 1 + GRAD_PARTS
    hidden_end = grad_end + HIDDEN_PARTS
    for copy in copies[:grad_end]:
        copy.wait()
    for k in range(grad_ref.shape[1] // LANES):
        turned_ref[pl.ds(k * LANES, LANES), :] = grad_ref[:, pl.ds(k * LANES, LANES)].T
    for copy in copies[grad_end:hidden_end]:
        copy.wait()
    peers = PARTS * out_ref.shape[0]
    block_products(
        1 - lax.axis_index("core"), 0, peers, blocks_ref, hidden_ref, turned_ref, out_ref
    )
    for copy in copies[hidden_end:]:
        copy.wait()


def late_terms_kernel(blocks_ref, hidden_ref, turned_ref, out_ref):
    rows = out_ref.shape[0]
    block_products(
        1 - lax.axis_index("core"), rows, PARTS * rows, blocks_ref, hidden_ref, turned_ref, out_ref
    )


def own_terms_kernel(
    after_ref, blocks_ref, live_ref, hidden_ref, turned_ref, out_ref, live_rows_ref
):
    peers = out_ref.shape[0]
    block_products(
        lax.axis_index("core"), 0, peers, blocks_ref, hidden_ref, turned_ref, out_ref
    )
    total = live_ref[0]
    for owner in range(1, live_ref.shape[0]):
        total = total + live_ref[owner]
    owners = live_ref.shape[0] // HALVES
    me = lax.axis_index(AXES[1:])
    for half in range(HALVES):
        live = live_ref[half * owners + me]
        live_rows_ref[half] = jnp.full((8, LANES), live, jnp.int32)
    live_rows_ref[HALVES] = jnp.full((8, LANES), total, jnp.int32)


def code_kernel(per_octave, own_ref, early_ref, late_ref, out_ref):
    def encode(value):
        octave = jnp.log(jnp.maximum(jnp.abs(value), 2.0**LOW_OCTAVE)) * INV_LN2
        code = (octave - LOW_OCTAVE) * per_octave
        return jnp.round(jnp.where(value < 0, -code, code)).astype(jnp.int32)

    def one_chip(first, other_ref, row, carry):
        code = []
        for pair in range(PAIRS):
            rows = pl.ds(pair * SIDE, SIDE)
            code.append(encode(own_ref[first + row, rows, :] + other_ref[row, rows, :]))
        out_ref[first + row] = (code[0] << 16) | (code[1] & 0xFFFF)
        return carry

    count = early_ref.shape[0]
    for k, other_ref in enumerate((early_ref, late_ref)):
        body = functools.partial(one_chip, k * count, other_ref)
        lax.fori_loop(0, count, body, 0, unroll=4)


def half_sum_kernel(per_octave, after_ref, recv_ref, code_ref):
    def decode(code):
        value = code.astype(jnp.float32)
        size = jnp.exp2(jnp.abs(value) * (1.0 / per_octave) + LOW_OCTAVE)
        return jnp.where(code > 0, size, jnp.where(code < 0, -size, 0.0))

    def add(offset, d, totals):
        word = recv_ref[d * HALVES + offset]
        return totals[0] + decode(word >> 16), totals[1] + decode((word << 16) >> 16)

    zero = jnp.zeros((SIDE, LANES), jnp.float32)
    chips = recv_ref.shape[0] // HALVES
    for offset in range(HALVES):
        totals = lax.fori_loop(
            0, chips, functools.partial(add, offset), (zero, zero), unroll=8
        )
        peak = jnp.max(jnp.maximum(*map(jnp.abs, totals)), axis=0, keepdims=True)
        exponent = jnp.floor(jnp.log(jnp.maximum(peak, SMALLEST)) * INV_LN2)
        scale = jnp.exp2(CODE_BITS - exponent)
        high, low = (jnp.round(total * scale).astype(jnp.int32) for total in totals)
        code_ref[offset, pl.ds(0, SIDE), :] = (high << 16) | (low & 0xFFFF)
        code_ref[offset, pl.ds(SIDE, EXP_ROWS), :] = jnp.broadcast_to(
            exponent.astype(jnp.int32), (EXP_ROWS, LANES)
        )


def sum_kernel(live_ref, own_ref, arrived_ref, grad_ref, square_ref, turned_ref):
    slot = lax.broadcasted_iota(jnp.int32, (SIDE, LANES), 1) // SIDE
    low_lane = lax.broadcasted_iota(jnp.int32, (TILES, LANES), 1) < SIDE

    def decode(code_ref, half):
        word = code_ref[half, pl.ds(0, SIDE), :]
        exponent = code_ref[half, pl.ds(SIDE, EXP_ROWS), :][:1].astype(jnp.float32)
        scale = jnp.exp2(exponent - CODE_BITS)
        return [code.astype(jnp.float32) * scale for code in (word >> 16, (word << 16) >> 16)]

    square = jnp.zeros((SIDE, LANES), jnp.float32)
    for half in range(HALVES):
        live = live_ref[half, 0:1, :]
        own, arrived = decode(own_ref, half), decode(arrived_ref, half)
        for pair in range(PAIRS):
            total = jnp.where(slot + pair * 2 < live, own[pair] + arrived[pair], 0.0)
            square = square + total * total
            turned = total.T
            turned_ref[half, pair] = jnp.concatenate([turned, turned], axis=1)
        for s in range(SLOTS):
            base = (s % 2) * SIDE
            even = turned_ref[half, s // 2, pl.ds(base, TILES, stride=2), :]
            odd = turned_ref[half, s // 2, pl.ds(base + 1, TILES, stride=2), :]
            grad_ref[half, pl.ds(s, TILES, stride=SLOTS), :] = jnp.where(low_lane, even, odd)
    square = jnp.sum(square, axis=0, keepdims=True)
    square_ref[...] = jnp.broadcast_to(square[None], square_ref.shape)


def update_kernel(
    live_ref, square_ref, grad_ref, state_ref, other_state_ref,
    spread_ref, new_master_ref, new_moment_ref, new_variance_ref, clipped_ref, rows_ref,
):
    square = square_ref[0]
    for owner in range(1, square_ref.shape[0]):
        square = square + square_ref[owner]
    square = jnp.sum(square, axis=1, keepdims=True)
    entries = live_ref[HALVES, 0:1, :].astype(jnp.float32) * BLOCK
    clip = jnp.minimum(1.0, 1.0 / jnp.sqrt(square / entries + 1e-06))
    half = lax.axis_index("half")

    def step(grad, state):
        clipped = clip * grad
        master, moment, variance = state
        moment = 0.9 * moment + 0.1 * clipped
        variance = 0.95 * variance + 0.05 * clipped * clipped
        moment_hat = moment / (1.0 - 0.9**20)
        variance_hat = variance / (1.0 - 0.95**20)
        change = moment_hat / (jnp.sqrt(variance_hat) + 1e-08) + 0.1 * master
        return master - 0.02 * change, moment, variance, clipped

    for t in range(TILES):
        lanes = pl.ds(t * LANES, LANES)
        rows = pl.ds(t * SLOTS, SLOTS)
        master, moment, variance, clipped = step(
            grad_ref[half, rows, :], [state_ref[k, :, lanes] for k in range(3)]
        )
        clipped_ref[:, lanes] = clipped
        new_moment_ref[:, lanes] = moment
        new_variance_ref[:, lanes] = variance
        new_master_ref[:, lanes] = master
        rows_ref[:, lanes] = step(
            grad_ref[1 - half, rows, :], [other_state_ref[k, :, lanes] for k in range(3)]
        )[0]
    own = new_master_ref[...].astype(jnp.bfloat16)
    other = rows_ref[...].astype(jnp.bfloat16)
    for chip in range(spread_ref.shape[0]):
        spread_ref[chip, half] = own
        spread_ref[chip, 1 - half] = other


def store_kernel(after_ref, *refs):
    half = len(refs) // 2
    for source, target in zip(refs[:half], refs[half:]):
        target[...] = source[...]


def publish_kernel(mine_ref, other_ref, out_hbm, woven_ref, sems):
    rows = CORES * SLOTS
    chips = mine_ref.shape[0]
    parts = sems.shape[0] // HALVES
    step = chips // parts
    core = lax.axis_index("core")

    def weave(first_ref, second_ref):
        copies = []
        for half in range(HALVES):
            for part in range(parts):
                for chip in range(part * step, (part + 1) * step, 2):
                    pieces = []
                    for k in range(2):
                        pieces.append(first_ref[chip + k, half])
                        pieces.append(second_ref[chip + k, half])
                    block = jnp.concatenate(pieces, axis=0)
                    woven_ref[pl.ds((half * chips + chip) * rows, 2 * rows), :] = block
                span = pl.ds((half * chips + part * step) * rows, step * rows)
                copies.append(
                    pltpu.make_async_copy(
                        woven_ref.at[span], out_hbm.at[span], sems.at[len(copies)]
                    )
                )
                copies[-1].start()
        for copy in copies:
            copy.wait()

    @pl.when(core == 0)
    def _():
        weave(mine_ref, other_ref)

    @pl.when(core == 1)
    def _():
        weave(other_ref, mine_ref)


VMEM = pl.BlockSpec(memory_space=pltpu.VMEM)
SMEM = pl.BlockSpec(memory_space=pltpu.SMEM)
ANY = pl.BlockSpec(memory_space=pl.ANY)
PARAMS = pltpu.CompilerParams(vmem_limit_bytes=40 * 1024 * 1024)


def local(hidden, grad_out, block_list, live_block_count, master, moment, variance):
    chips = lax.axis_size(CHIPS)
    tokens = hidden.shape[0]
    swap = [(0, 1), (1, 0)]
    shape = jax.ShapeDtypeStruct(master.shape, jnp.float32)
    kept = pltpu.VMEM(master.shape, jnp.float32)
    blocks = block_list.T
    top_octave = math.log2(CORES * tokens * LARGEST * LARGEST) + 0.05
    per_octave = 32767 / (top_octave - LOW_OCTAVE)
    cost = pl.CostEstimate(
        flops=2 * chips * SLOTS * SIDE * LANES * tokens,
        bytes_accessed=2 * (hidden.size + grad_out.size),
        transcendentals=0,
    )
    terms = pltpu.VMEM((chips, PAIRS * SIDE, LANES), jnp.float32)
    part_terms = pltpu.VMEM((chips // PARTS, PAIRS * SIDE, LANES), jnp.float32)
    partner_terms, hidden, turned, state = pl.pallas_call(
        partner_terms_kernel,
        out_shape=(
            part_terms,
            pltpu.VMEM(hidden.shape, hidden.dtype),
            pltpu.VMEM(grad_out.shape[::-1], grad_out.dtype),
            pltpu.VMEM((3,) + master.shape, jnp.float32),
        ),
        in_specs=[ANY] * 6,
        out_specs=(VMEM,) * 4,
        scratch_shapes=[
            pltpu.SMEM(blocks.shape, jnp.int32),
            pltpu.VMEM(grad_out.shape, grad_out.dtype),
            pltpu.SemaphoreType.DMA((4 + GRAD_PARTS + HIDDEN_PARTS,)),
        ],
        compiler_params=PARAMS,
        cost_estimate=cost,
        name="partner_terms",
    )(
        *(
            pltpu.with_memory_space_constraint(x, pltpu.HBM)
            for x in (blocks, hidden, grad_out, master, moment, variance)
        )
    )
    early = lax.ppermute(partner_terms, "core", swap)
    late_terms = pl.pallas_call(
        late_terms_kernel,
        out_shape=part_terms,
        in_specs=[SMEM, VMEM, VMEM],
        out_specs=VMEM,
        compiler_params=PARAMS,
        cost_estimate=cost,
        name="late_terms",
    )(blocks, hidden, turned)
    late = lax.ppermute(late_terms, "core", swap)
    other_state = lax.ppermute(state, "half", swap)
    own_terms, live_rows = pl.pallas_call(
        own_terms_kernel,
        out_shape=(terms, pltpu.VMEM((HALVES + 1, 8, LANES), jnp.int32)),
        in_specs=[ANY, SMEM, SMEM, VMEM, VMEM],
        out_specs=(VMEM, VMEM),
        compiler_params=PARAMS,
        cost_estimate=cost,
        name="own_terms",
    )(early, blocks, live_block_count, hidden, turned)
    codes = pl.pallas_call(
        functools.partial(code_kernel, per_octave),
        out_shape=pltpu.VMEM((chips, SIDE, LANES), jnp.int32),
        in_specs=[VMEM, VMEM, VMEM],
        out_specs=VMEM,
        compiler_params=PARAMS,
        name="code_terms",
    )(own_terms, early, late)
    received = lax.cond(
        live_block_count[0] > 0,
        lambda x: lax.all_to_all(x, "chip", split_axis=0, concat_axis=0, tiled=True),
        jnp.zeros_like,
        codes,
    )
    sum_codes = pl.pallas_call(
        functools.partial(half_sum_kernel, per_octave),
        out_shape=pltpu.VMEM((HALVES, SIDE + EXP_ROWS, LANES), jnp.int32),
        in_specs=[ANY, VMEM],
        out_specs=VMEM,
        compiler_params=PARAMS,
        name="sum_half",
    )(other_state, received)
    arrived = lax.ppermute(sum_codes, "half", swap)
    gradient, square = pl.pallas_call(
        sum_kernel,
        out_shape=(
            pltpu.VMEM((HALVES, TILES * SLOTS, LANES), jnp.float32),
            pltpu.VMEM((chips * CORES // HALVES, 1, LANES), jnp.float32),
        ),
        in_specs=[VMEM] * 3,
        out_specs=(VMEM, VMEM),
        scratch_shapes=[pltpu.VMEM((HALVES, PAIRS, LANES, LANES), jnp.float32)],
        compiler_params=PARAMS,
        name="sum_pair",
    )(live_rows, sum_codes, arrived)
    square = lax.all_to_all(square, ("core", "chip"), split_axis=0, concat_axis=0, tiled=True)
    spread, *updated = pl.pallas_call(
        update_kernel,
        out_shape=(
            pltpu.VMEM((chips // HALVES, HALVES) + master.shape, jnp.bfloat16),
            kept,
            kept,
            kept,
            kept,
        ),
        in_specs=[VMEM] * 5,
        out_specs=(VMEM,) * 5,
        scratch_shapes=[pltpu.VMEM(master.shape, jnp.float32)],
        compiler_params=PARAMS,
        name="adamw",
    )(live_rows, square, gradient, state, other_state)
    mine = lax.all_to_all(spread, "chip", split_axis=0, concat_axis=0, tiled=True)
    other = lax.ppermute(mine, "core", swap)
    results = pl.pallas_call(
        store_kernel,
        out_shape=(shape,) * 4,
        in_specs=[ANY] + [VMEM] * 4,
        out_specs=(VMEM,) * 4,
        compiler_params=PARAMS,
        name="store_state",
    )(mine, *updated)
    published = pl.pallas_call(
        publish_kernel,
        out_shape=jax.ShapeDtypeStruct((chips * CORES * SLOTS, BLOCK), jnp.bfloat16),
        in_specs=[VMEM, VMEM],
        out_specs=ANY,
        scratch_shapes=[
            pltpu.VMEM((chips * CORES * SLOTS, BLOCK), jnp.bfloat16),
            pltpu.SemaphoreType.DMA((STORE_PARTS,)),
        ],
        compiler_params=PARAMS,
        name="publish",
    )(mine, other)
    return (*results, published)


def solution(mesh):
    devices = mesh.devices.reshape(HALVES, -1, CORES)
    rows = P(AXES, None)
    return jax.shard_map(
        local,
        mesh=Mesh(devices, AXES),
        in_specs=(rows, rows, P(), P(), rows, rows, rows),
        out_specs=(rows, rows, rows, rows, P()),
        check_vma=False,
    )
```

```python
import functools
import math

import jax
import jax.numpy as jnp
from jax import lax
from jax.experimental import pallas as pl
from jax.experimental.pallas import tpu as pltpu
from jax.sharding import Mesh
from jax.sharding import PartitionSpec as P

SIDE = 64
LANES = 128
SLOTS = 4
PAIRS = SLOTS // 2
BLOCK = SIDE * SIDE
TILES = BLOCK // LANES
LOW_OCTAVE = -36
LARGEST = 6.0
SMALLEST = 1e-30
CODE_BITS = 13
EXP_ROWS = 8
GRAD_PARTS = 2
HIDDEN_PARTS = 4
STORE_PARTS = 4
CORES = 2
HALVES = 2
PARTS = 2
AXES = ("half", "chip", "core")
CHIPS = ("chip", "half")
INV_LN2 = 1.4426950408889634


def block_products(core, start, peers, blocks_ref, hidden_ref, turned_ref, out_ref):
    low_lane = lax.broadcasted_iota(jnp.int32, (SIDE, LANES), 1) < SIDE

    chips = peers // HALVES

    def one_chip(row, carry):
        peer = start + row
        owner = ((peer % HALVES) * chips + peer // HALVES) * CORES + core
        for pair in range(PAIRS):
            lefts, rights, rows = [], [], []
            for k in range(2):
                slot = owner * SLOTS + pair * 2 + k
                r = blocks_ref[0, slot]
                c = blocks_ref[1, slot]
                lefts.append(turned_ref[pl.ds(pl.multiple_of(c * SIDE, SIDE), SIDE), :])
                lanes = pl.ds(pl.multiple_of((r // 2) * LANES, LANES), LANES)
                rights.append(hidden_ref[:, lanes])
                rows.append(r)
            product = jnp.dot(
                jnp.concatenate(lefts, axis=0),
                jnp.concatenate(rights, axis=1),
                preferred_element_type=jnp.float32,
            )
            first = pltpu.roll(product[:SIDE, :LANES], (rows[0] % 2) * SIDE, 1)
            second = pltpu.roll(product[SIDE:, LANES:], ((rows[1] + 1) % 2) * SIDE, 1)
            out_ref[row, pl.ds(pair * SIDE, SIDE), :] = jnp.where(low_lane, first, second)
        return carry

    lax.fori_loop(0, out_ref.shape[0], one_chip, 0, unroll=min(16, out_ref.shape[0]))


def partner_terms_kernel(
    blocks_hbm, hidden_hbm, grad_hbm, master_hbm, moment_hbm, variance_hbm,
    out_ref, hidden_ref, turned_ref, state_ref, blocks_ref, grad_ref, sems,
):
    copies = [pltpu.make_async_copy(blocks_hbm, blocks_ref, sems.at[0])]
    for source, target, parts in ((grad_hbm, grad_ref, GRAD_PARTS), (hidden_hbm, hidden_ref, HIDDEN_PARTS)):
        step = source.shape[0] // parts
        for k in range(parts):
            rows = pl.ds(k * step, step)
            copies.append(
                pltpu.make_async_copy(source.at[rows], target.at[rows], sems.at[len(copies)])
            )
    for k, source in enumerate((master_hbm, moment_hbm, variance_hbm)):
        copies.append(pltpu.make_async_copy(source, state_ref.at[k], sems.at[len(copies)]))
    for copy in copies:
        copy.start()
    grad_end = 1 + GRAD_PARTS
    hidden_end = grad_end + HIDDEN_PARTS
    for copy in copies[:grad_end]:
        copy.wait()
    for k in range(grad_ref.shape[1] // LANES):
        turned_ref[pl.ds(k * LANES, LANES), :] = grad_ref[:, pl.ds(k * LANES, LANES)].T
    for copy in copies[grad_end:hidden_end]:
        copy.wait()
    peers = PARTS * out_ref.shape[0]
    block_products(
        1 - lax.axis_index("core"), 0, peers, blocks_ref, hidden_ref, turned_ref, out_ref
    )
    for copy in copies[hidden_end:]:
        copy.wait()


def late_terms_kernel(blocks_ref, hidden_ref, turned_ref, out_ref):
    rows = out_ref.shape[0]
    block_products(
        1 - lax.axis_index("core"), rows, PARTS * rows, blocks_ref, hidden_ref, turned_ref, out_ref
    )


def own_terms_kernel(
    after_ref, blocks_ref, live_ref, hidden_ref, turned_ref, out_ref, live_rows_ref
):
    peers = out_ref.shape[0]
    block_products(
        lax.axis_index("core"), 0, peers, blocks_ref, hidden_ref, turned_ref, out_ref
    )
    total = live_ref[0]
    for owner in range(1, live_ref.shape[0]):
        total = total + live_ref[owner]
    owners = live_ref.shape[0] // HALVES
    me = lax.axis_index(AXES[1:])
    for half in range(HALVES):
        live = live_ref[half * owners + me]
        live_rows_ref[half] = jnp.full((8, LANES), live, jnp.int32)
    live_rows_ref[HALVES] = jnp.full((8, LANES), total, jnp.int32)


def code_kernel(per_octave, own_ref, early_ref, late_ref, out_ref):
    def encode(value):
        octave = jnp.log(jnp.maximum(jnp.abs(value), 2.0**LOW_OCTAVE)) * INV_LN2
        code = (octave - LOW_OCTAVE) * per_octave
        return jnp.round(jnp.where(value < 0, -code, code)).astype(jnp.int32)

    def one_chip(first, other_ref, row, carry):
        code = []
        for pair in range(PAIRS):
            rows = pl.ds(pair * SIDE, SIDE)
            code.append(encode(own_ref[first + row, rows, :] + other_ref[row, rows, :]))
        out_ref[first + row] = (code[0] << 16) | (code[1] & 0xFFFF)
        return carry

    count = early_ref.shape[0]
    for k, other_ref in enumerate((early_ref, late_ref)):
        body = functools.partial(one_chip, k * count, other_ref)
        lax.fori_loop(0, count, body, 0, unroll=4)


def half_sum_kernel(per_octave, after_ref, recv_ref, code_ref):
    def decode(code):
        value = code.astype(jnp.float32)
        size = jnp.exp2(jnp.abs(value) * (1.0 / per_octave) + LOW_OCTAVE)
        return jnp.where(code > 0, size, jnp.where(code < 0, -size, 0.0))

    def add(offset, d, totals):
        word = recv_ref[d * HALVES + offset]
        return totals[0] + decode(word >> 16), totals[1] + decode((word << 16) >> 16)

    zero = jnp.zeros((SIDE, LANES), jnp.float32)
    chips = recv_ref.shape[0] // HALVES
    for offset in range(HALVES):
        totals = lax.fori_loop(
            0, chips, functools.partial(add, offset), (zero, zero), unroll=8
        )
        peak = jnp.max(jnp.maximum(*map(jnp.abs, totals)), axis=0, keepdims=True)
        exponent = jnp.floor(jnp.log(jnp.maximum(peak, SMALLEST)) * INV_LN2)
        scale = jnp.exp2(CODE_BITS - exponent)
        high, low = (jnp.round(total * scale).astype(jnp.int32) for total in totals)
        code_ref[offset, pl.ds(0, SIDE), :] = (high << 16) | (low & 0xFFFF)
        code_ref[offset, pl.ds(SIDE, EXP_ROWS), :] = jnp.broadcast_to(
            exponent.astype(jnp.int32), (EXP_ROWS, LANES)
        )


def sum_kernel(live_ref, own_ref, arrived_ref, grad_ref, square_ref, turned_ref):
    slot = lax.broadcasted_iota(jnp.int32, (SIDE, LANES), 1) // SIDE
    low_lane = lax.broadcasted_iota(jnp.int32, (TILES, LANES), 1) < SIDE

    def decode(code_ref, half):
        word = code_ref[half, pl.ds(0, SIDE), :]
        exponent = code_ref[half, pl.ds(SIDE, EXP_ROWS), :][:1].astype(jnp.float32)
        scale = jnp.exp2(exponent - CODE_BITS)
        return [code.astype(jnp.float32) * scale for code in (word >> 16, (word << 16) >> 16)]

    square = jnp.zeros((SIDE, LANES), jnp.float32)
    for half in range(HALVES):
        live = live_ref[half, 0:1, :]
        own, arrived = decode(own_ref, half), decode(arrived_ref, half)
        for pair in range(PAIRS):
            total = jnp.where(slot + pair * 2 < live, own[pair] + arrived[pair], 0.0)
            square = square + total * total
            turned = total.T
            turned_ref[half, pair] = jnp.concatenate([turned, turned], axis=1)
        for s in range(SLOTS):
            base = (s % 2) * SIDE
            even = turned_ref[half, s // 2, pl.ds(base, TILES, stride=2), :]
            odd = turned_ref[half, s // 2, pl.ds(base + 1, TILES, stride=2), :]
            grad_ref[half, pl.ds(s, TILES, stride=SLOTS), :] = jnp.where(low_lane, even, odd)
    square = jnp.sum(square, axis=0, keepdims=True)
    square_ref[...] = jnp.broadcast_to(square[None], square_ref.shape)


def update_kernel(
    live_ref, square_ref, grad_ref, state_ref, other_state_ref,
    spread_ref, new_master_ref, new_moment_ref, new_variance_ref, clipped_ref, rows_ref,
):
    square = square_ref[0]
    for owner in range(1, square_ref.shape[0]):
        square = square + square_ref[owner]
    square = jnp.sum(square, axis=1, keepdims=True)
    entries = live_ref[HALVES, 0:1, :].astype(jnp.float32) * BLOCK
    clip = jnp.minimum(1.0, 1.0 / jnp.sqrt(square / entries + 1e-06))
    half = lax.axis_index("half")

    def step(grad, state):
        clipped = clip * grad
        master, moment, variance = state
        moment = 0.9 * moment + 0.1 * clipped
        variance = 0.95 * variance + 0.05 * clipped * clipped
        moment_hat = moment / (1.0 - 0.9**20)
        variance_hat = variance / (1.0 - 0.95**20)
        change = moment_hat / (jnp.sqrt(variance_hat) + 1e-08) + 0.1 * master
        return master - 0.02 * change, moment, variance, clipped

    for t in range(TILES):
        lanes = pl.ds(t * LANES, LANES)
        rows = pl.ds(t * SLOTS, SLOTS)
        master, moment, variance, clipped = step(
            grad_ref[half, rows, :], [state_ref[k, :, lanes] for k in range(3)]
        )
        clipped_ref[:, lanes] = clipped
        new_moment_ref[:, lanes] = moment
        new_variance_ref[:, lanes] = variance
        new_master_ref[:, lanes] = master
        rows_ref[:, lanes] = step(
            grad_ref[1 - half, rows, :], [other_state_ref[k, :, lanes] for k in range(3)]
        )[0]
    own = new_master_ref[...].astype(jnp.bfloat16)
    other = rows_ref[...].astype(jnp.bfloat16)
    for chip in range(spread_ref.shape[0]):
        spread_ref[chip, half] = own
        spread_ref[chip, 1 - half] = other


def store_kernel(after_ref, *refs):
    half = len(refs) // 2
    for source, target in zip(refs[:half], refs[half:]):
        target[...] = source[...]


def publish_kernel(mine_ref, other_ref, out_hbm, woven_ref, sems):
    rows = CORES * SLOTS
    chips = mine_ref.shape[0]
    parts = sems.shape[0] // HALVES
    step = chips // parts
    core = lax.axis_index("core")

    def weave(first_ref, second_ref):
        copies = []
        for half in range(HALVES):
            for part in range(parts):
                for chip in range(part * step, (part + 1) * step, 2):
                    pieces = []
                    for k in range(2):
                        pieces.append(first_ref[chip + k, half])
                        pieces.append(second_ref[chip + k, half])
                    block = jnp.concatenate(pieces, axis=0)
                    woven_ref[pl.ds((half * chips + chip) * rows, 2 * rows), :] = block
                span = pl.ds((half * chips + part * step) * rows, step * rows)
                copies.append(
                    pltpu.make_async_copy(
                        woven_ref.at[span], out_hbm.at[span], sems.at[len(copies)]
                    )
                )
                copies[-1].start()
        for copy in copies:
            copy.wait()

    @pl.when(core == 0)
    def _():
        weave(mine_ref, other_ref)

    @pl.when(core == 1)
    def _():
        weave(other_ref, mine_ref)


VMEM = pl.BlockSpec(memory_space=pltpu.VMEM)
SMEM = pl.BlockSpec(memory_space=pltpu.SMEM)
ANY = pl.BlockSpec(memory_space=pl.ANY)
PARAMS = pltpu.CompilerParams(vmem_limit_bytes=40 * 1024 * 1024)


def local(hidden, grad_out, block_list, live_block_count, master, moment, variance):
    chips = lax.axis_size(CHIPS)
    tokens = hidden.shape[0]
    swap = [(0, 1), (1, 0)]
    shape = jax.ShapeDtypeStruct(master.shape, jnp.float32)
    kept = pltpu.VMEM(master.shape, jnp.float32)
    blocks = block_list.T
    top_octave = math.log2(CORES * tokens * LARGEST * LARGEST) + 0.05
    per_octave = 32767 / (top_octave - LOW_OCTAVE)
    cost = pl.CostEstimate(
        flops=2 * chips * SLOTS * SIDE * LANES * tokens,
        bytes_accessed=2 * (hidden.size + grad_out.size),
        transcendentals=0,
    )
    terms = pltpu.VMEM((chips, PAIRS * SIDE, LANES), jnp.float32)
    part_terms = pltpu.VMEM((chips // PARTS, PAIRS * SIDE, LANES), jnp.float32)
    partner_terms, hidden, turned, state = pl.pallas_call(
        partner_terms_kernel,
        out_shape=(
            part_terms,
            pltpu.VMEM(hidden.shape, hidden.dtype),
            pltpu.VMEM(grad_out.shape[::-1], grad_out.dtype),
            pltpu.VMEM((3,) + master.shape, jnp.float32),
        ),
        in_specs=[ANY] * 6,
        out_specs=(VMEM,) * 4,
        scratch_shapes=[
            pltpu.SMEM(blocks.shape, jnp.int32),
            pltpu.VMEM(grad_out.shape, grad_out.dtype),
            pltpu.SemaphoreType.DMA((4 + GRAD_PARTS + HIDDEN_PARTS,)),
        ],
        compiler_params=PARAMS,
        cost_estimate=cost,
        name="partner_terms",
    )(
        *(
            pltpu.with_memory_space_constraint(x, pltpu.HBM)
            for x in (blocks, hidden, grad_out, master, moment, variance)
        )
    )
    early = lax.ppermute(partner_terms, "core", swap)
    late_terms = pl.pallas_call(
        late_terms_kernel,
        out_shape=part_terms,
        in_specs=[SMEM, VMEM, VMEM],
        out_specs=VMEM,
        compiler_params=PARAMS,
        cost_estimate=cost,
        name="late_terms",
    )(blocks, hidden, turned)
    late = lax.ppermute(late_terms, "core", swap)
    other_state = lax.ppermute(state, "half", swap)
    own_terms, live_rows = pl.pallas_call(
        own_terms_kernel,
        out_shape=(terms, pltpu.VMEM((HALVES + 1, 8, LANES), jnp.int32)),
        in_specs=[ANY, SMEM, SMEM, VMEM, VMEM],
        out_specs=(VMEM, VMEM),
        compiler_params=PARAMS,
        cost_estimate=cost,
        name="own_terms",
    )(early, blocks, live_block_count, hidden, turned)
    codes = pl.pallas_call(
        functools.partial(code_kernel, per_octave),
        out_shape=pltpu.VMEM((chips, SIDE, LANES), jnp.int32),
        in_specs=[VMEM, VMEM, VMEM],
        out_specs=VMEM,
        compiler_params=PARAMS,
        name="code_terms",
    )(own_terms, early, late)
    received = lax.cond(
        live_block_count[0] > 0,
        lambda x: lax.all_to_all(x, "chip", split_axis=0, concat_axis=0, tiled=True),
        jnp.zeros_like,
        codes,
    )
    sum_codes = pl.pallas_call(
        functools.partial(half_sum_kernel, per_octave),
        out_shape=pltpu.VMEM((HALVES, SIDE + EXP_ROWS, LANES), jnp.int32),
        in_specs=[ANY, VMEM],
        out_specs=VMEM,
        compiler_params=PARAMS,
        name="sum_half",
    )(other_state, received)
    arrived = lax.ppermute(sum_codes, "half", swap)
    gradient, square = pl.pallas_call(
        sum_kernel,
        out_shape=(
            pltpu.VMEM((HALVES, TILES * SLOTS, LANES), jnp.float32),
            pltpu.VMEM((chips * CORES // HALVES, 1, LANES), jnp.float32),
        ),
        in_specs=[VMEM] * 3,
        out_specs=(VMEM, VMEM),
        scratch_shapes=[pltpu.VMEM((HALVES, PAIRS, LANES, LANES), jnp.float32)],
        compiler_params=PARAMS,
        name="sum_pair",
    )(live_rows, sum_codes, arrived)
    square = lax.all_to_all(square, ("core", "chip"), split_axis=0, concat_axis=0, tiled=True)
    spread, *updated = pl.pallas_call(
        update_kernel,
        out_shape=(
            pltpu.VMEM((chips // HALVES, HALVES) + master.shape, jnp.bfloat16),
            kept,
            kept,
            kept,
            kept,
        ),
        in_specs=[VMEM] * 5,
        out_specs=(VMEM,) * 5,
        scratch_shapes=[pltpu.VMEM(master.shape, jnp.float32)],
        compiler_params=PARAMS,
        name="adamw",
    )(live_rows, square, gradient, state, other_state)
    mine = lax.all_to_all(spread, "chip", split_axis=0, concat_axis=0, tiled=True)
    other = lax.ppermute(mine, "core", swap)
    results = pl.pallas_call(
        store_kernel,
        out_shape=(shape,) * 4,
        in_specs=[ANY] + [VMEM] * 4,
        out_specs=(VMEM,) * 4,
        compiler_params=PARAMS,
        name="store_state",
    )(mine, *updated)
    published = pl.pallas_call(
        publish_kernel,
        out_shape=jax.ShapeDtypeStruct((chips * CORES * SLOTS, BLOCK), jnp.bfloat16),
        in_specs=[VMEM, VMEM],
        out_specs=ANY,
        scratch_shapes=[
            pltpu.VMEM((chips * CORES * SLOTS, BLOCK), jnp.bfloat16),
            pltpu.SemaphoreType.DMA((STORE_PARTS,)),
        ],
        compiler_params=PARAMS,
        name="publish",
    )(mine, other)
    return (*results, published)


def solution(mesh):
    devices = mesh.devices.reshape(HALVES, -1, CORES)
    rows = P(AXES, None)
    return jax.shard_map(
        local,
        mesh=Mesh(devices, AXES),
        in_specs=(rows, rows, P(), P(), rows, rows, rows),
        out_specs=(rows, rows, rows, rows, P()),
        check_vma=False,
    )
```
